768 devices in a mesh: dp: 96 (over z, y), mp: 8 (over x, core).
Axes of the slice: x: 4, y: 8, z: 12, core: 2. Of those that a mesh axis runs over, the one named last changes fastest.
Arguments:
- grad_proj: bfloat16 [12288, 12800], P(('dp', 'mp')), may hold values from -6 to 6
- tile_counts: int32 [96, 1], P('dp'), may hold values from 1 to 8, as said below
- tile_home: int32 [96, 8], P('dp'), may hold values from 0 to 7, each once within a row
- saved_feat: bfloat16 [12288, 12800], P(('dp', 'mp')), may hold values from -6 to 6
- ln_gain: float32 [12800], replicated, may hold values from 0.1 to 1.9
- layer_scale: float32 [3200], replicated, may hold values from 0.2 to 2
- attn_saved: bfloat16 [49152, 1664], P('dp', 'mp'), may hold values from -6 to 6
- proj_weight: bfloat16 [3200, 1664], P(None, 'mp'), may hold values from -0.109375 to 0.109375
Outputs:
- residual_grad: bfloat16 [49152, 3200], P(('dp', 'mp'))
- attn_grad: bfloat16 [49152, 1664], P('dp', 'mp')
- proj_grad: float32 [3264, 1664], P('dp', 'mp')
- gain_grad: float32 [12800], replicated
The draws below stay inside these ranges and needn't reach their ends.
Inputs may be any that keep to these rules, and one draw needn't show every extreme that they name: `tile_counts`: tiles of each sample; in every draw some vision group has its sample at 8 tiles. `tile_home`: each row names every vision slot of its group once.
All inputs are finite; a program needn't handle non-finite values.
Results may differ from the reference program's by a relative error of at most 0.0049.
Values may be sent and summed in bfloat16 or wider, within the bound.
No kernel may reach another device: no remote copies, remote signals or barrier semaphores. Data moves between devices by JAX's collectives and lax.ppermute only.
A program may use at most 32 MiB of HBM per device.

```python
import math
import jax
import jax.numpy as jnp
from jax import lax

VW = 3200
AW = 1664
PW = 12800
TILE_SIDE = 8
VT = 64
PR = 16
MAXT = 8
SAMP = 1
CAPT = 8
COLPAD = 3264
N_DP = 96


def draw_tile_counts(key, part):
    key = jax.random.fold_in(key, 11)
    count_key, full_key = jax.random.split(key)
    counts = jax.random.randint(count_key, (N_DP, SAMP), 1, MAXT + 1)
    full_group = jax.random.randint(full_key, (), 0, N_DP)
    chosen = jnp.arange(N_DP)[:, None] == full_group
    return jnp.where(chosen, MAXT, counts).astype(jnp.int32)


def steps_of(own_key, dims, shards, least, top_value):
    level, own = 1.0, jax.random.fold_in(own_key, 6)
    for axis_at, blocks in shards:
        steps = jnp.exp(jax.random.uniform(jax.random.fold_in(own, axis_at), (blocks,), jnp.float32, least / len(shards), top_value / len(shards)))
        level = level * jnp.repeat(steps, dims[axis_at] // blocks).reshape([-1 if axis == axis_at else 1 for axis in range(len(dims))])
    return level


def gaussian(own_key, dims, deviation, bound, shards=(), kind=jnp.bfloat16):
    gain = steps_of(own_key, dims, shards, -0.22, 0.18) if shards else 1.0
    array = jax.random.normal(own_key, dims, jnp.float32) * deviation * gain
    return jnp.minimum(jnp.maximum(array, -bound), bound).astype(kind)


def setup_inputs(seed: int = 0) -> dict:
    seeds = jax.random.split(jax.random.key(seed), 9)
    grad_proj = gaussian(seeds[0], (N_DP * CAPT * PR, PW), 1.0, 6.0, ((0, 768),))
    tile_counts = draw_tile_counts(jax.random.fold_in(seeds[8], 71), 0)
    tile_home = jax.vmap(lambda own: jax.random.permutation(own, CAPT))(jax.random.split(seeds[2], N_DP)).reshape((N_DP, CAPT)).astype(jnp.int32)
    saved_feat = gaussian(seeds[3], (N_DP * CAPT * PR, PW), 1.0, 6.0, ((0, 768),))
    ln_gain = jnp.clip(1.0 + 0.18 * jax.random.normal(seeds[4], (PW,), jnp.float32), 0.1, 1.9)
    layer_scale = jnp.clip(jnp.exp(jax.random.uniform(seeds[5], (VW,), jnp.float32, math.log(0.2), math.log(2.0))), 0.2, 2.0)
    attn_saved = gaussian(seeds[6], (N_DP * CAPT * VT, AW), 1.0, 6.0, ((0, 96), (1, 8)))
    proj_weight = gaussian(seeds[7], (VW, AW), VW ** -0.5, 0.109375, ((1, 8),))
    return {"grad_proj": grad_proj, "tile_counts": tile_counts, "tile_home": tile_home, "saved_feat": saved_feat, "ln_gain": ln_gain, "layer_scale": layer_scale, "attn_saved": attn_saved, "proj_weight": proj_weight}


EPSILON = 1e-05

def layer_norm_back(upstream, features, ln_gain):
    values = features.astype(jnp.float32)
    centered = values - lax.optimization_barrier(jnp.mean(values, axis=-1, keepdims=True))
    inverse_std = lax.rsqrt(lax.optimization_barrier(jnp.mean(centered * centered, axis=-1, keepdims=True)) + EPSILON)
    normed = centered * inverse_std
    scaled = upstream * ln_gain
    first_mean = lax.optimization_barrier(jnp.mean(scaled, axis=-1, keepdims=True))
    second_mean = lax.optimization_barrier(jnp.mean(scaled * normed, axis=-1, keepdims=True))
    return (inverse_std * (scaled - first_mean - normed * second_mean), normed)

def unshuffle(rows, tiles, tile_side):
    half_side = tile_side // 2
    blocks = rows.reshape(tiles, half_side, half_side, 2, 2, VW)
    blocks = jnp.transpose(blocks, (0, 1, 3, 2, 4, 5))
    return blocks.reshape(tiles * tile_side * tile_side, VW)

def reference(grad_proj, tile_counts, tile_home, saved_feat, ln_gain, layer_scale, attn_saved, proj_weight):
    capacity = SAMP * MAXT
    tile_rows = TILE_SIDE * TILE_SIDE // 4
    packed = grad_proj.reshape(N_DP, capacity, tile_rows, 4 * VW)
    features = saved_feat.reshape(N_DP, capacity * tile_rows, 4 * VW)
    live_total = lax.optimization_barrier(jnp.sum(tile_counts, axis=1)).astype(jnp.int32)
    source = jnp.argsort(tile_home, axis=1).astype(jnp.int32)

    def one_group(items):
        packed_group, source_group, total_group, feat_group = items
        routed = jnp.take(packed_group, source_group, axis=0).astype(jnp.float32)
        live_slot = (source_group < total_group)[:, None, None]
        upstream = jnp.where(live_slot, routed, jnp.zeros_like(routed))
        upstream = upstream.reshape(capacity * tile_rows, 4 * VW)
        grad_input, normed = layer_norm_back(upstream, feat_group, ln_gain)
        gain_part = lax.optimization_barrier(jnp.sum(upstream * normed, axis=0))
        vit_grad = unshuffle(grad_input, capacity, TILE_SIDE)
        residual_part = vit_grad.astype(jnp.bfloat16)
        branch_part = (vit_grad * layer_scale).astype(jnp.bfloat16)
        return (residual_part, branch_part, gain_part)
    residual_all, branch_all, gain_parts = lax.map(one_group, (packed, source, live_total, features))
    residual_grad = residual_all.reshape(N_DP * capacity * TILE_SIDE * TILE_SIDE, VW)
    branch = branch_all.reshape(N_DP * capacity * TILE_SIDE * TILE_SIDE, VW)
    gain_grad = lax.optimization_barrier(jnp.sum(gain_parts, axis=0))
    attn_grad = jnp.dot(branch, proj_weight, preferred_element_type=jnp.float32).astype(jnp.bfloat16)
    weight_total = lax.dot_general(branch, attn_saved, (((0,), (0,)), ((), ())), preferred_element_type=jnp.float32)
    proj_grad = jnp.pad(weight_total, ((0, COLPAD - VW), (0, 0)))
    return (residual_grad, attn_grad, proj_grad, gain_grad)
```

```python
import jax
import jax.numpy as jnp
from jax import lax
from jax.sharding import Mesh
from jax.sharding import PartitionSpec as P

VW = 3200
TILE_SIDE = 8
EPSILON = 1e-05
DP = ("z", "y")
MP = ("x", "c")


def layer_norm_back(upstream, features, ln_gain):
    values = features.astype(jnp.float32)
    centered = values - jnp.mean(values, axis=-1, keepdims=True)
    inverse_std = lax.rsqrt(jnp.mean(centered * centered, axis=-1, keepdims=True) + EPSILON)
    normed = centered * inverse_std
    scaled = upstream * ln_gain
    first_mean = jnp.mean(scaled, axis=-1, keepdims=True)
    second_mean = jnp.mean(scaled * normed, axis=-1, keepdims=True)
    return (inverse_std * (scaled - first_mean - normed * second_mean), normed)


def unshuffle(rows, tiles, tile_side):
    half_side = tile_side // 2
    blocks = rows.reshape(tiles, half_side, half_side, 2, 2, VW)
    blocks = jnp.transpose(blocks, (0, 1, 3, 2, 4, 5))
    return blocks.reshape(tiles * tile_side * tile_side, VW)


def sum_everywhere(part, axis):
    count = lax.axis_size(axis)
    terms = jnp.broadcast_to(part[None], (count,) + part.shape)
    return jnp.sum(lax.all_to_all(terms, axis, 0, 0), axis=0)


def body(
    grad_proj, tile_counts, tile_home, saved_feat, ln_gain, layer_scale, attn_saved, proj_weight
):
    mp_count = lax.axis_size("x") * lax.axis_size("c")
    z_count = lax.axis_size("z")
    y_count = lax.axis_size("y")
    dp_count = z_count * y_count
    mp_index = lax.axis_index(MP)
    capacity = tile_home.shape[1]
    rows_dev = grad_proj.shape[0]
    tiles_dev = capacity // mp_count
    tile_rows = rows_dev // tiles_dev
    live_total = jnp.sum(tile_counts)
    slot_ids = mp_index * tiles_dev + jnp.arange(tiles_dev, dtype=jnp.int32)
    matches = tile_home[0][None, :] == slot_ids[:, None]
    packed_ids = jnp.arange(capacity, dtype=jnp.int32)[None, :]
    source_tile = jnp.sum(jnp.where(matches, packed_ids, jnp.zeros_like(packed_ids)), axis=1)
    row_tile = jnp.repeat(source_tile, tile_rows)
    wanted = row_tile * tile_rows + jnp.tile(jnp.arange(tile_rows, dtype=jnp.int32), tiles_dev)
    row_live = row_tile < live_total
    pieces = lax.all_gather(grad_proj, MP, axis=0, tiled=True)
    columns = jnp.arange(pieces.shape[0], dtype=jnp.int32)
    select = ((wanted[:, None] == columns[None, :]) & row_live[:, None]).astype(jnp.bfloat16)
    upstream = jnp.dot(select, pieces, preferred_element_type=jnp.float32)
    grad_input, normed = layer_norm_back(upstream, saved_feat, ln_gain)
    gain_local = jnp.sum(upstream * normed, axis=0)
    vit_grad = unshuffle(grad_input, tiles_dev, TILE_SIDE)
    residual_grad = vit_grad.astype(jnp.bfloat16)
    branch = (vit_grad * layer_scale).astype(jnp.bfloat16)
    pieces = lax.all_gather(branch, MP, axis=0, tiled=True)

    gain_part = gain_local.reshape(mp_count, -1)
    gain_part = jnp.sum(lax.all_to_all(gain_part, MP, 0, 0), axis=0)
    gain_part = sum_everywhere(gain_part, "y")
    gain_part = sum_everywhere(gain_part, "z")
    terms = jnp.broadcast_to(gain_part[None], (mp_count,) + gain_part.shape)
    gain_grad = lax.all_to_all(terms, MP, 0, 0).reshape(-1)

    local_grad = jnp.dot(pieces, proj_weight, preferred_element_type=jnp.float32)
    weight_part = lax.dot_general(
        pieces, attn_saved, (((0,), (0,)), ((), ())), preferred_element_type=jnp.float32
    )
    block = -(-VW // dp_count)
    cols = weight_part.shape[1]
    padded = jnp.pad(weight_part, ((0, block * dp_count - VW), (0, 0))).astype(jnp.bfloat16)
    terms = padded.reshape(z_count, y_count, block, cols).transpose(1, 0, 2, 3)
    terms = lax.all_to_all(terms.reshape(y_count, z_count * block, cols), "y", 0, 0)
    part = jnp.sum(terms.astype(jnp.float32), axis=0).astype(jnp.bfloat16)
    terms = lax.all_to_all(part.reshape(z_count, block, cols), "z", 0, 0)
    proj_grad = jnp.sum(terms.astype(jnp.float32), axis=0)
    return (residual_grad, local_grad.astype(jnp.bfloat16), proj_grad, gain_grad)


def solution(mesh):
    shape = (12, 8, 4, 2)
    fine = Mesh(mesh.devices.reshape(shape), DP + MP)
    in_specs = (
        P(DP + MP, None),
        P(DP, None),
        P(DP, None),
        P(DP + MP, None),
        P(),
        P(),
        P(DP, MP),
        P(None, MP),
    )
    out_specs = (P(DP + MP, None), P(DP, MP), P(DP, MP), P())
    return jax.shard_map(body, mesh=fine, in_specs=in_specs, out_specs=out_specs, check_vma=False)
```

```python
import jax
import jax.numpy as jnp
from jax import lax
from jax.experimental import pallas as pl
from jax.experimental.pallas import tpu as pltpu
from jax.sharding import Mesh
from jax.sharding import PartitionSpec as P

VW = 3200
PW = 12800
EPSILON = 1e-05
DP = ("z", "y")
MP = ("x", "c")
NZ, NY, NMP = 12, 8, 8
BLOCK = 34
FEAT = NZ * BLOCK
WIDE = 512
TILES, PR, SUB, VT = 8, 16, 4, 64
VMEM = pltpu.CompilerParams(vmem_limit_bytes=48 * 1024 * 1024)
F32, BF16 = jnp.float32, jnp.bfloat16


def split3(value):
    high = value.astype(BF16).astype(F32)
    middle = (value - high).astype(BF16).astype(F32)
    low = (value - high - middle).astype(BF16).astype(F32)
    return high, middle, low


def cut_kernel(grad_ref, feat_ref, out_ref):
    values = feat_ref[...].astype(F32)
    mean = jnp.mean(values, axis=-1, keepdims=True)
    centered = values - mean
    inverse_std = lax.rsqrt(jnp.mean(centered * centered, axis=-1, keepdims=True) + EPSILON)
    marks = split3(mean) + split3(inverse_std)
    lane = lax.broadcasted_iota(jnp.int32, (PR, WIDE), 1)
    for sub in range(SUB):
        for part in range(NMP):
            low = sub * VW + part * FEAT
            start = low // 128 * 128
            width = min(640, PW - start)
            live = lane < min(FEAT, VW - part * FEAT)
            for which, ref in enumerate((grad_ref, feat_ref)):
                window = ref[:, start : start + width].astype(F32)
                if width < 640:
                    window = jnp.concatenate([window, jnp.zeros((PR, 640 - width), F32)], axis=1)
                if low > start:
                    window = pltpu.roll(window, 640 - (low - start), 1)
                chunk = jnp.where(live, window[:, :WIDE], 0.0)
                if which == 1:
                    for at, mark in enumerate(marks):
                        chunk = jnp.where(lane == FEAT + at, mark, chunk)
                row = which * VT + sub * PR
                out_ref[part, row : row + PR, :] = chunk.astype(BF16)


def slot_values(tile, source_ref, live_ref, recv_ref):
    grads = recv_ref[source_ref[tile], 0:VT, :].astype(F32)
    grads = jnp.where(live_ref[tile] > 0, grads, 0.0)
    feats = recv_ref[tile, VT : 2 * VT, :].astype(F32)
    marks = feats[0:PR, 384:512]
    lane = lax.broadcasted_iota(jnp.int32, (PR, 128), 1) + 384
    in_mean = (lane >= FEAT) & (lane < FEAT + 3)
    in_std = (lane >= FEAT + 3) & (lane < FEAT + 6)
    mean = jnp.sum(jnp.where(in_mean, marks, 0.0), axis=-1, keepdims=True)
    inverse_std = jnp.sum(jnp.where(in_std, marks, 0.0), axis=-1, keepdims=True)
    upstream = [grads[s * PR : (s + 1) * PR] for s in range(SUB)]
    normed = [(feats[s * PR : (s + 1) * PR] - mean) * inverse_std for s in range(SUB)]
    return upstream, normed, inverse_std


def sums_kernel(source_ref, live_ref, recv_ref, gain_ref, out_ref):
    lane = lax.broadcasted_iota(jnp.int32, (PR, 128), 1)
    rows = []
    for tile in range(TILES):
        upstream, normed, _ = slot_values(tile, source_ref, live_ref, recv_ref)
        first = jnp.zeros((PR, WIDE), F32)
        second = jnp.zeros((PR, WIDE), F32)
        for s in range(SUB):
            scaled = upstream[s] * gain_ref[s : s + 1, :]
            first = first + scaled
            second = second + scaled * normed[s]
        first = jnp.sum(first, axis=-1, keepdims=True)
        second = jnp.sum(second, axis=-1, keepdims=True)
        rows.append(jnp.where(lane == 0, first, jnp.where(lane == 1, second, 0.0)))
    turned = jnp.concatenate(rows, axis=0).T[0:8, :]
    for part in range(NMP):
        out_ref[part] = turned


def branch_kernel(
    source_ref, live_ref, recv_ref, gain_ref, scale_ref, sums_ref, attn_ref,
    branch_ref, residual_ref, gain_out_ref, terms_ref,
):
    total = sums_ref[0]
    for part in range(1, NMP):
        total = total + sums_ref[part]
    means = jnp.concatenate([total, jnp.zeros((120, 128), F32)], axis=0).T * (1.0 / PW)
    lane = lax.broadcasted_iota(jnp.int32, (PR, 128), 1)
    token = lax.broadcasted_iota(jnp.int32, (VT, VT), 0)
    place = lax.broadcasted_iota(jnp.int32, (VT, VT), 1)
    sub_of = ((token >> 3) & 1) * 2 + (token & 1)
    row_of = (token >> 4) * 4 + ((token >> 1) & 3)
    order = (place == sub_of * PR + row_of).astype(BF16)
    gains = [jnp.zeros((PR, WIDE), F32) for _ in range(SUB)]
    for tile in range(TILES):
        upstream, normed, inverse_std = slot_values(tile, source_ref, live_ref, recv_ref)
        own = means[tile * PR : (tile + 1) * PR]
        first = jnp.sum(jnp.where(lane == 0, own, 0.0), axis=-1, keepdims=True)
        second = jnp.sum(jnp.where(lane == 1, own, 0.0), axis=-1, keepdims=True)
        residual, branch = [], []
        for s in range(SUB):
            scaled = upstream[s] * gain_ref[s : s + 1, :]
            grad = inverse_std * (scaled - first - normed[s] * second)
            residual.append(grad.astype(BF16))
            branch.append((grad * scale_ref[...]).astype(BF16))
            gains[s] = gains[s] + upstream[s] * normed[s]
        residual = jnp.concatenate(residual, axis=0)
        branch = jnp.concatenate(branch, axis=0)
        residual = jnp.dot(order, residual, preferred_element_type=F32)
        branch = jnp.dot(order, branch, preferred_element_type=F32)
        residual_ref[tile] = residual.astype(BF16)
        branch_ref[tile * VT : (tile + 1) * VT, :] = branch.astype(BF16)
    gain_out_ref[...] = jnp.concatenate(
        [jnp.sum(g, axis=0, keepdims=True) for g in gains] + [jnp.zeros((4, WIDE), F32)], axis=0
    )
    turned = branch_ref[...].T
    for part in range(NMP):
        term = jnp.dot(turned, attn_ref[part], preferred_element_type=F32)
        terms_ref[part] = term[:FEAT].astype(BF16)


def whole(count):
    return [pl.BlockSpec(memory_space=pltpu.VMEM)] * count


def scalars(count):
    return [pl.BlockSpec(memory_space=pltpu.SMEM)] * count


def sum_everywhere(part, axis):
    count = lax.axis_size(axis)
    terms = jnp.broadcast_to(part[None], (count,) + part.shape)
    return jnp.sum(lax.all_to_all(terms, axis, 0, 0), axis=0)


def last_places():
    pairs = []
    for z in range(NZ):
        for y in range(NY):
            for part in range(NMP):
                pairs.append(((z * NY + y) * NMP + part, (NZ * part + z) * NMP + y))
    return pairs


def body(
    grad_proj, tile_counts, tile_home, saved_feat, ln_gain, layer_scale, attn_saved, proj_weight
):
    mp_index = lax.axis_index(MP)
    cols = attn_saved.shape[1]
    attn = lax.all_gather(attn_saved, MP, axis=0)

    send = pl.pallas_call(
        cut_kernel,
        out_shape=jax.ShapeDtypeStruct((NMP, 2 * VT, WIDE), BF16),
        in_specs=whole(2),
        out_specs=whole(1)[0],
        compiler_params=VMEM,
        name="cut",
    )(grad_proj, saved_feat)
    recv = lax.all_to_all(send, MP, 0, 0)

    slot_ids = jnp.arange(TILES, dtype=jnp.int32)
    matches = tile_home[0][None, :] == slot_ids[:, None]
    source = jnp.sum(jnp.where(matches, slot_ids[None, :], 0), axis=1).astype(jnp.int32)
    live = (source < jnp.sum(tile_counts)).astype(jnp.int32)
    pad = NMP * FEAT - VW
    gain = jnp.pad(ln_gain.reshape(SUB, VW), ((0, 0), (0, pad + WIDE - FEAT)))
    gain = lax.dynamic_slice_in_dim(gain, mp_index * FEAT, WIDE, axis=1)
    scale = jnp.pad(layer_scale, (0, pad + WIDE - FEAT))
    scale = lax.dynamic_slice_in_dim(scale, mp_index * FEAT, WIDE, axis=0)[None]
    inside = (jnp.arange(WIDE) < FEAT)[None]
    gain = jnp.where(inside, gain, 0.0)
    scale = jnp.where(inside, scale, 0.0)

    sums = pl.pallas_call(
        sums_kernel,
        out_shape=jax.ShapeDtypeStruct((NMP, 8, 128), F32),
        in_specs=scalars(2) + whole(2),
        out_specs=whole(1)[0],
        compiler_params=VMEM,
        name="sums",
    )(source, live, recv, gain)
    sums = lax.all_to_all(sums, MP, 0, 0)

    branch, residual, gain_part, terms = pl.pallas_call(
        branch_kernel,
        out_shape=(
            jax.ShapeDtypeStruct((TILES * VT, WIDE), BF16),
            jax.ShapeDtypeStruct((TILES, VT, WIDE), BF16),
            jax.ShapeDtypeStruct((8, WIDE), F32),
            jax.ShapeDtypeStruct((NMP, FEAT, cols), BF16),
        ),
        in_specs=scalars(2) + whole(5),
        out_specs=tuple(whole(4)),
        compiler_params=VMEM,
        name="branch",
    )(source, live, recv, gain, scale, sums, attn)

    terms = lax.all_to_all(terms, "y", 0, 0)
    part = jnp.sum(terms.astype(F32), axis=0).astype(BF16)
    terms = lax.all_to_all(part.reshape(NZ, BLOCK, cols), "z", 0, 0)
    part = jnp.sum(terms.astype(F32), axis=0)
    proj_grad = lax.ppermute(part, DP + MP, last_places())

    pieces = lax.all_gather(branch, MP, axis=0)
    pieces = jnp.transpose(pieces[:, :, :FEAT], (1, 0, 2)).reshape(TILES * VT, NMP * FEAT)
    attn_grad = jnp.dot(pieces[:, :VW], proj_weight, preferred_element_type=F32).astype(BF16)

    residual = lax.all_to_all(residual, MP, 0, 0)
    residual = jnp.transpose(residual[:, :, :FEAT], (1, 0, 2)).reshape(VT, NMP * FEAT)
    residual_grad = residual[:, :VW]

    gain_part = sum_everywhere(gain_part, "y")
    gain_part = sum_everywhere(gain_part, "z")
    gains = jnp.broadcast_to(gain_part[None], (NMP,) + gain_part.shape)
    gains = lax.all_to_all(gains, MP, 0, 0)[:, :SUB, :FEAT]
    gain_grad = jnp.transpose(gains, (1, 0, 2)).reshape(SUB, NMP * FEAT)[:, :VW].reshape(-1)
    return (residual_grad, attn_grad, proj_grad, gain_grad)


def solution(mesh):
    fine = Mesh(mesh.devices.reshape(NZ, NY, 4, 2), DP + MP)
    in_specs = (
        P(DP + MP, None),
        P(DP, None),
        P(DP, None),
        P(DP + MP, None),
        P(),
        P(),
        P(DP, MP),
        P(None, MP),
    )
    out_specs = (P(DP + MP, None), P(DP, MP), P(DP, MP), P())
    return jax.shard_map(body, mesh=fine, in_specs=in_specs, out_specs=out_specs, check_vma=False)
```

```python
import jax
import jax.numpy as jnp
from jax import lax
from jax.experimental import pallas as pl
from jax.experimental.pallas import tpu as pltpu
from jax.sharding import Mesh
from jax.sharding import PartitionSpec as P

VW = 3200
PW = 12800
EPSILON = 1e-05
DP = ("z", "y")
MP = ("x", "c")
NZ, NY, NMP = 12, 8, 8
BLOCK = 34
FEAT = NZ * BLOCK
WIDE = 512
TILES, PR, SUB, VT = 8, 16, 4, 64
VMEM = pltpu.CompilerParams(vmem_limit_bytes=48 * 1024 * 1024)
F32, BF16 = jnp.float32, jnp.bfloat16


def split3(value):
    high = value.astype(BF16).astype(F32)
    middle = (value - high).astype(BF16).astype(F32)
    low = (value - high - middle).astype(BF16).astype(F32)
    return high, middle, low


def cut_kernel(grad_hbm, feat_hbm, out_ref, grad_ref, feat_ref, sems):
    feat_copy = pltpu.make_async_copy(feat_hbm, feat_ref, sems.at[0])
    grad_copy = pltpu.make_async_copy(grad_hbm, grad_ref, sems.at[1])
    feat_copy.start()
    grad_copy.start()
    feat_copy.wait()
    values = feat_ref[...].astype(F32)
    mean = jnp.mean(values, axis=-1, keepdims=True)
    centered = values - mean
    inverse_std = lax.rsqrt(jnp.mean(centered * centered, axis=-1, keepdims=True) + EPSILON)
    marks = split3(mean) + split3(inverse_std)
    lane = lax.broadcasted_iota(jnp.int32, (PR, WIDE), 1)
    grad_copy.wait()
    for sub in range(SUB):
        for part in range(NMP):
            low = sub * VW + part * FEAT
            start = low // 128 * 128
            width = min(640, PW - start)
            live = lane < min(FEAT, VW - part * FEAT)
            for which, ref in enumerate((grad_ref, feat_ref)):
                window = ref[:, start : start + width].astype(F32)
                if width < 640:
                    window = jnp.concatenate([window, jnp.zeros((PR, 640 - width), F32)], axis=1)
                if low > start:
                    window = pltpu.roll(window, 640 - (low - start), 1)
                chunk = jnp.where(live, window[:, :WIDE], 0.0)
                if which == 1:
                    for at, mark in enumerate(marks):
                        chunk = jnp.where(lane == FEAT + at, mark, chunk)
                row = which * VT + sub * PR
                out_ref[part, row : row + PR, :] = chunk.astype(BF16)


def slot_values(tile, source_ref, live_ref, recv_ref):
    grads = recv_ref[source_ref[tile], 0:VT, :].astype(F32)
    grads = jnp.where(live_ref[tile] > 0, grads, 0.0)
    feats = recv_ref[tile, VT : 2 * VT, :].astype(F32)
    marks = feats[0:PR, 384:512]
    lane = lax.broadcasted_iota(jnp.int32, (PR, 128), 1) + 384
    in_mean = (lane >= FEAT) & (lane < FEAT + 3)
    in_std = (lane >= FEAT + 3) & (lane < FEAT + 6)
    mean = jnp.sum(jnp.where(in_mean, marks, 0.0), axis=-1, keepdims=True)
    inverse_std = jnp.sum(jnp.where(in_std, marks, 0.0), axis=-1, keepdims=True)
    upstream = [grads[s * PR : (s + 1) * PR] for s in range(SUB)]
    normed = [(feats[s * PR : (s + 1) * PR] - mean) * inverse_std for s in range(SUB)]
    return upstream, normed, inverse_std


def sums_kernel(source_ref, live_ref, recv_ref, gain_ref, out_ref):
    lane = lax.broadcasted_iota(jnp.int32, (PR, 128), 1)
    rows = []
    for tile in range(TILES):
        upstream, normed, _ = slot_values(tile, source_ref, live_ref, recv_ref)
        first = jnp.zeros((PR, WIDE), F32)
        second = jnp.zeros((PR, WIDE), F32)
        for s in range(SUB):
            scaled = upstream[s] * gain_ref[s : s + 1, :]
            first = first + scaled
            second = second + scaled * normed[s]
        first = jnp.sum(first, axis=-1, keepdims=True)
        second = jnp.sum(second, axis=-1, keepdims=True)
        rows.append(jnp.where(lane == 0, first, jnp.where(lane == 1, second, 0.0)))
    turned = jnp.concatenate(rows, axis=0).T[0:8, :]
    for part in range(NMP):
        out_ref[part] = turned


def dot_nt(left, right):
    return lax.dot_general(left, right, (((1,), (1,)), ((), ())), preferred_element_type=F32)


ROWS1, ROWS2, ROWS3, GAIN = 416, 208, 64, 16
AT2, AT3, AT4, AT5 = ROWS1, ROWS1 + ROWS2, ROWS1 + ROWS2 + ROWS3, ROWS1 + ROWS2 + ROWS3 + GAIN
MESSAGE = AT5 + GAIN


def branch_kernel(
    source_ref, live_ref, recv_ref, gain_ref, scale_ref, sums_ref, attn_hbm,
    turned_ref, terms_hbm, attn_ref, terms_ref, branch_ref, attn_sem, terms_sems,
):
    attn_copy = pltpu.make_async_copy(attn_hbm, attn_ref, attn_sem)
    attn_copy.start()
    total = sums_ref[0]
    for part in range(1, NMP):
        total = total + sums_ref[part]
    means = jnp.concatenate([total, jnp.zeros((120, 128), F32)], axis=0).T * (1.0 / PW)
    lane = lax.broadcasted_iota(jnp.int32, (PR, 128), 1)
    token = lax.broadcasted_iota(jnp.int32, (VT, VT), 0)
    place = lax.broadcasted_iota(jnp.int32, (VT, VT), 1)
    sub_of = ((token >> 3) & 1) * 2 + (token & 1)
    row_of = (token >> 4) * 4 + ((token >> 1) & 3)
    order = (place == sub_of * PR + row_of).astype(BF16)
    gains = [jnp.zeros((PR, WIDE), F32) for _ in range(SUB)]
    for tile in range(TILES):
        upstream, normed, inverse_std = slot_values(tile, source_ref, live_ref, recv_ref)
        own = means[tile * PR : (tile + 1) * PR]
        first = jnp.sum(jnp.where(lane == 0, own, 0.0), axis=-1, keepdims=True)
        second = jnp.sum(jnp.where(lane == 1, own, 0.0), axis=-1, keepdims=True)
        branch = []
        for s in range(SUB):
            scaled = upstream[s] * gain_ref[s : s + 1, :]
            grad = inverse_std * (scaled - first - normed[s] * second)
            branch.append((grad * scale_ref[...]).astype(BF16))
            gains[s] = gains[s] + upstream[s] * normed[s]
        branch = jnp.dot(order, jnp.concatenate(branch, axis=0), preferred_element_type=F32)
        branch_ref[tile * VT : (tile + 1) * VT, :] = branch.astype(BF16)
    gain = jnp.concatenate([jnp.sum(g, axis=0, keepdims=True) for g in gains], axis=0)
    gain = jnp.concatenate([gain[:, q * 128 : (q + 1) * 128] for q in range(4)], axis=0)
    gain_high = gain.astype(BF16)
    gain_low = (gain - gain_high.astype(F32)).astype(BF16)
    turned = branch_ref[...].T
    turned_ref[...] = turned[:FEAT]
    attn_copy.wait()
    half = lax.broadcasted_iota(jnp.int32, (ROWS2, 128), 1) < 64
    group = lax.broadcasted_iota(jnp.int32, (ROWS3, 128), 1) >> 4
    copies = []
    for part in range(NMP):
        attn = attn_ref[part]
        terms_ref[part, 0:AT2, :] = dot_nt(turned[:ROWS1], attn[0:128]).astype(BF16)
        second = dot_nt(turned[:ROWS1], jnp.concatenate([attn[128:192]] * 2, axis=0))
        second = jnp.where(half, second[:ROWS2], second[ROWS2:])
        terms_ref[part, AT2:AT3, :] = second.astype(BF16)
        third = dot_nt(turned[: 7 * ROWS3], jnp.concatenate([attn[192:208]] * 8, axis=0))
        packed = third[:ROWS3]
        for g in range(1, 7):
            packed = jnp.where(group == g, third[g * ROWS3 : (g + 1) * ROWS3], packed)
        terms_ref[part, AT3:AT4, :] = packed.astype(BF16)
        terms_ref[part, AT4:AT5, :] = gain_high
        terms_ref[part, AT5:MESSAGE, :] = gain_low
        copies.append(
            pltpu.make_async_copy(terms_ref.at[part], terms_hbm.at[part], terms_sems.at[part])
        )
        copies[-1].start()
    for copy in copies:
        copy.wait()


def fold_kernel(recv_ref, out_ref, wide_ref):
    total = recv_ref[0].astype(F32)
    for part in range(1, NY):
        total = total + recv_ref[part].astype(F32)
    second = total[AT2:AT3]
    second = jnp.concatenate([second, pltpu.roll(second, 64, 1)], axis=0)
    third = total[AT3:AT4]
    third = [pltpu.roll(third, (64 - 16 * g) % 128, 1) if g != 4 else third for g in range(7)]
    third = jnp.concatenate(third, axis=0)[:ROWS1]
    lane = lax.broadcasted_iota(jnp.int32, (ROWS1, 128), 1)
    wide_ref[:, 0:128] = total[0:ROWS1]
    wide_ref[:, 128:256] = jnp.where(lane < 64, second, jnp.where(lane < 80, third, 0.0))
    gain = total[AT4:AT5] + total[AT5:MESSAGE]
    gain = jnp.concatenate([gain[0:8], gain[8:16]], axis=1)
    for z in range(NZ):
        rows = wide_ref[z * BLOCK : z * BLOCK + 40, :]
        out_ref[z] = jnp.concatenate([rows, gain], axis=0).astype(BF16)


def settle_kernel(recv_ref, block_ref, gain_ref):
    total = recv_ref[0].astype(F32)
    for part in range(1, NZ):
        total = total + recv_ref[part].astype(F32)
    block_ref[...] = total[0:BLOCK, 0 : block_ref.shape[1]]
    gain = jnp.concatenate([total[40:48, 0:128], total[40:48, 128:256]], axis=0)
    for part in range(NMP):
        gain_ref[part] = gain


def spread_kernel(gain_ref, out_ref, wide_ref):
    wide_ref[...] = jnp.zeros_like(wide_ref)
    for part in range(NMP):
        gain = gain_ref[part]
        pieces = [gain[q * SUB : (q + 1) * SUB] for q in range(4)] + [jnp.zeros((SUB, 128), F32)]
        low = part * FEAT
        start = low // 128 * 128
        pieces = jnp.concatenate(pieces, axis=1)
        if low > start:
            pieces = pltpu.roll(pieces, low - start, 1)
        wide_ref[:, start : start + 640] += pieces
    out_ref[...] = wide_ref[:, 0:VW]


def gathered_kernel(own_ref, turned_ref, weight_ref, scale_ref, attn_ref, residual_ref):
    attn = jnp.dot(weight_ref[...], turned_ref[0:VW, :], preferred_element_type=F32)
    attn_ref[...] = attn.astype(BF16)
    own = own_ref[0]
    at = pl.multiple_of((own >> 1) * 128, 128)
    tokens = turned_ref[0:VW, pl.ds(at, 128)].astype(F32).T
    tokens = jnp.where((own & 1) == 0, tokens[0:VT], tokens[VT : 2 * VT])
    residual_ref[...] = (tokens / scale_ref[...]).astype(BF16)


def whole(count):
    return [pl.BlockSpec(memory_space=pltpu.VMEM)] * count


def scalars(count):
    return [pl.BlockSpec(memory_space=pltpu.SMEM)] * count


def last_places():
    pairs = []
    for z in range(NZ):
        for y in range(NY):
            for part in range(NMP):
                pairs.append(((z * NY + y) * NMP + part, (NZ * part + z) * NMP + y))
    return pairs


def in_hbm(count):
    return [pl.BlockSpec(memory_space=pltpu.HBM)] * count


def body(
    grad_proj, tile_counts, tile_home, saved_feat, ln_gain, layer_scale, attn_saved, proj_weight
):
    mp_index = lax.axis_index(MP)
    cols = attn_saved.shape[1]
    attn = lax.all_gather(attn_saved.T, MP, axis=0)

    send = pl.pallas_call(
        cut_kernel,
        out_shape=jax.ShapeDtypeStruct((NMP, 2 * VT, WIDE), BF16),
        in_specs=in_hbm(2),
        out_specs=whole(1)[0],
        scratch_shapes=[
            pltpu.VMEM((PR, PW), BF16),
            pltpu.VMEM((PR, PW), BF16),
            pltpu.SemaphoreType.DMA((2,)),
        ],
        compiler_params=VMEM,
        name="cut",
    )(grad_proj, saved_feat)
    recv = lax.all_to_all(send, MP, 0, 0)

    slot_ids = jnp.arange(TILES, dtype=jnp.int32)
    matches = tile_home[0][None, :] == slot_ids[:, None]
    source = jnp.sum(jnp.where(matches, slot_ids[None, :], 0), axis=1).astype(jnp.int32)
    live = (source < jnp.sum(tile_counts)).astype(jnp.int32)
    pad = NMP * FEAT - VW
    gain = jnp.pad(ln_gain.reshape(SUB, VW), ((0, 0), (0, pad + WIDE - FEAT)))
    gain = lax.dynamic_slice_in_dim(gain, mp_index * FEAT, WIDE, axis=1)
    scale = jnp.pad(layer_scale, (0, pad + WIDE - FEAT))
    scale = lax.dynamic_slice_in_dim(scale, mp_index * FEAT, WIDE, axis=0)[None]
    inside = (jnp.arange(WIDE) < FEAT)[None]
    gain = jnp.where(inside, gain, 0.0)
    scale = jnp.where(inside, scale, 0.0)

    sums = pl.pallas_call(
        sums_kernel,
        out_shape=jax.ShapeDtypeStruct((NMP, 8, 128), F32),
        in_specs=scalars(2) + whole(2),
        out_specs=whole(1)[0],
        compiler_params=VMEM,
        name="sums",
    )(source, live, recv, gain)
    sums = lax.all_to_all(sums, MP, 0, 0)

    turned, terms = pl.pallas_call(
        branch_kernel,
        out_shape=(
            jax.ShapeDtypeStruct((FEAT, TILES * VT), BF16),
            jax.ShapeDtypeStruct((NMP, MESSAGE, 128), BF16),
        ),
        in_specs=scalars(2) + whole(4) + in_hbm(1),
        out_specs=(whole(1)[0], in_hbm(1)[0]),
        scratch_shapes=[
            pltpu.VMEM((NMP, cols, TILES * VT), BF16),
            pltpu.VMEM((NMP, MESSAGE, 128), BF16),
            pltpu.VMEM((TILES * VT, WIDE), BF16),
            pltpu.SemaphoreType.DMA,
            pltpu.SemaphoreType.DMA((NMP,)),
        ],
        compiler_params=VMEM,
        name="branch",
    )(source, live, recv, gain, scale, sums, attn)

    terms = lax.all_to_all(terms, "y", 0, 0)
    terms = pl.pallas_call(
        fold_kernel,
        out_shape=jax.ShapeDtypeStruct((NZ, 48, 256), BF16),
        in_specs=whole(1),
        out_specs=whole(1)[0],
        scratch_shapes=[pltpu.VMEM((ROWS1, 256), F32)],
        compiler_params=VMEM,
        name="fold",
    )(terms)
    terms = lax.all_to_all(terms, "z", 0, 0)

    turned = lax.all_gather(turned, MP, axis=0, tiled=True)
    attn_grad, residual_grad = pl.pallas_call(
        gathered_kernel,
        out_shape=(
            jax.ShapeDtypeStruct((cols, TILES * VT), BF16),
            jax.ShapeDtypeStruct((VT, VW), BF16),
        ),
        in_specs=scalars(1) + whole(3),
        out_specs=tuple(whole(2)),
        compiler_params=VMEM,
        name="gathered",
    )(mp_index.astype(jnp.int32)[None], turned, proj_weight.T, layer_scale[None])

    terms, attn_grad, residual_grad = lax.optimization_barrier((terms, attn_grad, residual_grad))
    part, gains = pl.pallas_call(
        settle_kernel,
        out_shape=(
            jax.ShapeDtypeStruct((BLOCK, cols), F32),
            jax.ShapeDtypeStruct((NMP, GAIN, 128), F32),
        ),
        in_specs=whole(1),
        out_specs=tuple(whole(2)),
        compiler_params=VMEM,
        name="settle",
    )(terms)

    proj_grad = lax.ppermute(part, DP + MP, last_places())
    gains = lax.all_to_all(gains, MP, 0, 0)
    gain_grad = pl.pallas_call(
        spread_kernel,
        out_shape=jax.ShapeDtypeStruct((SUB, VW), F32),
        in_specs=whole(1),
        out_specs=whole(1)[0],
        scratch_shapes=[pltpu.VMEM((SUB, 3456), F32)],
        compiler_params=VMEM,
        name="spread",
    )(gains)
    return (residual_grad, attn_grad.T, proj_grad, gain_grad.reshape(-1))


def solution(mesh):
    fine = Mesh(mesh.devices.reshape(NZ, NY, 4, 2), DP + MP)
    in_specs = (
        P(DP + MP, None),
        P(DP, None),
        P(DP, None),
        P(DP + MP, None),
        P(),
        P(),
        P(DP, MP),
        P(None, MP),
    )
    out_specs = (P(DP + MP, None), P(DP, MP), P(DP, MP), P())
    return jax.shard_map(body, mesh=fine, in_specs=in_specs, out_specs=out_specs, check_vma=False)
```

```python
import jax
import jax.numpy as jnp
from jax import lax
from jax.experimental import pallas as pl
from jax.experimental.pallas import tpu as pltpu
from jax.sharding import Mesh
from jax.sharding import PartitionSpec as P

VW = 3200
PW = 12800
EPSILON = 1e-05
DP = ("z", "y")
MP = ("x", "c")
NZ, NY, NMP = 12, 8, 8
BLOCK = 34
FEAT = NZ * BLOCK
WIDE = 512
REST = 384
TILES, PR, SUB, VT = 8, 16, 4, 64
VMEM = pltpu.CompilerParams(vmem_limit_bytes=48 * 1024 * 1024)
F32, BF16 = jnp.float32, jnp.bfloat16


def split3(value):
    high = value.astype(BF16).astype(F32)
    middle = (value - high).astype(BF16).astype(F32)
    low = (value - high - middle).astype(BF16).astype(F32)
    return high, middle, low


def cut_kernel(grad_hbm, feat_hbm, out_ref, grad_ref, feat_ref, sems):
    feat_copy = pltpu.make_async_copy(feat_hbm, feat_ref, sems.at[0])
    grad_copy = pltpu.make_async_copy(grad_hbm, grad_ref, sems.at[1])
    feat_copy.start()
    grad_copy.start()
    feat_copy.wait()
    values = feat_ref[...].astype(F32)
    mean = jnp.mean(values, axis=-1, keepdims=True)
    centered = values - mean
    inverse_std = lax.rsqrt(jnp.mean(centered * centered, axis=-1, keepdims=True) + EPSILON)
    marks = split3(mean) + split3(inverse_std)
    lane = lax.broadcasted_iota(jnp.int32, (PR, WIDE), 1)
    grad_copy.wait()
    for part in range(NMP):
        rest = [jnp.zeros((PR, 128), F32), jnp.zeros((PR, 128), F32)]
        live = lane < min(FEAT, VW - part * FEAT)
        for sub in range(SUB):
            low = sub * VW + part * FEAT
            start = low // 128 * 128
            width = min(640, PW - start)
            for which, ref in enumerate((grad_ref, feat_ref)):
                window = ref[:, start : start + width].astype(F32)
                if width < 640:
                    window = jnp.concatenate([window, jnp.zeros((PR, 640 - width), F32)], axis=1)
                if low > start:
                    window = pltpu.roll(window, 640 - (low - start), 1)
                chunk = jnp.where(live, window[:, :WIDE], 0.0)
                if which == 1 and sub == 0:
                    for at, mark in enumerate(marks):
                        chunk = jnp.where(lane == FEAT + at, mark, chunk)
                row = which * VT + sub * PR
                for tile in range(3):
                    at = tile * 2 * VT + row
                    out_ref[part, at : at + PR, :] = chunk[:, tile * 128 : tile * 128 + 128].astype(BF16)
                group = row // 32
                last = chunk[:, 384:512]
                rest[sub % 2] += pltpu.roll(last, 32 * group, 1) if group else last
        out_ref[part, REST : REST + PR, :] = rest[0].astype(BF16)
        out_ref[part, REST + PR : REST + 2 * PR, :] = rest[1].astype(BF16)


def unpack(ref, tile, which):
    at = [q * 2 * VT + which * VT for q in range(3)]
    pieces = [ref[tile, r : r + VT, :].astype(F32) for r in at]
    rest = ref[tile, REST : REST + 2 * PR, :].astype(F32)
    turn = (128 - 64 * which) % 128
    rest = jnp.concatenate(
        [pltpu.roll(rest, turn, 1) if turn else rest, pltpu.roll(rest, (turn + 96) % 128, 1)], axis=0
    )
    return pieces, rest


def slot_values(tile, source_ref, live_ref, recv_ref):
    pieces, rest = unpack(recv_ref, source_ref[tile], 0)
    rest = jnp.where(lax.broadcasted_iota(jnp.int32, (VT, 128), 1) < FEAT - 384, rest, 0.0)
    grads = jnp.concatenate(pieces + [rest], axis=1)
    grads = jnp.where(live_ref[tile] > 0, grads, 0.0)
    pieces, rest = unpack(recv_ref, tile, 1)
    feats = jnp.concatenate(pieces + [rest], axis=1)
    marks = rest[0:PR]
    lane = lax.broadcasted_iota(jnp.int32, (PR, 128), 1) + 384
    in_mean = (lane >= FEAT) & (lane < FEAT + 3)
    in_std = (lane >= FEAT + 3) & (lane < FEAT + 6)
    mean = jnp.sum(jnp.where(in_mean, marks, 0.0), axis=-1, keepdims=True)
    inverse_std = jnp.sum(jnp.where(in_std, marks, 0.0), axis=-1, keepdims=True)
    upstream = [grads[s * PR : (s + 1) * PR] for s in range(SUB)]
    normed = [(feats[s * PR : (s + 1) * PR] - mean) * inverse_std for s in range(SUB)]
    return upstream, normed, inverse_std


def sums_kernel(source_ref, live_ref, recv_ref, gain_ref, out_ref):
    lane = lax.broadcasted_iota(jnp.int32, (PR, 128), 1)
    rows = []
    for tile in range(TILES):
        upstream, normed, _ = slot_values(tile, source_ref, live_ref, recv_ref)
        first = jnp.zeros((PR, WIDE), F32)
        second = jnp.zeros((PR, WIDE), F32)
        for s in range(SUB):
            scaled = upstream[s] * gain_ref[s : s + 1, :]
            first = first + scaled
            second = second + scaled * normed[s]
        first = jnp.sum(first, axis=-1, keepdims=True)
        second = jnp.sum(second, axis=-1, keepdims=True)
        rows.append(jnp.where(lane == 0, first, jnp.where(lane == 1, second, 0.0)))
    turned = jnp.concatenate(rows, axis=0).T[0:8, :]
    for part in range(NMP):
        out_ref[part] = turned


COLS, GROUP, GAIN = 208, 48, 16
AT1, AT2, AT3 = COLS, 2 * COLS, 3 * COLS
AT4 = AT3 + GROUP
AT5 = AT4 + GAIN
MESSAGE = AT5 + GAIN


def branch_kernel(
    source_ref, live_ref, recv_ref, gain_ref, scale_ref, sums_ref, attn_hbm,
    turned_ref, terms_hbm, attn_ref, terms_ref, branch_ref, attn_sem, terms_sems,
):
    attn_copy = pltpu.make_async_copy(attn_hbm, attn_ref, attn_sem)
    attn_copy.start()
    total = sums_ref[0]
    for part in range(1, NMP):
        total = total + sums_ref[part]
    means = jnp.concatenate([total, jnp.zeros((120, 128), F32)], axis=0).T * (1.0 / PW)
    lane = lax.broadcasted_iota(jnp.int32, (PR, 128), 1)
    token = lax.broadcasted_iota(jnp.int32, (VT, VT), 0)
    place = lax.broadcasted_iota(jnp.int32, (VT, VT), 1)
    sub_of = ((token >> 3) & 1) * 2 + (token & 1)
    row_of = (token >> 4) * 4 + ((token >> 1) & 3)
    order = (place == sub_of * PR + row_of).astype(BF16)
    gains = [jnp.zeros((PR, WIDE), F32) for _ in range(SUB)]
    for tile in range(TILES):
        upstream, normed, inverse_std = slot_values(tile, source_ref, live_ref, recv_ref)
        own = means[tile * PR : (tile + 1) * PR]
        first = jnp.sum(jnp.where(lane == 0, own, 0.0), axis=-1, keepdims=True)
        second = jnp.sum(jnp.where(lane == 1, own, 0.0), axis=-1, keepdims=True)
        branch = []
        for s in range(SUB):
            scaled = upstream[s] * gain_ref[s : s + 1, :]
            grad = inverse_std * (scaled - first - normed[s] * second)
            branch.append((grad * scale_ref[...]).astype(BF16))
            gains[s] = gains[s] + upstream[s] * normed[s]
        branch = jnp.dot(order, jnp.concatenate(branch, axis=0), preferred_element_type=F32)
        branch_ref[tile * VT : (tile + 1) * VT, :] = branch.astype(BF16)
    gain = jnp.concatenate([jnp.sum(g, axis=0, keepdims=True) for g in gains], axis=0)
    gain = jnp.concatenate([gain[:, q * 128 : (q + 1) * 128] for q in range(4)], axis=0)
    gain_high = gain.astype(BF16)
    gain_low = (gain - gain_high.astype(F32)).astype(BF16)
    attn_copy.wait()
    copies = []
    for part in range(NMP):
        term = jnp.dot(attn_ref[part], branch_ref[...], preferred_element_type=F32)
        for q in range(3):
            terms_ref[part, q * COLS : (q + 1) * COLS, :] = term[:, q * 128 : q * 128 + 128].astype(BF16)
        last = term[:, 384:512]
        rest = last[0:GROUP]
        for g in range(1, 4):
            rest = rest + pltpu.roll(last[g * GROUP : (g + 1) * GROUP], 24 * g, 1)
        tail = pltpu.roll(last[4 * GROUP : COLS], 96, 1)
        rest = jnp.concatenate([rest[0:16] + tail, rest[16:]], axis=0)
        terms_ref[part, AT3:AT4, :] = rest.astype(BF16)
        terms_ref[part, AT4:AT5, :] = gain_high
        terms_ref[part, AT5:MESSAGE, :] = gain_low
        copies.append(
            pltpu.make_async_copy(terms_ref.at[part], terms_hbm.at[part], terms_sems.at[part])
        )
        copies[-1].start()
    turned_ref[...] = branch_ref[...].T[:FEAT]
    for copy in copies:
        copy.wait()


def fold_kernel(recv_ref, out_ref, wide_ref):
    total = recv_ref[0].astype(F32)
    for part in range(1, NY):
        total = total + recv_ref[part].astype(F32)
    rest = total[AT3:AT4]
    rest = [rest] + [pltpu.roll(rest, 128 - 24 * g, 1) for g in range(1, 5)]
    rest = jnp.concatenate(rest[:4] + [rest[4][0:16]], axis=0)
    wide = jnp.concatenate([total[0:AT1], total[AT1:AT2], total[AT2:AT3], rest], axis=1)
    wide = jnp.concatenate([wide, jnp.zeros((256 - COLS, WIDE), F32)], axis=0)
    wide_ref[...] = wide.T
    gain = total[AT4:AT5] + total[AT5:MESSAGE]
    gain = jnp.concatenate([gain[0:8], gain[8:16]], axis=1)
    for z in range(NZ):
        rows = wide_ref[z * BLOCK : z * BLOCK + 40, :]
        out_ref[z] = jnp.concatenate([rows, gain], axis=0).astype(BF16)


def settle_kernel(recv_ref, block_ref, gain_ref):
    total = recv_ref[0].astype(F32)
    for part in range(1, NZ):
        total = total + recv_ref[part].astype(F32)
    block_ref[...] = total[0:BLOCK, 0 : block_ref.shape[1]]
    gain = jnp.concatenate([total[40:48, 0:128], total[40:48, 128:256]], axis=0)
    for part in range(NMP):
        gain_ref[part] = gain


def spread_kernel(gain_ref, out_ref, wide_ref):
    wide_ref[...] = jnp.zeros_like(wide_ref)
    for part in range(NMP):
        gain = gain_ref[part]
        pieces = [gain[q * SUB : (q + 1) * SUB] for q in range(4)] + [jnp.zeros((SUB, 128), F32)]
        low = part * FEAT
        start = low // 128 * 128
        pieces = jnp.concatenate(pieces, axis=1)
        if low > start:
            pieces = pltpu.roll(pieces, low - start, 1)
        wide_ref[:, start : start + 640] += pieces
    out_ref[...] = wide_ref[:, 0:VW]


def gathered_kernel(own_ref, turned_ref, weight_ref, scale_ref, attn_ref, residual_ref):
    attn = jnp.dot(weight_ref[...], turned_ref[0:VW, :], preferred_element_type=F32)
    attn_ref[...] = attn.astype(BF16)
    own = own_ref[0]
    at = pl.multiple_of((own >> 1) * 128, 128)
    tokens = turned_ref[0:VW, pl.ds(at, 128)].astype(F32).T
    tokens = jnp.where((own & 1) == 0, tokens[0:VT], tokens[VT : 2 * VT])
    residual_ref[...] = (tokens / scale_ref[...]).astype(BF16)


def whole(count):
    return [pl.BlockSpec(memory_space=pltpu.VMEM)] * count


def scalars(count):
    return [pl.BlockSpec(memory_space=pltpu.SMEM)] * count


def last_places():
    pairs = []
    for z in range(NZ):
        for y in range(NY):
            for part in range(NMP):
                pairs.append(((z * NY + y) * NMP + part, (NZ * part + z) * NMP + y))
    return pairs


def in_hbm(count):
    return [pl.BlockSpec(memory_space=pltpu.HBM)] * count


def body(
    grad_proj, tile_counts, tile_home, saved_feat, ln_gain, layer_scale, attn_saved, proj_weight
):
    mp_index = lax.axis_index(MP)
    cols = attn_saved.shape[1]
    attn = lax.all_gather(attn_saved.T, MP, axis=0)

    send = pl.pallas_call(
        cut_kernel,
        out_shape=jax.ShapeDtypeStruct((NMP, REST + 2 * PR, 128), BF16),
        in_specs=in_hbm(2),
        out_specs=whole(1)[0],
        scratch_shapes=[
            pltpu.VMEM((PR, PW), BF16),
            pltpu.VMEM((PR, PW), BF16),
            pltpu.SemaphoreType.DMA((2,)),
        ],
        compiler_params=pltpu.CompilerParams(vmem_limit_bytes=60 * 1024 * 1024),
        name="cut",
    )(grad_proj, saved_feat)
    recv = lax.all_to_all(send, MP, 0, 0)

    slot_ids = jnp.arange(TILES, dtype=jnp.int32)
    matches = tile_home[0][None, :] == slot_ids[:, None]
    source = jnp.sum(jnp.where(matches, slot_ids[None, :], 0), axis=1).astype(jnp.int32)
    live = (source < jnp.sum(tile_counts)).astype(jnp.int32)
    pad = NMP * FEAT - VW
    gain = jnp.pad(ln_gain.reshape(SUB, VW), ((0, 0), (0, pad + WIDE - FEAT)))
    gain = lax.dynamic_slice_in_dim(gain, mp_index * FEAT, WIDE, axis=1)
    scale = jnp.pad(layer_scale, (0, pad + WIDE - FEAT))
    scale = lax.dynamic_slice_in_dim(scale, mp_index * FEAT, WIDE, axis=0)[None]
    inside = (jnp.arange(WIDE) < FEAT)[None]
    gain = jnp.where(inside, gain, 0.0)
    scale = jnp.where(inside, scale, 0.0)

    sums = pl.pallas_call(
        sums_kernel,
        out_shape=jax.ShapeDtypeStruct((NMP, 8, 128), F32),
        in_specs=scalars(2) + whole(2),
        out_specs=whole(1)[0],
        compiler_params=VMEM,
        name="sums",
    )(source, live, recv, gain)
    sums = lax.all_to_all(sums, MP, 0, 0)

    turned, terms = pl.pallas_call(
        branch_kernel,
        out_shape=(
            jax.ShapeDtypeStruct((FEAT, TILES * VT), BF16),
            jax.ShapeDtypeStruct((NMP, MESSAGE, 128), BF16),
        ),
        in_specs=scalars(2) + whole(4) + in_hbm(1),
        out_specs=(whole(1)[0], in_hbm(1)[0]),
        scratch_shapes=[
            pltpu.VMEM((NMP, cols, TILES * VT), BF16),
            pltpu.VMEM((NMP, MESSAGE, 128), BF16),
            pltpu.VMEM((TILES * VT, WIDE), BF16),
            pltpu.SemaphoreType.DMA,
            pltpu.SemaphoreType.DMA((NMP,)),
        ],
        compiler_params=VMEM,
        name="branch",
    )(source, live, recv, gain, scale, sums, attn)

    terms = lax.all_to_all(terms, "y", 0, 0)
    terms = pl.pallas_call(
        fold_kernel,
        out_shape=jax.ShapeDtypeStruct((NZ, 48, 256), BF16),
        in_specs=whole(1),
        out_specs=whole(1)[0],
        scratch_shapes=[pltpu.VMEM((WIDE, 256), F32)],
        compiler_params=VMEM,
        name="fold",
    )(terms)
    terms = lax.all_to_all(terms, "z", 0, 0)

    turned = lax.all_gather(turned, MP, axis=0, tiled=True)
    attn_grad, residual_grad = pl.pallas_call(
        gathered_kernel,
        out_shape=(
            jax.ShapeDtypeStruct((cols, TILES * VT), BF16),
            jax.ShapeDtypeStruct((VT, VW), BF16),
        ),
        in_specs=scalars(1) + whole(3),
        out_specs=tuple(whole(2)),
        compiler_params=VMEM,
        name="gathered",
    )(mp_index.astype(jnp.int32)[None], turned, proj_weight.T, layer_scale[None])

    terms, attn_grad, residual_grad = lax.optimization_barrier((terms, attn_grad, residual_grad))
    part, gains = pl.pallas_call(
        settle_kernel,
        out_shape=(
            jax.ShapeDtypeStruct((BLOCK, cols), F32),
            jax.ShapeDtypeStruct((NMP, GAIN, 128), F32),
        ),
        in_specs=whole(1),
        out_specs=tuple(whole(2)),
        compiler_params=VMEM,
        name="settle",
    )(terms)

    proj_grad = lax.ppermute(part, DP + MP, last_places())
    gains = lax.all_to_all(gains, MP, 0, 0)
    gain_grad = pl.pallas_call(
        spread_kernel,
        out_shape=jax.ShapeDtypeStruct((SUB, VW), F32),
        in_specs=whole(1),
        out_specs=whole(1)[0],
        scratch_shapes=[pltpu.VMEM((SUB, 3456), F32)],
        compiler_params=VMEM,
        name="spread",
    )(gains)
    return (residual_grad, attn_grad.T, proj_grad, gain_grad.reshape(-1))


def solution(mesh):
    fine = Mesh(mesh.devices.reshape(NZ, NY, 4, 2), DP + MP)
    in_specs = (
        P(DP + MP, None),
        P(DP, None),
        P(DP, None),
        P(DP + MP, None),
        P(),
        P(),
        P(DP, MP),
        P(None, MP),
    )
    out_specs = (P(DP + MP, None), P(DP, MP), P(DP, MP), P())
    return jax.shard_map(body, mesh=fine, in_specs=in_specs, out_specs=out_specs, check_vma=False)
```

```python
import jax
import jax.numpy as jnp
from jax import lax
from jax.experimental import pallas as pl
from jax.experimental.pallas import tpu as pltpu
from jax.sharding import Mesh
from jax.sharding import PartitionSpec as P

VW = 3200
PW = 12800
EPSILON = 1e-05
DP = ("z", "y")
MP = ("x", "c")
NZ, NY, NMP = 12, 8, 8
BLOCK = 34
FEAT = NZ * BLOCK
WIDE = 512
ROWS = 416
REST = 384
TILES, PR, SUB, VT = 8, 16, 4, 64
VMEM = pltpu.CompilerParams(vmem_limit_bytes=48 * 1024 * 1024)
F32, BF16 = jnp.float32, jnp.bfloat16


def split3(value):
    high = value.astype(BF16).astype(F32)
    middle = (value - high).astype(BF16).astype(F32)
    low = (value - high - middle).astype(BF16).astype(F32)
    return high, middle, low


def cut_kernel(grad_hbm, feat_hbm, out_ref, grad_ref, feat_ref, sems):
    feat_copy = pltpu.make_async_copy(feat_hbm, feat_ref, sems.at[0])
    grad_copy = pltpu.make_async_copy(grad_hbm, grad_ref, sems.at[1])
    feat_copy.start()
    grad_copy.start()
    feat_copy.wait()
    values = feat_ref[...].astype(F32)
    mean = jnp.mean(values, axis=-1, keepdims=True)
    centered = values - mean
    inverse_std = lax.rsqrt(jnp.mean(centered * centered, axis=-1, keepdims=True) + EPSILON)
    marks = split3(mean) + split3(inverse_std)
    lane = lax.broadcasted_iota(jnp.int32, (PR, WIDE), 1)
    grad_copy.wait()
    for part in range(NMP):
        rest = [jnp.zeros((PR, 128), F32), jnp.zeros((PR, 128), F32)]
        live = lane < min(FEAT, VW - part * FEAT)
        for sub in range(SUB):
            low = sub * VW + part * FEAT
            start = low // 128 * 128
            width = min(640, PW - start)
            for which, ref in enumerate((grad_ref, feat_ref)):
                window = ref[:, start : start + width].astype(F32)
                if width < 640:
                    window = jnp.concatenate([window, jnp.zeros((PR, 640 - width), F32)], axis=1)
                if low > start:
                    window = pltpu.roll(window, 640 - (low - start), 1)
                chunk = jnp.where(live, window[:, :WIDE], 0.0)
                if which == 1 and sub == 0:
                    for at, mark in enumerate(marks):
                        chunk = jnp.where(lane == FEAT + at, mark, chunk)
                row = which * VT + sub * PR
                for tile in range(3):
                    at = tile * 2 * VT + row
                    out_ref[part, at : at + PR, :] = chunk[:, tile * 128 : tile * 128 + 128].astype(BF16)
                group = row // 32
                last = chunk[:, 384:512]
                rest[sub % 2] += pltpu.roll(last, 32 * group, 1) if group else last
        out_ref[part, REST : REST + PR, :] = rest[0].astype(BF16)
        out_ref[part, REST + PR : REST + 2 * PR, :] = rest[1].astype(BF16)


def unpack(ref, tile, which):
    at = [q * 2 * VT + which * VT for q in range(3)]
    pieces = [ref[tile, r : r + VT, :].astype(F32) for r in at]
    rest = ref[tile, REST : REST + 2 * PR, :].astype(F32)
    turn = (128 - 64 * which) % 128
    rest = jnp.concatenate(
        [pltpu.roll(rest, turn, 1) if turn else rest, pltpu.roll(rest, (turn + 96) % 128, 1)], axis=0
    )
    return pieces, rest


def slot_values(tile, source_ref, live_ref, recv_ref):
    pieces, rest = unpack(recv_ref, source_ref[tile], 0)
    rest = jnp.where(lax.broadcasted_iota(jnp.int32, (VT, 128), 1) < FEAT - 384, rest, 0.0)
    grads = jnp.concatenate(pieces + [rest], axis=1)
    grads = jnp.where(live_ref[tile] > 0, grads, 0.0)
    pieces, rest = unpack(recv_ref, tile, 1)
    feats = jnp.concatenate(pieces + [rest], axis=1)
    marks = rest[0:PR]
    lane = lax.broadcasted_iota(jnp.int32, (PR, 128), 1) + 384
    in_mean = (lane >= FEAT) & (lane < FEAT + 3)
    in_std = (lane >= FEAT + 3) & (lane < FEAT + 6)
    mean = jnp.sum(jnp.where(in_mean, marks, 0.0), axis=-1, keepdims=True)
    inverse_std = jnp.sum(jnp.where(in_std, marks, 0.0), axis=-1, keepdims=True)
    upstream = [grads[s * PR : (s + 1) * PR] for s in range(SUB)]
    normed = [(feats[s * PR : (s + 1) * PR] - mean) * inverse_std for s in range(SUB)]
    return upstream, normed, inverse_std


def sums_kernel(source_ref, live_ref, recv_ref, gain_ref, out_ref):
    lane = lax.broadcasted_iota(jnp.int32, (PR, 128), 1)
    rows = []
    for tile in range(TILES):
        upstream, normed, _ = slot_values(tile, source_ref, live_ref, recv_ref)
        first = jnp.zeros((PR, WIDE), F32)
        second = jnp.zeros((PR, WIDE), F32)
        for s in range(SUB):
            scaled = upstream[s] * gain_ref[s : s + 1, :]
            first = first + scaled
            second = second + scaled * normed[s]
        first = jnp.sum(first, axis=-1, keepdims=True)
        second = jnp.sum(second, axis=-1, keepdims=True)
        rows.append(jnp.where(lane == 0, first, jnp.where(lane == 1, second, 0.0)))
    turned = jnp.concatenate(rows, axis=0).T[0:8, :]
    for part in range(NMP):
        out_ref[part] = turned


COLS, GROUP, GAIN = 208, 48, 16
AT1, AT2, AT3 = COLS, 2 * COLS, 3 * COLS
AT4 = AT3 + GROUP
AT5 = AT4 + GAIN
MESSAGE = AT5 + GAIN


def branch_kernel(
    source_ref, live_ref, parts_ref, recv_ref, gain_ref, scale_ref, sums_ref,
    own_ref, before_ref, after_ref, far_ref, other_ref, turned_ref, terms_ref, branch_ref,
):
    total = sums_ref[0]
    for part in range(1, NMP):
        total = total + sums_ref[part]
    means = jnp.concatenate([total, jnp.zeros((120, 128), F32)], axis=0).T * (1.0 / PW)
    lane = lax.broadcasted_iota(jnp.int32, (PR, 128), 1)
    token = lax.broadcasted_iota(jnp.int32, (VT, VT), 0)
    place = lax.broadcasted_iota(jnp.int32, (VT, VT), 1)
    sub_of = ((token >> 3) & 1) * 2 + (token & 1)
    row_of = (token >> 4) * 4 + ((token >> 1) & 3)
    order = (place == sub_of * PR + row_of).astype(BF16)
    gains = [jnp.zeros((PR, WIDE), F32) for _ in range(SUB)]
    for tile in range(TILES):
        upstream, normed, inverse_std = slot_values(tile, source_ref, live_ref, recv_ref)
        own = means[tile * PR : (tile + 1) * PR]
        first = jnp.sum(jnp.where(lane == 0, own, 0.0), axis=-1, keepdims=True)
        second = jnp.sum(jnp.where(lane == 1, own, 0.0), axis=-1, keepdims=True)
        branch = []
        for s in range(SUB):
            scaled = upstream[s] * gain_ref[s : s + 1, :]
            grad = inverse_std * (scaled - first - normed[s] * second)
            branch.append((grad * scale_ref[...]).astype(BF16))
            gains[s] = gains[s] + upstream[s] * normed[s]
        branch = jnp.dot(order, jnp.concatenate(branch, axis=0), preferred_element_type=F32)
        branch_ref[tile * VT : (tile + 1) * VT, :] = branch.astype(BF16)
    gain = jnp.concatenate([jnp.sum(g, axis=0, keepdims=True) for g in gains], axis=0)
    gain = jnp.concatenate([gain[:, q * 128 : (q + 1) * 128] for q in range(4)], axis=0)
    gain_high = gain.astype(BF16)
    gain_low = (gain - gain_high.astype(F32)).astype(BF16)
    attns = [own_ref, before_ref, after_ref, far_ref] + [other_ref.at[p] for p in range(4)]
    for place, attn in enumerate(attns):
        part = parts_ref[place]
        term = jnp.dot(attn[...], branch_ref[...], preferred_element_type=F32)
        for q in range(3):
            terms_ref[part, q * COLS : (q + 1) * COLS, :] = term[:, q * 128 : q * 128 + 128].astype(BF16)
        last = term[:, 384:512]
        rest = last[0:GROUP]
        for g in range(1, 4):
            rest = rest + pltpu.roll(last[g * GROUP : (g + 1) * GROUP], 24 * g, 1)
        tail = pltpu.roll(last[4 * GROUP : COLS], 96, 1)
        rest = jnp.concatenate([rest[0:16] + tail, rest[16:]], axis=0)
        terms_ref[part, AT3:AT4, :] = rest.astype(BF16)
        terms_ref[part, AT4:AT5, :] = gain_high
        terms_ref[part, AT5:MESSAGE, :] = gain_low
    turned_ref[...] = branch_ref[...].T[:ROWS]


def fold_kernel(recv_ref, out_ref, wide_ref):
    total = recv_ref[0].astype(F32)
    for part in range(1, NY):
        total = total + recv_ref[part].astype(F32)
    rest = total[AT3:AT4]
    rest = [rest] + [pltpu.roll(rest, 128 - 24 * g, 1) for g in range(1, 5)]
    rest = jnp.concatenate(rest[:4] + [rest[4][0:16]], axis=0)
    wide = jnp.concatenate([total[0:AT1], total[AT1:AT2], total[AT2:AT3], rest], axis=1)
    wide = jnp.concatenate([wide, jnp.zeros((256 - COLS, WIDE), F32)], axis=0)
    wide_ref[...] = wide.T
    gain = total[AT4:AT5] + total[AT5:MESSAGE]
    gain = jnp.concatenate([gain[0:8], gain[8:16]], axis=1)
    for z in range(NZ):
        rows = wide_ref[z * BLOCK : z * BLOCK + 40, :]
        out_ref[z] = jnp.concatenate([rows, gain], axis=0).astype(BF16)


def settle_kernel(recv_ref, block_ref, gain_ref):
    total = recv_ref[0].astype(F32)
    for part in range(1, NZ):
        total = total + recv_ref[part].astype(F32)
    block_ref[...] = total[0:BLOCK, 0 : block_ref.shape[1]]
    gain = jnp.concatenate([total[40:48, 0:128], total[40:48, 128:256]], axis=0)
    for part in range(NMP):
        gain_ref[part] = gain


def spread_kernel(gain_ref, out_ref, wide_ref):
    wide_ref[...] = jnp.zeros_like(wide_ref)
    for part in range(NMP):
        gain = gain_ref[part]
        pieces = [gain[q * SUB : (q + 1) * SUB] for q in range(4)] + [jnp.zeros((SUB, 128), F32)]
        low = part * FEAT
        start = low // 128 * 128
        pieces = jnp.concatenate(pieces, axis=1)
        if low > start:
            pieces = pltpu.roll(pieces, low - start, 1)
        wide_ref[:, start : start + 640] += pieces
    out_ref[...] = wide_ref[:, 0:VW]


def gathered_kernel(
    tile_ref, parts_ref, weight_ref, scale_ref, own_ref, before_ref, after_ref, far_ref, other_ref,
    attn_ref, residual_ref, all_ref,
):
    pieces = [own_ref, before_ref, after_ref, far_ref] + [other_ref.at[p] for p in range(4)]
    for place, piece in enumerate(pieces):
        all_ref[parts_ref[place]] = piece[...]
    tile = tile_ref[0]
    at = pl.multiple_of((tile >> 1) * 128, 128)
    lane = lax.broadcasted_iota(jnp.int32, (COLS, WIDE), 1)
    total = jnp.zeros((COLS, TILES * VT), F32)
    tokens = []
    for part in range(NMP):
        low = part * FEAT
        start = low // 128 * 128
        width = min(640, VW - start)
        weight = weight_ref[:, start : start + width].astype(F32)
        if width < 640:
            weight = jnp.concatenate([weight, jnp.zeros((COLS, 640 - width), F32)], axis=1)
        if low > start:
            weight = pltpu.roll(weight, 640 - (low - start), 1)
        weight = jnp.where(lane < min(FEAT, VW - low), weight[:, :WIDE], 0.0).astype(BF16)
        total += jnp.dot(weight[:, :ROWS], all_ref[part], preferred_element_type=F32)
        tokens.append(all_ref[part, :, pl.ds(at, 128)].astype(F32)[:FEAT])
    attn_ref[...] = total.astype(BF16)
    tokens = jnp.concatenate(tokens, axis=0)[:VW].T
    tokens = jnp.where((tile & 1) == 0, tokens[0:VT], tokens[VT : 2 * VT])
    residual_ref[...] = (tokens / scale_ref[...]).astype(BF16)


def whole(count):
    return [pl.BlockSpec(memory_space=pltpu.VMEM)] * count


def scalars(count):
    return [pl.BlockSpec(memory_space=pltpu.SMEM)] * count


def gather(own):
    before, after, far = (
        lax.ppermute(own, "x", [(x, (x + step) % 4) for x in range(4)]) for step in (1, 3, 2)
    )
    other = lax.ppermute(jnp.stack([own, before, after, far]), "c", [(0, 1), (1, 0)])
    return own, before, after, far, other


def last_places():
    pairs = []
    for z in range(NZ):
        for y in range(NY):
            for part in range(NMP):
                pairs.append(((z * NY + y) * NMP + part, (NZ * part + z) * NMP + y))
    return pairs


def in_hbm(count):
    return [pl.BlockSpec(memory_space=pltpu.HBM)] * count


def body(
    grad_proj, tile_counts, tile_home, saved_feat, ln_gain, layer_scale, attn_saved, proj_weight
):
    mp_index = lax.axis_index(MP)
    cols = attn_saved.shape[1]
    send = pl.pallas_call(
        cut_kernel,
        out_shape=jax.ShapeDtypeStruct((NMP, REST + 2 * PR, 128), BF16),
        in_specs=in_hbm(2),
        out_specs=whole(1)[0],
        scratch_shapes=[
            pltpu.VMEM((PR, PW), BF16),
            pltpu.VMEM((PR, PW), BF16),
            pltpu.SemaphoreType.DMA((2,)),
        ],
        compiler_params=pltpu.CompilerParams(vmem_limit_bytes=60 * 1024 * 1024),
        name="cut",
    )(grad_proj, saved_feat)
    attn_own, send = lax.optimization_barrier((attn_saved.T, send))
    recv = lax.all_to_all(send, MP, 0, 0)
    attns = gather(attn_own)
    x_index, c_index = lax.axis_index("x"), lax.axis_index("c")
    near = jnp.stack([x_index, (x_index + 3) % 4, (x_index + 1) % 4, (x_index + 2) % 4]) * 2
    parts = jnp.concatenate([near + c_index, near + 1 - c_index]).astype(jnp.int32)

    slot_ids = jnp.arange(TILES, dtype=jnp.int32)
    matches = tile_home[0][None, :] == slot_ids[:, None]
    source = jnp.sum(jnp.where(matches, slot_ids[None, :], 0), axis=1).astype(jnp.int32)
    live = (source < jnp.sum(tile_counts)).astype(jnp.int32)
    pad = NMP * FEAT - VW
    gain = jnp.pad(ln_gain.reshape(SUB, VW), ((0, 0), (0, pad + WIDE - FEAT)))
    gain = lax.dynamic_slice_in_dim(gain, mp_index * FEAT, WIDE, axis=1)
    scale = jnp.pad(layer_scale, (0, pad + WIDE - FEAT))
    scale = lax.dynamic_slice_in_dim(scale, mp_index * FEAT, WIDE, axis=0)[None]
    inside = (jnp.arange(WIDE) < FEAT)[None]
    gain = jnp.where(inside, gain, 0.0)
    scale = jnp.where(inside, scale, 0.0)

    sums = pl.pallas_call(
        sums_kernel,
        out_shape=jax.ShapeDtypeStruct((NMP, 8, 128), F32),
        in_specs=scalars(2) + whole(2),
        out_specs=whole(1)[0],
        compiler_params=VMEM,
        name="sums",
    )(source, live, recv, gain)
    sums = lax.all_to_all(sums, MP, 0, 0)

    turned, terms = pl.pallas_call(
        branch_kernel,
        out_shape=(
            jax.ShapeDtypeStruct((ROWS, TILES * VT), BF16),
            jax.ShapeDtypeStruct((NMP, MESSAGE, 128), BF16),
        ),
        in_specs=scalars(3) + whole(9),
        out_specs=tuple(whole(2)),
        scratch_shapes=[pltpu.VMEM((TILES * VT, WIDE), BF16)],
        compiler_params=VMEM,
        name="branch",
    )(source, live, parts, recv, gain, scale, sums, *attns)

    terms = lax.all_to_all(terms, "y", 0, 0)
    terms = pl.pallas_call(
        fold_kernel,
        out_shape=jax.ShapeDtypeStruct((NZ, 48, 256), BF16),
        in_specs=whole(1),
        out_specs=whole(1)[0],
        scratch_shapes=[pltpu.VMEM((WIDE, 256), F32)],
        compiler_params=VMEM,
        name="fold",
    )(terms)
    terms = lax.all_to_all(terms, "z", 0, 0)

    turned = gather(turned)
    attn_grad, residual_grad = pl.pallas_call(
        gathered_kernel,
        out_shape=(
            jax.ShapeDtypeStruct((cols, TILES * VT), BF16),
            jax.ShapeDtypeStruct((VT, VW), BF16),
        ),
        in_specs=scalars(2) + whole(7),
        out_specs=tuple(whole(2)),
        scratch_shapes=[pltpu.VMEM((NMP, ROWS, TILES * VT), BF16)],
        compiler_params=VMEM,
        name="gathered",
    )(mp_index.astype(jnp.int32)[None], parts, proj_weight.T, layer_scale[None], *turned)

    terms, attn_grad, residual_grad = lax.optimization_barrier((terms, attn_grad, residual_grad))
    part, gains = pl.pallas_call(
        settle_kernel,
        out_shape=(
            jax.ShapeDtypeStruct((BLOCK, cols), F32),
            jax.ShapeDtypeStruct((NMP, GAIN, 128), F32),
        ),
        in_specs=whole(1),
        out_specs=tuple(whole(2)),
        compiler_params=VMEM,
        name="settle",
    )(terms)

    proj_grad = lax.ppermute(part, DP + MP, last_places())
    gains = lax.all_to_all(gains, MP, 0, 0)
    gain_grad = pl.pallas_call(
        spread_kernel,
        out_shape=jax.ShapeDtypeStruct((SUB, VW), F32),
        in_specs=whole(1),
        out_specs=whole(1)[0],
        scratch_shapes=[pltpu.VMEM((SUB, 3456), F32)],
        compiler_params=VMEM,
        name="spread",
    )(gains)
    return (residual_grad, attn_grad.T, proj_grad, gain_grad.reshape(-1))


def solution(mesh):
    fine = Mesh(mesh.devices.reshape(NZ, NY, 4, 2), DP + MP)
    in_specs = (
        P(DP + MP, None),
        P(DP, None),
        P(DP, None),
        P(DP + MP, None),
        P(),
        P(),
        P(DP, MP),
        P(None, MP),
    )
    out_specs = (P(DP + MP, None), P(DP, MP), P(DP, MP), P())
    return jax.shard_map(body, mesh=fine, in_specs=in_specs, out_specs=out_specs, check_vma=False)
```

```python
import jax
import jax.numpy as jnp
from jax import lax
from jax.experimental import pallas as pl
from jax.experimental.pallas import tpu as pltpu
from jax.sharding import Mesh
from jax.sharding import PartitionSpec as P

VW = 3200
PW = 12800
EPSILON = 1e-05
DP = ("z", "y")
MP = ("x", "c")
NZ, NY, NMP = 12, 8, 8
BLOCK = 34
FEAT = NZ * BLOCK
WIDE = 512
ROWS = 416
REST = 384
TILES, PR, SUB, VT = 8, 16, 4, 64
VMEM = pltpu.CompilerParams(vmem_limit_bytes=48 * 1024 * 1024)
F32, BF16 = jnp.float32, jnp.bfloat16


def split3(value):
    high = value.astype(BF16).astype(F32)
    middle = (value - high).astype(BF16).astype(F32)
    low = (value - high - middle).astype(BF16).astype(F32)
    return high, middle, low


def cut_kernel(grad_hbm, feat_hbm, out_ref, grad_ref, feat_ref, last_ref, sems):
    feat_copy = pltpu.make_async_copy(feat_hbm, feat_ref, sems.at[0])
    grad_copy = pltpu.make_async_copy(grad_hbm, grad_ref, sems.at[1])
    feat_copy.start()
    grad_copy.start()
    feat_copy.wait()
    values = feat_ref[...].astype(F32)
    mean = jnp.mean(values, axis=-1, keepdims=True)
    centered = values - mean
    inverse_std = lax.rsqrt(jnp.mean(centered * centered, axis=-1, keepdims=True) + EPSILON)
    marks = split3(mean) + split3(inverse_std)
    lane = lax.broadcasted_iota(jnp.int32, (PR, WIDE), 1)
    grad_copy.wait()
    for part in range(NMP):
        live = lane < min(FEAT, VW - part * FEAT)
        for sub in range(SUB):
            low = sub * VW + part * FEAT
            start = low // 128 * 128
            width = min(640, PW - start)
            for which, ref in enumerate((grad_ref, feat_ref)):
                window = ref[:, start : start + width].astype(F32)
                if width < 640:
                    window = jnp.concatenate([window, jnp.zeros((PR, 640 - width), F32)], axis=1)
                if low > start:
                    window = pltpu.roll(window, 640 - (low - start), 1)
                chunk = jnp.where(live, window[:, :WIDE], 0.0)
                if which == 1 and sub == 0:
                    for at, mark in enumerate(marks):
                        chunk = jnp.where(lane == FEAT + at, mark, chunk)
                row = which * VT + sub * PR
                for tile in range(3):
                    at = tile * 2 * VT + row
                    out_ref[part, at : at + PR, :] = chunk[:, tile * 128 : tile * 128 + 128].astype(BF16)
                last_ref[part, row : row + PR, :] = chunk[:, 384:512]
    for part in range(NMP):
        rest = last_ref[part, 0:32, :]
        for group in range(1, 4):
            rest = rest + pltpu.roll(last_ref[part, 32 * group : 32 * group + 32, :], 32 * group, 1)
        out_ref[part, REST : REST + 2 * PR, :] = rest.astype(BF16)


def unpack(ref, tile, which):
    at = [q * 2 * VT + which * VT for q in range(3)]
    pieces = [ref[tile, r : r + VT, :].astype(F32) for r in at]
    rest = ref[tile, REST : REST + 2 * PR, :].astype(F32)
    turn = (128 - 64 * which) % 128
    rest = jnp.concatenate(
        [pltpu.roll(rest, turn, 1) if turn else rest, pltpu.roll(rest, (turn + 96) % 128, 1)], axis=0
    )
    return pieces, rest


def slot_values(tile, source_ref, live_ref, recv_ref):
    pieces, rest = unpack(recv_ref, source_ref[tile], 0)
    rest = jnp.where(lax.broadcasted_iota(jnp.int32, (VT, 128), 1) < FEAT - 384, rest, 0.0)
    grads = jnp.concatenate(pieces + [rest], axis=1)
    grads = jnp.where(live_ref[tile] > 0, grads, 0.0)
    pieces, rest = unpack(recv_ref, tile, 1)
    feats = jnp.concatenate(pieces + [rest], axis=1)
    marks = rest[0:PR]
    lane = lax.broadcasted_iota(jnp.int32, (PR, 128), 1) + 384
    in_mean = (lane >= FEAT) & (lane < FEAT + 3)
    in_std = (lane >= FEAT + 3) & (lane < FEAT + 6)
    mean = jnp.sum(jnp.where(in_mean, marks, 0.0), axis=-1, keepdims=True)
    inverse_std = jnp.sum(jnp.where(in_std, marks, 0.0), axis=-1, keepdims=True)
    upstream = [grads[s * PR : (s + 1) * PR] for s in range(SUB)]
    normed = [(feats[s * PR : (s + 1) * PR] - mean) * inverse_std for s in range(SUB)]
    return upstream, normed, inverse_std


def sums_kernel(source_ref, live_ref, recv_ref, gain_ref, out_ref):
    lane = lax.broadcasted_iota(jnp.int32, (PR, 128), 1)
    rows = []
    for tile in range(TILES):
        upstream, normed, _ = slot_values(tile, source_ref, live_ref, recv_ref)
        first = jnp.zeros((PR, WIDE), F32)
        second = jnp.zeros((PR, WIDE), F32)
        for s in range(SUB):
            scaled = upstream[s] * gain_ref[s : s + 1, :]
            first = first + scaled
            second = second + scaled * normed[s]
        first = jnp.sum(first, axis=-1, keepdims=True)
        second = jnp.sum(second, axis=-1, keepdims=True)
        rows.append(jnp.where(lane == 0, first, jnp.where(lane == 1, second, 0.0)))
    turned = jnp.concatenate(rows, axis=0).T[0:8, :]
    for part in range(NMP):
        out_ref[part] = turned


COLS, GROUP, GAIN = 208, 48, 16
AT1, AT2, AT3 = COLS, 2 * COLS, 3 * COLS
AT4 = AT3 + GROUP
AT5 = AT4 + GAIN
MESSAGE = AT5 + GAIN


def branch_kernel(
    source_ref, live_ref, parts_ref, recv_ref, gain_ref, scale_ref, sums_ref,
    own_ref, before_ref, after_ref, far_ref, other_ref, turned_ref, terms_ref, branch_ref,
):
    total = sums_ref[0]
    for part in range(1, NMP):
        total = total + sums_ref[part]
    means = jnp.concatenate([total, jnp.zeros((120, 128), F32)], axis=0).T * (1.0 / PW)
    lane = lax.broadcasted_iota(jnp.int32, (PR, 128), 1)
    token = lax.broadcasted_iota(jnp.int32, (VT, VT), 0)
    place = lax.broadcasted_iota(jnp.int32, (VT, VT), 1)
    sub_of = ((token >> 3) & 1) * 2 + (token & 1)
    row_of = (token >> 4) * 4 + ((token >> 1) & 3)
    order = (place == sub_of * PR + row_of).astype(BF16)
    gains = [jnp.zeros((PR, WIDE), F32) for _ in range(SUB)]
    for tile in range(TILES):
        upstream, normed, inverse_std = slot_values(tile, source_ref, live_ref, recv_ref)
        own = means[tile * PR : (tile + 1) * PR]
        first = jnp.sum(jnp.where(lane == 0, own, 0.0), axis=-1, keepdims=True)
        second = jnp.sum(jnp.where(lane == 1, own, 0.0), axis=-1, keepdims=True)
        branch = []
        for s in range(SUB):
            scaled = upstream[s] * gain_ref[s : s + 1, :]
            grad = inverse_std * (scaled - first - normed[s] * second)
            branch.append((grad * scale_ref[...]).astype(BF16))
            gains[s] = gains[s] + upstream[s] * normed[s]
        branch = jnp.dot(order, jnp.concatenate(branch, axis=0), preferred_element_type=F32)
        branch_ref[tile * VT : (tile + 1) * VT, :] = branch.astype(BF16)
    gain = jnp.concatenate([jnp.sum(g, axis=0, keepdims=True) for g in gains], axis=0)
    gain = jnp.concatenate([gain[:, q * 128 : (q + 1) * 128] for q in range(4)], axis=0)
    gain_high = gain.astype(BF16)
    gain_low = (gain - gain_high.astype(F32)).astype(BF16)
    attns = [own_ref, before_ref, after_ref, far_ref] + [other_ref.at[p] for p in range(4)]
    for place, attn in enumerate(attns):
        part = parts_ref[place]
        term = jnp.dot(attn[...], branch_ref[...], preferred_element_type=F32)
        for q in range(3):
            terms_ref[part, q * COLS : (q + 1) * COLS, :] = term[:, q * 128 : q * 128 + 128].astype(BF16)
        last = term[:, 384:512]
        rest = last[0:GROUP]
        for g in range(1, 4):
            rest = rest + pltpu.roll(last[g * GROUP : (g + 1) * GROUP], 24 * g, 1)
        tail = pltpu.roll(last[4 * GROUP : COLS], 96, 1)
        rest = jnp.concatenate([rest[0:16] + tail, rest[16:]], axis=0)
        terms_ref[part, AT3:AT4, :] = rest.astype(BF16)
        terms_ref[part, AT4:AT5, :] = gain_high
        terms_ref[part, AT5:MESSAGE, :] = gain_low
    turned_ref[...] = branch_ref[...].T[:ROWS]


def fold_kernel(recv_ref, out_ref, wide_ref):
    total = recv_ref[0].astype(F32)
    for part in range(1, NY):
        total = total + recv_ref[part].astype(F32)
    rest = total[AT3:AT4]
    rest = [rest] + [pltpu.roll(rest, 128 - 24 * g, 1) for g in range(1, 5)]
    rest = jnp.concatenate(rest[:4] + [rest[4][0:16]], axis=0)
    wide = jnp.concatenate([total[0:AT1], total[AT1:AT2], total[AT2:AT3], rest], axis=1)
    wide = jnp.concatenate([wide, jnp.zeros((256 - COLS, WIDE), F32)], axis=0)
    wide_ref[...] = wide.T
    gain = total[AT4:AT5] + total[AT5:MESSAGE]
    gain = jnp.concatenate([gain[0:8], gain[8:16]], axis=1)
    for z in range(NZ):
        rows = wide_ref[z * BLOCK : z * BLOCK + 40, :]
        out_ref[z] = jnp.concatenate([rows, gain], axis=0).astype(BF16)


def settle_kernel(recv_ref, block_ref, gain_ref):
    total = recv_ref[0].astype(F32)
    for part in range(1, NZ):
        total = total + recv_ref[part].astype(F32)
    block_ref[...] = total[0:BLOCK, 0 : block_ref.shape[1]]
    gain = jnp.concatenate([total[40:48, 0:128], total[40:48, 128:256]], axis=0)
    for part in range(NMP):
        gain_ref[part] = gain


def spread_kernel(gain_ref, out_ref, wide_ref):
    wide_ref[...] = jnp.zeros_like(wide_ref)
    for part in range(NMP):
        gain = gain_ref[part]
        pieces = [gain[q * SUB : (q + 1) * SUB] for q in range(4)] + [jnp.zeros((SUB, 128), F32)]
        low = part * FEAT
        start = low // 128 * 128
        pieces = jnp.concatenate(pieces, axis=1)
        if low > start:
            pieces = pltpu.roll(pieces, low - start, 1)
        wide_ref[:, start : start + 640] += pieces
    out_ref[...] = wide_ref[:, 0:VW]


def gathered_kernel(
    tile_ref, parts_ref, weight_ref, scale_ref, own_ref, before_ref, after_ref, far_ref, other_ref,
    attn_ref, residual_ref, all_ref,
):
    pieces = [own_ref, before_ref, after_ref, far_ref] + [other_ref.at[p] for p in range(4)]
    for place, piece in enumerate(pieces):
        all_ref[parts_ref[place]] = piece[...]
    tile = tile_ref[0]
    at = pl.multiple_of((tile >> 1) * 128, 128)
    lane = lax.broadcasted_iota(jnp.int32, (COLS, WIDE), 1)
    total = jnp.zeros((COLS, TILES * VT), F32)
    tokens = []
    for part in range(NMP):
        low = part * FEAT
        start = low // 128 * 128
        width = min(640, VW - start)
        weight = weight_ref[:, start : start + width].astype(F32)
        if width < 640:
            weight = jnp.concatenate([weight, jnp.zeros((COLS, 640 - width), F32)], axis=1)
        if low > start:
            weight = pltpu.roll(weight, 640 - (low - start), 1)
        weight = jnp.where(lane < min(FEAT, VW - low), weight[:, :WIDE], 0.0).astype(BF16)
        total += jnp.dot(weight[:, :ROWS], all_ref[part], preferred_element_type=F32)
        tokens.append(all_ref[part, :, pl.ds(at, 128)].astype(F32)[:FEAT])
    attn_ref[...] = total.astype(BF16)
    tokens = jnp.concatenate(tokens, axis=0)[:VW].T
    tokens = jnp.where((tile & 1) == 0, tokens[0:VT], tokens[VT : 2 * VT])
    residual_ref[...] = (tokens / scale_ref[...]).astype(BF16)


def whole(count):
    return [pl.BlockSpec(memory_space=pltpu.VMEM)] * count


def scalars(count):
    return [pl.BlockSpec(memory_space=pltpu.SMEM)] * count


def gather_x(own):
    return tuple(
        lax.ppermute(own, "x", [(x, (x + step) % 4) for x in range(4)]) for step in (1, 3, 2)
    )


def gather_core(own, before, after, far):
    return lax.ppermute(jnp.stack([own, before, after, far]), "c", [(0, 1), (1, 0)])


def last_places():
    pairs = []
    for z in range(NZ):
        for y in range(NY):
            for part in range(NMP):
                pairs.append(((z * NY + y) * NMP + part, (NZ * part + z) * NMP + y))
    return pairs


def in_hbm(count):
    return [pl.BlockSpec(memory_space=pltpu.HBM)] * count


def body(
    grad_proj, tile_counts, tile_home, saved_feat, ln_gain, layer_scale, attn_saved, proj_weight
):
    mp_index = lax.axis_index(MP)
    cols = attn_saved.shape[1]
    send = pl.pallas_call(
        cut_kernel,
        out_shape=jax.ShapeDtypeStruct((NMP, REST + 2 * PR, 128), BF16),
        in_specs=in_hbm(2),
        out_specs=whole(1)[0],
        scratch_shapes=[
            pltpu.VMEM((PR, PW), BF16),
            pltpu.VMEM((PR, PW), BF16),
            pltpu.VMEM((NMP, 2 * VT, 128), F32),
            pltpu.SemaphoreType.DMA((2,)),
        ],
        compiler_params=pltpu.CompilerParams(vmem_limit_bytes=60 * 1024 * 1024),
        name="cut",
    )(grad_proj, saved_feat)
    attn_own, send = lax.optimization_barrier((attn_saved.T, send))
    recv = lax.all_to_all(send, MP, 0, 0)
    attns = (attn_own,) + gather_x(attn_own)
    x_index, c_index = lax.axis_index("x"), lax.axis_index("c")
    near = jnp.stack([x_index, (x_index + 3) % 4, (x_index + 1) % 4, (x_index + 2) % 4]) * 2
    parts = jnp.concatenate([near + c_index, near + 1 - c_index]).astype(jnp.int32)

    slot_ids = jnp.arange(TILES, dtype=jnp.int32)
    matches = tile_home[0][None, :] == slot_ids[:, None]
    source = jnp.sum(jnp.where(matches, slot_ids[None, :], 0), axis=1).astype(jnp.int32)
    live = (source < jnp.sum(tile_counts)).astype(jnp.int32)
    pad = NMP * FEAT - VW
    gain = jnp.pad(ln_gain.reshape(SUB, VW), ((0, 0), (0, pad + WIDE - FEAT)))
    gain = lax.dynamic_slice_in_dim(gain, mp_index * FEAT, WIDE, axis=1)
    scale = jnp.pad(layer_scale, (0, pad + WIDE - FEAT))
    scale = lax.dynamic_slice_in_dim(scale, mp_index * FEAT, WIDE, axis=0)[None]
    inside = (jnp.arange(WIDE) < FEAT)[None]
    gain = jnp.where(inside, gain, 0.0)
    scale = jnp.where(inside, scale, 0.0)

    sums = pl.pallas_call(
        sums_kernel,
        out_shape=jax.ShapeDtypeStruct((NMP, 8, 128), F32),
        in_specs=scalars(2) + whole(2),
        out_specs=whole(1)[0],
        compiler_params=VMEM,
        name="sums",
    )(source, live, recv, gain)
    attns = lax.optimization_barrier(attns + (sums,))[:4]
    attns = attns + (gather_core(*attns),)
    sums = lax.all_to_all(sums, MP, 0, 0)

    turned, terms = pl.pallas_call(
        branch_kernel,
        out_shape=(
            jax.ShapeDtypeStruct((ROWS, TILES * VT), BF16),
            jax.ShapeDtypeStruct((NMP, MESSAGE, 128), BF16),
        ),
        in_specs=scalars(3) + whole(9),
        out_specs=tuple(whole(2)),
        scratch_shapes=[pltpu.VMEM((TILES * VT, WIDE), BF16)],
        compiler_params=VMEM,
        name="branch",
    )(source, live, parts, recv, gain, scale, sums, *attns)

    terms = lax.all_to_all(terms, "y", 0, 0)
    terms = pl.pallas_call(
        fold_kernel,
        out_shape=jax.ShapeDtypeStruct((NZ, 48, 256), BF16),
        in_specs=whole(1),
        out_specs=whole(1)[0],
        scratch_shapes=[pltpu.VMEM((WIDE, 256), F32)],
        compiler_params=VMEM,
        name="fold",
    )(terms)
    terms = lax.all_to_all(terms, "z", 0, 0)

    turned = (turned,) + gather_x(turned)
    turned = turned + (gather_core(*turned),)
    attn_grad, residual_grad = pl.pallas_call(
        gathered_kernel,
        out_shape=(
            jax.ShapeDtypeStruct((cols, TILES * VT), BF16),
            jax.ShapeDtypeStruct((VT, VW), BF16),
        ),
        in_specs=scalars(2) + whole(7),
        out_specs=tuple(whole(2)),
        scratch_shapes=[pltpu.VMEM((NMP, ROWS, TILES * VT), BF16)],
        compiler_params=VMEM,
        name="gathered",
    )(mp_index.astype(jnp.int32)[None], parts, proj_weight.T, layer_scale[None], *turned)

    terms, attn_grad, residual_grad = lax.optimization_barrier((terms, attn_grad, residual_grad))
    part, gains = pl.pallas_call(
        settle_kernel,
        out_shape=(
            jax.ShapeDtypeStruct((BLOCK, cols), F32),
            jax.ShapeDtypeStruct((NMP, GAIN, 128), F32),
        ),
        in_specs=whole(1),
        out_specs=tuple(whole(2)),
        compiler_params=VMEM,
        name="settle",
    )(terms)

    proj_grad = lax.ppermute(part, DP + MP, last_places())
    gains = lax.all_to_all(gains, MP, 0, 0)
    gain_grad = pl.pallas_call(
        spread_kernel,
        out_shape=jax.ShapeDtypeStruct((SUB, VW), F32),
        in_specs=whole(1),
        out_specs=whole(1)[0],
        scratch_shapes=[pltpu.VMEM((SUB, 3456), F32)],
        compiler_params=VMEM,
        name="spread",
    )(gains)
    return (residual_grad, attn_grad.T, proj_grad, gain_grad.reshape(-1))


def solution(mesh):
    fine = Mesh(mesh.devices.reshape(NZ, NY, 4, 2), DP + MP)
    in_specs = (
        P(DP + MP, None),
        P(DP, None),
        P(DP, None),
        P(DP + MP, None),
        P(),
        P(),
        P(DP, MP),
        P(None, MP),
    )
    out_specs = (P(DP + MP, None), P(DP, MP), P(DP, MP), P())
    return jax.shard_map(body, mesh=fine, in_specs=in_specs, out_specs=out_specs, check_vma=False)
```

```python
import jax
import jax.numpy as jnp
from jax import lax
from jax.experimental import pallas as pl
from jax.experimental.pallas import tpu as pltpu
from jax.sharding import Mesh
from jax.sharding import PartitionSpec as P

VW = 3200
PW = 12800
EPSILON = 1e-05
DP = ("z", "y")
MP = ("x", "c")
NZ, NY, NMP = 12, 8, 8
BLOCK = 34
FEAT = NZ * BLOCK
WIDE = 512
ROWS = 416
REST = 384
TILES, PR, SUB, VT = 8, 16, 4, 64
VMEM = pltpu.CompilerParams(vmem_limit_bytes=48 * 1024 * 1024)
F32, BF16 = jnp.float32, jnp.bfloat16


def split3(value):
    high = value.astype(BF16).astype(F32)
    middle = (value - high).astype(BF16).astype(F32)
    low = (value - high - middle).astype(BF16).astype(F32)
    return high, middle, low


def cut_kernel(grad_hbm, feat_hbm, out_ref, grad_ref, feat_ref, last_ref, sems):
    feat_copy = pltpu.make_async_copy(feat_hbm, feat_ref, sems.at[0])
    grad_copy = pltpu.make_async_copy(grad_hbm, grad_ref, sems.at[1])
    feat_copy.start()
    grad_copy.start()
    feat_copy.wait()
    values = feat_ref[...].astype(F32)
    mean = jnp.mean(values, axis=-1, keepdims=True)
    centered = values - mean
    inverse_std = lax.rsqrt(jnp.mean(centered * centered, axis=-1, keepdims=True) + EPSILON)
    marks = split3(mean) + split3(inverse_std)
    lane = lax.broadcasted_iota(jnp.int32, (PR, WIDE), 1)
    grad_copy.wait()
    for part in range(NMP):
        live = lane < min(FEAT, VW - part * FEAT)
        for sub in range(SUB):
            low = sub * VW + part * FEAT
            start = low // 128 * 128
            width = min(640, PW - start)
            for which, ref in enumerate((grad_ref, feat_ref)):
                window = ref[:, start : start + width].astype(F32)
                if width < 640:
                    window = jnp.concatenate([window, jnp.zeros((PR, 640 - width), F32)], axis=1)
                if low > start:
                    window = pltpu.roll(window, 640 - (low - start), 1)
                chunk = jnp.where(live, window[:, :WIDE], 0.0)
                if which == 1 and sub == 0:
                    for at, mark in enumerate(marks):
                        chunk = jnp.where(lane == FEAT + at, mark, chunk)
                row = which * VT + sub * PR
                for tile in range(3):
                    at = tile * 2 * VT + row
                    out_ref[part, at : at + PR, :] = chunk[:, tile * 128 : tile * 128 + 128].astype(BF16)
                last_ref[part, row : row + PR, :] = chunk[:, 384:512]
    for part in range(NMP):
        rest = last_ref[part, 0:32, :]
        for group in range(1, 4):
            rest = rest + pltpu.roll(last_ref[part, 32 * group : 32 * group + 32, :], 32 * group, 1)
        out_ref[part, REST : REST + 2 * PR, :] = rest.astype(BF16)


def unpack(ref, tile, which):
    at = [q * 2 * VT + which * VT for q in range(3)]
    pieces = [ref[tile, r : r + VT, :].astype(F32) for r in at]
    rest = ref[tile, REST : REST + 2 * PR, :].astype(F32)
    turn = (128 - 64 * which) % 128
    rest = jnp.concatenate(
        [pltpu.roll(rest, turn, 1) if turn else rest, pltpu.roll(rest, (turn + 96) % 128, 1)], axis=0
    )
    return pieces, rest


def slot_values(tile, source_ref, live_ref, recv_ref):
    pieces, rest = unpack(recv_ref, source_ref[tile], 0)
    rest = jnp.where(lax.broadcasted_iota(jnp.int32, (VT, 128), 1) < FEAT - 384, rest, 0.0)
    grads = jnp.concatenate(pieces + [rest], axis=1)
    grads = jnp.where(live_ref[tile] > 0, grads, 0.0)
    pieces, rest = unpack(recv_ref, tile, 1)
    feats = jnp.concatenate(pieces + [rest], axis=1)
    marks = rest[0:PR]
    lane = lax.broadcasted_iota(jnp.int32, (PR, 128), 1) + 384
    in_mean = (lane >= FEAT) & (lane < FEAT + 3)
    in_std = (lane >= FEAT + 3) & (lane < FEAT + 6)
    mean = jnp.sum(jnp.where(in_mean, marks, 0.0), axis=-1, keepdims=True)
    inverse_std = jnp.sum(jnp.where(in_std, marks, 0.0), axis=-1, keepdims=True)
    upstream = [grads[s * PR : (s + 1) * PR] for s in range(SUB)]
    normed = [(feats[s * PR : (s + 1) * PR] - mean) * inverse_std for s in range(SUB)]
    return upstream, normed, inverse_std


def sums_kernel(source_ref, live_ref, recv_ref, gain_ref, out_ref):
    lane = lax.broadcasted_iota(jnp.int32, (PR, 128), 1)
    rows = []
    for tile in range(TILES):
        upstream, normed, _ = slot_values(tile, source_ref, live_ref, recv_ref)
        first = jnp.zeros((PR, WIDE), F32)
        second = jnp.zeros((PR, WIDE), F32)
        for s in range(SUB):
            scaled = upstream[s] * gain_ref[s : s + 1, :]
            first = first + scaled
            second = second + scaled * normed[s]
        first = jnp.sum(first, axis=-1, keepdims=True)
        second = jnp.sum(second, axis=-1, keepdims=True)
        rows.append(jnp.where(lane == 0, first, jnp.where(lane == 1, second, 0.0)))
    turned = jnp.concatenate(rows, axis=0).T[0:8, :]
    for part in range(NMP):
        out_ref[part] = turned


COLS, GROUP, GAIN = 208, 48, 16
AT1, AT2, AT3 = COLS, 2 * COLS, 3 * COLS
AT4 = AT3 + GROUP
AT5 = AT4 + GAIN
MESSAGE = AT5 + GAIN


def branch_kernel(
    source_ref, live_ref, recv_ref, gain_ref, scale_ref, sums_ref, branch_ref, gain_out_ref
):
    total = sums_ref[0]
    for part in range(1, NMP):
        total = total + sums_ref[part]
    means = jnp.concatenate([total, jnp.zeros((120, 128), F32)], axis=0).T * (1.0 / PW)
    lane = lax.broadcasted_iota(jnp.int32, (PR, 128), 1)
    token = lax.broadcasted_iota(jnp.int32, (VT, VT), 0)
    place = lax.broadcasted_iota(jnp.int32, (VT, VT), 1)
    sub_of = ((token >> 3) & 1) * 2 + (token & 1)
    row_of = (token >> 4) * 4 + ((token >> 1) & 3)
    order = (place == sub_of * PR + row_of).astype(BF16)
    gains = [jnp.zeros((PR, WIDE), F32) for _ in range(SUB)]
    for tile in range(TILES):
        upstream, normed, inverse_std = slot_values(tile, source_ref, live_ref, recv_ref)
        own = means[tile * PR : (tile + 1) * PR]
        first = jnp.sum(jnp.where(lane == 0, own, 0.0), axis=-1, keepdims=True)
        second = jnp.sum(jnp.where(lane == 1, own, 0.0), axis=-1, keepdims=True)
        branch = []
        for s in range(SUB):
            scaled = upstream[s] * gain_ref[s : s + 1, :]
            grad = inverse_std * (scaled - first - normed[s] * second)
            branch.append((grad * scale_ref[...]).astype(BF16))
            gains[s] = gains[s] + upstream[s] * normed[s]
        branch = jnp.dot(order, jnp.concatenate(branch, axis=0), preferred_element_type=F32)
        branch_ref[tile * VT : (tile + 1) * VT, :] = branch.astype(BF16)
    gain = jnp.concatenate([jnp.sum(g, axis=0, keepdims=True) for g in gains], axis=0)
    gain = jnp.concatenate([gain[:, q * 128 : (q + 1) * 128] for q in range(4)], axis=0)
    gain_high = gain.astype(BF16)
    gain_out_ref[0:GAIN, :] = gain_high
    gain_out_ref[GAIN : 2 * GAIN, :] = (gain - gain_high.astype(F32)).astype(BF16)


def terms_kernel(
    parts_ref, branch_ref, gain_ref, own_ref, before_ref, after_ref, far_ref, other_ref,
    turned_ref, terms_ref,
):
    attns = [own_ref, before_ref, after_ref, far_ref] + [other_ref.at[p] for p in range(4)]
    for place, attn in enumerate(attns):
        part = parts_ref[place]
        term = jnp.dot(attn[...], branch_ref[...], preferred_element_type=F32)
        for q in range(3):
            terms_ref[part, q * COLS : (q + 1) * COLS, :] = term[:, q * 128 : q * 128 + 128].astype(BF16)
        last = term[:, 384:512]
        rest = last[0:GROUP]
        for g in range(1, 4):
            rest = rest + pltpu.roll(last[g * GROUP : (g + 1) * GROUP], 24 * g, 1)
        tail = pltpu.roll(last[4 * GROUP : COLS], 96, 1)
        rest = jnp.concatenate([rest[0:16] + tail, rest[16:]], axis=0)
        terms_ref[part, AT3:AT4, :] = rest.astype(BF16)
        terms_ref[part, AT4:MESSAGE, :] = gain_ref[...]
    turned_ref[...] = branch_ref[...].T[:ROWS]


def fold_kernel(recv_ref, out_ref, wide_ref):
    total = recv_ref[0].astype(F32)
    for part in range(1, NY):
        total = total + recv_ref[part].astype(F32)
    rest = total[AT3:AT4]
    rest = [rest] + [pltpu.roll(rest, 128 - 24 * g, 1) for g in range(1, 5)]
    rest = jnp.concatenate(rest[:4] + [rest[4][0:16]], axis=0)
    wide = jnp.concatenate([total[0:AT1], total[AT1:AT2], total[AT2:AT3], rest], axis=1)
    wide = jnp.concatenate([wide, jnp.zeros((256 - COLS, WIDE), F32)], axis=0)
    wide_ref[...] = wide.T
    gain = total[AT4:AT5] + total[AT5:MESSAGE]
    gain = jnp.concatenate([gain[0:8], gain[8:16]], axis=1)
    for z in range(NZ):
        rows = wide_ref[z * BLOCK : z * BLOCK + 40, :]
        out_ref[z] = jnp.concatenate([rows, gain], axis=0).astype(BF16)


def settle_kernel(recv_ref, block_ref, gain_ref):
    total = recv_ref[0].astype(F32)
    for part in range(1, NZ):
        total = total + recv_ref[part].astype(F32)
    block_ref[...] = jnp.concatenate([total, jnp.zeros((16, 256), F32)], axis=0)
    gain = jnp.concatenate([total[40:48, 0:128], total[40:48, 128:256]], axis=0)
    for part in range(NMP):
        gain_ref[part] = gain


def spread_kernel(gain_ref, out_ref, wide_ref):
    wide_ref[...] = jnp.zeros_like(wide_ref)
    for part in range(NMP):
        gain = gain_ref[part]
        pieces = [gain[q * SUB : (q + 1) * SUB] for q in range(4)] + [jnp.zeros((SUB, 128), F32)]
        low = part * FEAT
        start = low // 128 * 128
        pieces = jnp.concatenate(pieces, axis=1)
        if low > start:
            pieces = pltpu.roll(pieces, low - start, 1)
        wide_ref[:, start : start + 640] += pieces
    out_ref[...] = wide_ref[:, 0:VW]


def gathered_kernel(
    tile_ref, parts_ref, weight_ref, scale_ref, own_ref, before_ref, after_ref, far_ref, other_ref,
    attn_ref, residual_ref, all_ref,
):
    pieces = [own_ref, before_ref, after_ref, far_ref] + [other_ref.at[p] for p in range(4)]
    for place, piece in enumerate(pieces):
        all_ref[parts_ref[place]] = piece[...]
    tile = tile_ref[0]
    at = pl.multiple_of((tile >> 1) * 128, 128)
    lane = lax.broadcasted_iota(jnp.int32, (COLS, WIDE), 1)
    total = jnp.zeros((COLS, TILES * VT), F32)
    tokens = []
    for part in range(NMP):
        low = part * FEAT
        start = low // 128 * 128
        width = min(640, VW - start)
        weight = weight_ref[:, start : start + width].astype(F32)
        if width < 640:
            weight = jnp.concatenate([weight, jnp.zeros((COLS, 640 - width), F32)], axis=1)
        if low > start:
            weight = pltpu.roll(weight, 640 - (low - start), 1)
        weight = jnp.where(lane < min(FEAT, VW - low), weight[:, :WIDE], 0.0).astype(BF16)
        total += jnp.dot(weight[:, :ROWS], all_ref[part], preferred_element_type=F32)
        tokens.append(all_ref[part, :, pl.ds(at, 128)].astype(F32)[:FEAT])
    attn_ref[...] = total.astype(BF16)
    tokens = jnp.concatenate(tokens, axis=0)[:VW].T
    tokens = jnp.where((tile & 1) == 0, tokens[0:VT], tokens[VT : 2 * VT])
    residual_ref[...] = (tokens / scale_ref[...]).astype(BF16)


def whole(count):
    return [pl.BlockSpec(memory_space=pltpu.VMEM)] * count


def scalars(count):
    return [pl.BlockSpec(memory_space=pltpu.SMEM)] * count


def gather_x(own):
    return tuple(
        lax.ppermute(own, "x", [(x, (x + step) % 4) for x in range(4)]) for step in (1, 3, 2)
    )


def swap_cores(four):
    return lax.ppermute(four, "c", [(0, 1), (1, 0)])


def last_places():
    pairs = []
    for z in range(NZ):
        for y in range(NY):
            for part in range(NMP):
                pairs.append(((z * NY + y) * NMP + part, (NZ * part + z) * NMP + y))
    return pairs


def in_hbm(count):
    return [pl.BlockSpec(memory_space=pltpu.HBM)] * count


def body(
    grad_proj, tile_counts, tile_home, saved_feat, ln_gain, layer_scale, attn_saved, proj_weight
):
    mp_index = lax.axis_index(MP)
    cols = attn_saved.shape[1]
    send = pl.pallas_call(
        cut_kernel,
        out_shape=jax.ShapeDtypeStruct((NMP, REST + 2 * PR, 128), BF16),
        in_specs=in_hbm(2),
        out_specs=whole(1)[0],
        scratch_shapes=[
            pltpu.VMEM((PR, PW), BF16),
            pltpu.VMEM((PR, PW), BF16),
            pltpu.VMEM((NMP, 2 * VT, 128), F32),
            pltpu.SemaphoreType.DMA((2,)),
        ],
        compiler_params=pltpu.CompilerParams(vmem_limit_bytes=60 * 1024 * 1024),
        name="cut",
    )(grad_proj, saved_feat)
    attn_own, send = lax.optimization_barrier((attn_saved.T, send))
    recv = lax.all_to_all(send, MP, 0, 0)
    attns = (attn_own,) + gather_x(attn_own)
    x_index, c_index = lax.axis_index("x"), lax.axis_index("c")
    near = jnp.stack([x_index, (x_index + 3) % 4, (x_index + 1) % 4, (x_index + 2) % 4]) * 2
    parts = jnp.concatenate([near + c_index, near + 1 - c_index]).astype(jnp.int32)

    slot_ids = jnp.arange(TILES, dtype=jnp.int32)
    matches = tile_home[0][None, :] == slot_ids[:, None]
    source = jnp.sum(jnp.where(matches, slot_ids[None, :], 0), axis=1).astype(jnp.int32)
    live = (source < jnp.sum(tile_counts)).astype(jnp.int32)
    pad = NMP * FEAT - VW
    gain = jnp.pad(ln_gain.reshape(SUB, VW), ((0, 0), (0, pad + WIDE - FEAT)))
    gain = lax.dynamic_slice_in_dim(gain, mp_index * FEAT, WIDE, axis=1)
    scale = jnp.pad(layer_scale, (0, pad + WIDE - FEAT))
    scale = lax.dynamic_slice_in_dim(scale, mp_index * FEAT, WIDE, axis=0)[None]
    inside = (jnp.arange(WIDE) < FEAT)[None]
    gain = jnp.where(inside, gain, 0.0)
    scale = jnp.where(inside, scale, 0.0)

    sums = pl.pallas_call(
        sums_kernel,
        out_shape=jax.ShapeDtypeStruct((NMP, 8, 128), F32),
        in_specs=scalars(2) + whole(2),
        out_specs=whole(1)[0],
        compiler_params=VMEM,
        name="sums",
    )(source, live, recv, gain)
    sums = lax.all_to_all(sums, MP, 0, 0)
    four, sums = lax.optimization_barrier((jnp.stack(attns), sums))
    attns = attns + (swap_cores(four),)

    branch, gains = pl.pallas_call(
        branch_kernel,
        out_shape=(
            jax.ShapeDtypeStruct((TILES * VT, WIDE), BF16),
            jax.ShapeDtypeStruct((2 * GAIN, 128), BF16),
        ),
        in_specs=scalars(2) + whole(4),
        out_specs=tuple(whole(2)),
        compiler_params=VMEM,
        name="branch",
    )(source, live, recv, gain, scale, sums)
    turned, terms = pl.pallas_call(
        terms_kernel,
        out_shape=(
            jax.ShapeDtypeStruct((ROWS, TILES * VT), BF16),
            jax.ShapeDtypeStruct((NMP, MESSAGE, 128), BF16),
        ),
        in_specs=scalars(1) + whole(7),
        out_specs=tuple(whole(2)),
        compiler_params=VMEM,
        name="terms",
    )(parts, branch, gains, *attns)

    terms = lax.all_to_all(terms, "y", 0, 0)
    terms = pl.pallas_call(
        fold_kernel,
        out_shape=jax.ShapeDtypeStruct((NZ, 48, 256), BF16),
        in_specs=whole(1),
        out_specs=whole(1)[0],
        scratch_shapes=[pltpu.VMEM((WIDE, 256), F32)],
        compiler_params=VMEM,
        name="fold",
    )(terms)
    terms = lax.all_to_all(terms, "z", 0, 0)

    turned = (turned,) + gather_x(turned)
    turned = turned + (swap_cores(jnp.stack(turned)),)
    attn_grad, residual_grad = pl.pallas_call(
        gathered_kernel,
        out_shape=(
            jax.ShapeDtypeStruct((cols, TILES * VT), BF16),
            jax.ShapeDtypeStruct((VT, VW), BF16),
        ),
        in_specs=scalars(2) + whole(7),
        out_specs=tuple(whole(2)),
        scratch_shapes=[pltpu.VMEM((NMP, ROWS, TILES * VT), BF16)],
        compiler_params=VMEM,
        name="gathered",
    )(mp_index.astype(jnp.int32)[None], parts, proj_weight.T, layer_scale[None], *turned)

    terms, attn_grad, residual_grad = lax.optimization_barrier((terms, attn_grad, residual_grad))
    part, gains = pl.pallas_call(
        settle_kernel,
        out_shape=(
            jax.ShapeDtypeStruct((64, 256), F32),
            jax.ShapeDtypeStruct((NMP, GAIN, 128), F32),
        ),
        in_specs=whole(1),
        out_specs=tuple(whole(2)),
        compiler_params=VMEM,
        name="settle",
    )(terms)

    proj_grad = lax.ppermute(part, DP + MP, last_places())[:BLOCK, :cols]
    gains = lax.all_to_all(gains, MP, 0, 0)
    gain_grad = pl.pallas_call(
        spread_kernel,
        out_shape=jax.ShapeDtypeStruct((SUB, VW), F32),
        in_specs=whole(1),
        out_specs=whole(1)[0],
        scratch_shapes=[pltpu.VMEM((SUB, 3456), F32)],
        compiler_params=VMEM,
        name="spread",
    )(gains)
    return (residual_grad, attn_grad.T, proj_grad, gain_grad.reshape(-1))


def solution(mesh):
    fine = Mesh(mesh.devices.reshape(NZ, NY, 4, 2), DP + MP)
    in_specs = (
        P(DP + MP, None),
        P(DP, None),
        P(DP, None),
        P(DP + MP, None),
        P(),
        P(),
        P(DP, MP),
        P(None, MP),
    )
    out_specs = (P(DP + MP, None), P(DP, MP), P(DP, MP), P())
    return jax.shard_map(body, mesh=fine, in_specs=in_specs, out_specs=out_specs, check_vma=False)
```

```python
import jax
import jax.numpy as jnp
from jax import lax
from jax.experimental import pallas as pl
from jax.experimental.pallas import tpu as pltpu
from jax.sharding import Mesh
from jax.sharding import PartitionSpec as P

VW = 3200
PW = 12800
EPSILON = 1e-05
DP = ("z", "y")
MP = ("x", "c")
NZ, NY, NMP = 12, 8, 8
BLOCK = 34
FEAT = NZ * BLOCK
WIDE = 512
ROWS = 416
REST = 384
TILES, PR, SUB, VT = 8, 16, 4, 64
VMEM = pltpu.CompilerParams(vmem_limit_bytes=48 * 1024 * 1024)
F32, BF16 = jnp.float32, jnp.bfloat16


def split3(value):
    high = value.astype(BF16).astype(F32)
    middle = (value - high).astype(BF16).astype(F32)
    low = (value - high - middle).astype(BF16).astype(F32)
    return high, middle, low


def cut_kernel(grad_hbm, feat_hbm, out_ref, grad_ref, feat_ref, last_ref, sems):
    feat_copy = pltpu.make_async_copy(feat_hbm, feat_ref, sems.at[0])
    grad_copy = pltpu.make_async_copy(grad_hbm, grad_ref, sems.at[1])
    feat_copy.start()
    grad_copy.start()
    feat_copy.wait()
    values = feat_ref[...].astype(F32)
    mean = jnp.mean(values, axis=-1, keepdims=True)
    centered = values - mean
    inverse_std = lax.rsqrt(jnp.mean(centered * centered, axis=-1, keepdims=True) + EPSILON)
    marks = split3(mean) + split3(inverse_std)
    lane = lax.broadcasted_iota(jnp.int32, (PR, WIDE), 1)
    grad_copy.wait()
    for part in range(NMP):
        live = lane < min(FEAT, VW - part * FEAT)
        for sub in range(SUB):
            low = sub * VW + part * FEAT
            start = low // 128 * 128
            width = min(640, PW - start)
            for which, ref in enumerate((grad_ref, feat_ref)):
                window = ref[:, start : start + width].astype(F32)
                if width < 640:
                    window = jnp.concatenate([window, jnp.zeros((PR, 640 - width), F32)], axis=1)
                if low > start:
                    window = pltpu.roll(window, 640 - (low - start), 1)
                chunk = jnp.where(live, window[:, :WIDE], 0.0)
                if which == 1 and sub == 0:
                    for at, mark in enumerate(marks):
                        chunk = jnp.where(lane == FEAT + at, mark, chunk)
                row = which * VT + sub * PR
                for tile in range(3):
                    at = tile * 2 * VT + row
                    out_ref[part, at : at + PR, :] = chunk[:, tile * 128 : tile * 128 + 128].astype(BF16)
                last_ref[part, row : row + PR, :] = chunk[:, 384:512]
    for part in range(NMP):
        rest = last_ref[part, 0:32, :]
        for group in range(1, 4):
            rest = rest + pltpu.roll(last_ref[part, 32 * group : 32 * group + 32, :], 32 * group, 1)
        out_ref[part, REST : REST + 2 * PR, :] = rest.astype(BF16)


def unpack(ref, tile, which):
    at = [q * 2 * VT + which * VT for q in range(3)]
    pieces = [ref[tile, r : r + VT, :].astype(F32) for r in at]
    rest = ref[tile, REST : REST + 2 * PR, :].astype(F32)
    turn = (128 - 64 * which) % 128
    rest = jnp.concatenate(
        [pltpu.roll(rest, turn, 1) if turn else rest, pltpu.roll(rest, (turn + 96) % 128, 1)], axis=0
    )
    return pieces, rest


def slot_values(tile, source_ref, live_ref, recv_ref):
    pieces, rest = unpack(recv_ref, source_ref[tile], 0)
    rest = jnp.where(lax.broadcasted_iota(jnp.int32, (VT, 128), 1) < FEAT - 384, rest, 0.0)
    grads = jnp.concatenate(pieces + [rest], axis=1)
    grads = jnp.where(live_ref[tile] > 0, grads, 0.0)
    pieces, rest = unpack(recv_ref, tile, 1)
    feats = jnp.concatenate(pieces + [rest], axis=1)
    marks = rest[0:PR]
    lane = lax.broadcasted_iota(jnp.int32, (PR, 128), 1) + 384
    in_mean = (lane >= FEAT) & (lane < FEAT + 3)
    in_std = (lane >= FEAT + 3) & (lane < FEAT + 6)
    mean = jnp.sum(jnp.where(in_mean, marks, 0.0), axis=-1, keepdims=True)
    inverse_std = jnp.sum(jnp.where(in_std, marks, 0.0), axis=-1, keepdims=True)
    upstream = [grads[s * PR : (s + 1) * PR] for s in range(SUB)]
    normed = [(feats[s * PR : (s + 1) * PR] - mean) * inverse_std for s in range(SUB)]
    return upstream, normed, inverse_std


def sums_kernel(source_ref, live_ref, recv_ref, gain_ref, out_ref):
    lane = lax.broadcasted_iota(jnp.int32, (PR, 128), 1)
    rows = []
    for tile in range(TILES):
        upstream, normed, _ = slot_values(tile, source_ref, live_ref, recv_ref)
        first = jnp.zeros((PR, WIDE), F32)
        second = jnp.zeros((PR, WIDE), F32)
        for s in range(SUB):
            scaled = upstream[s] * gain_ref[s : s + 1, :]
            first = first + scaled
            second = second + scaled * normed[s]
        first = jnp.sum(first, axis=-1, keepdims=True)
        second = jnp.sum(second, axis=-1, keepdims=True)
        rows.append(jnp.where(lane == 0, first, jnp.where(lane == 1, second, 0.0)))
    turned = jnp.concatenate(rows, axis=0).T[0:8, :]
    for part in range(NMP):
        out_ref[part] = turned


COLS, GROUP, GAIN = 208, 48, 16
AT1, AT2, AT3 = COLS, 2 * COLS, 3 * COLS
AT4 = AT3 + GROUP
MESSAGE = AT4 + GAIN
THIRD = 72
SPARE = 3 * BLOCK


def branch_kernel(
    source_ref, live_ref, recv_ref, gain_ref, scale_ref, sums_ref, branch_ref, gain_out_ref
):
    total = sums_ref[0]
    for part in range(1, NMP):
        total = total + sums_ref[part]
    means = jnp.concatenate([total, jnp.zeros((120, 128), F32)], axis=0).T * (1.0 / PW)
    lane = lax.broadcasted_iota(jnp.int32, (PR, 128), 1)
    token = lax.broadcasted_iota(jnp.int32, (VT, VT), 0)
    place = lax.broadcasted_iota(jnp.int32, (VT, VT), 1)
    sub_of = ((token >> 3) & 1) * 2 + (token & 1)
    row_of = (token >> 4) * 4 + ((token >> 1) & 3)
    order = (place == sub_of * PR + row_of).astype(BF16)
    gains = [jnp.zeros((PR, WIDE), F32) for _ in range(SUB)]
    for tile in range(TILES):
        upstream, normed, inverse_std = slot_values(tile, source_ref, live_ref, recv_ref)
        own = means[tile * PR : (tile + 1) * PR]
        first = jnp.sum(jnp.where(lane == 0, own, 0.0), axis=-1, keepdims=True)
        second = jnp.sum(jnp.where(lane == 1, own, 0.0), axis=-1, keepdims=True)
        branch = []
        for s in range(SUB):
            scaled = upstream[s] * gain_ref[s : s + 1, :]
            grad = inverse_std * (scaled - first - normed[s] * second)
            branch.append((grad * scale_ref[...]).astype(BF16))
            gains[s] = gains[s] + upstream[s] * normed[s]
        branch = jnp.dot(order, jnp.concatenate(branch, axis=0), preferred_element_type=F32)
        branch_ref[tile * VT : (tile + 1) * VT, :] = branch.astype(BF16)
    gain = jnp.concatenate([jnp.sum(g, axis=0, keepdims=True) for g in gains], axis=0)
    gain = jnp.concatenate([gain[:, q * 128 : (q + 1) * 128] for q in range(4)], axis=0)
    gain_out_ref[...] = gain.astype(BF16)


def terms_kernel(
    parts_ref, branch_ref, gain_ref, own_ref, before_ref, after_ref, far_ref, other_ref,
    terms_ref,
):
    attns = [own_ref, before_ref, after_ref, far_ref] + [other_ref.at[p] for p in range(4)]
    for place, attn in enumerate(attns):
        part = parts_ref[place]
        term = jnp.dot(attn[...], branch_ref[...], preferred_element_type=F32)
        for q in range(3):
            terms_ref[part, q * COLS : (q + 1) * COLS, :] = term[:, q * 128 : q * 128 + 128].astype(BF16)
        last = term[:, 384:512]
        rest = last[0:GROUP]
        for g in range(1, 4):
            rest = rest + pltpu.roll(last[g * GROUP : (g + 1) * GROUP], 24 * g, 1)
        tail = pltpu.roll(last[4 * GROUP : COLS], 96, 1)
        rest = jnp.concatenate([rest[0:16] + tail, rest[16:]], axis=0)
        terms_ref[part, AT3:AT4, :] = rest.astype(BF16)
        terms_ref[part, AT4:MESSAGE, :] = gain_ref[...]


def turn_kernel(branch_ref, turned_ref):
    turned_ref[...] = branch_ref[...].T[:ROWS]


def left(array, lanes):
    lanes = lanes % 128
    return pltpu.roll(array, 128 - lanes, 1) if lanes else array


def fold_kernel(recv_ref, out_ref):
    total = recv_ref[0].astype(F32)
    for part in range(1, NY):
        total = total + recv_ref[part].astype(F32)
    rest = total[AT3:AT4]
    rest = [left(rest, 24 * g) for g in range(5)]
    rest = jnp.concatenate(rest[:4] + [rest[4][0:16]], axis=0)
    tiles = [total[0:AT1], total[AT1:AT2], total[AT2:AT3], rest]
    gain = total[AT4:MESSAGE]
    gains = [left(gain[0:12], 26 * e - SPARE) for e in range(5)] + [left(gain[12:16], -SPARE)]
    gains = jnp.concatenate(gains + [jnp.zeros((THIRD - 64, 128), F32)], axis=0)
    lane = lax.broadcasted_iota(jnp.int32, (THIRD, 128), 1)
    for z in range(NZ):
        tile, at = divmod(z * BLOCK, 128)
        packed = gains
        for group in range(3):
            rows = slice(group * THIRD, min(COLS, (group + 1) * THIRD))
            shift = at - group * BLOCK
            piece = left(tiles[tile][rows], shift)
            if at + BLOCK > 128:
                inside = lane[: piece.shape[0]] < group * BLOCK + 128 - at
                piece = jnp.where(inside, piece, left(tiles[tile + 1][rows], shift))
            if group == 2:
                piece = jnp.concatenate([piece, jnp.zeros((3 * THIRD - COLS, 128), F32)], axis=0)
            inside = (lane >= group * BLOCK) & (lane < (group + 1) * BLOCK)
            packed = jnp.where(inside, piece, packed)
        out_ref[z] = packed.astype(BF16)


def settle_kernel(recv_ref, block_ref, gain_ref):
    total = recv_ref[0].astype(F32)
    for part in range(1, NZ):
        total = total + recv_ref[part].astype(F32)
    block = [total, left(total, BLOCK), left(total, 2 * BLOCK)[0 : COLS - 2 * THIRD]]
    block = jnp.concatenate(block + [jnp.zeros((256 - COLS, 128), F32)], axis=0).T
    block_ref[...] = block[0 : block_ref.shape[0]]
    lane = lax.broadcasted_iota(jnp.int32, (12, 128), 1)
    gain = jnp.zeros((12, 128), F32)
    for e in range(5):
        inside = (lane >= 26 * e) & (lane < 26 * e + 26)
        gain = jnp.where(inside, left(total[12 * e : 12 * e + 12], SPARE - 26 * e), gain)
    rest = jnp.where(lane[0:4] < FEAT - 384, left(total[60:64], SPARE), 0.0)
    gain = jnp.concatenate([gain, rest], axis=0)
    for part in range(NMP):
        gain_ref[part] = gain


def spread_kernel(gain_ref, out_ref, wide_ref):
    wide_ref[...] = jnp.zeros_like(wide_ref)
    for part in range(NMP):
        gain = gain_ref[part]
        pieces = [gain[q * SUB : (q + 1) * SUB] for q in range(4)] + [jnp.zeros((SUB, 128), F32)]
        low = part * FEAT
        start = low // 128 * 128
        pieces = jnp.concatenate(pieces, axis=1)
        if low > start:
            pieces = pltpu.roll(pieces, low - start, 1)
        wide_ref[:, start : start + 640] += pieces
    out_ref[...] = wide_ref[:, 0:VW]


def gathered_kernel(
    tile_ref, parts_ref, weight_ref, scale_ref, own_ref, before_ref, after_ref, far_ref, other_ref,
    attn_ref, residual_ref, all_ref,
):
    pieces = [own_ref, before_ref, after_ref, far_ref] + [other_ref.at[p] for p in range(4)]
    for place, piece in enumerate(pieces):
        all_ref[parts_ref[place]] = piece[...]
    tile = tile_ref[0]
    at = pl.multiple_of((tile >> 1) * 128, 128)
    lane = lax.broadcasted_iota(jnp.int32, (COLS, WIDE), 1)
    total = jnp.zeros((COLS, TILES * VT), F32)
    tokens = []
    for part in range(NMP):
        low = part * FEAT
        start = low // 128 * 128
        width = min(640, VW - start)
        weight = weight_ref[:, start : start + width].astype(F32)
        if width < 640:
            weight = jnp.concatenate([weight, jnp.zeros((COLS, 640 - width), F32)], axis=1)
        if low > start:
            weight = pltpu.roll(weight, 640 - (low - start), 1)
        weight = jnp.where(lane < min(FEAT, VW - low), weight[:, :WIDE], 0.0).astype(BF16)
        total += jnp.dot(weight[:, :ROWS], all_ref[part], preferred_element_type=F32)
        tokens.append(all_ref[part, :, pl.ds(at, 128)].astype(F32)[:FEAT])
    attn_ref[...] = total.astype(BF16)
    tokens = jnp.concatenate(tokens, axis=0)[:VW].T
    tokens = jnp.where((tile & 1) == 0, tokens[0:VT], tokens[VT : 2 * VT])
    residual_ref[...] = (tokens / scale_ref[...]).astype(BF16)


def whole(count):
    return [pl.BlockSpec(memory_space=pltpu.VMEM)] * count


def scalars(count):
    return [pl.BlockSpec(memory_space=pltpu.SMEM)] * count


def gather_x(own):
    return tuple(
        lax.ppermute(own, "x", [(x, (x + step) % 4) for x in range(4)]) for step in (1, 3, 2)
    )


def swap_cores(four):
    return lax.ppermute(four, "c", [(0, 1), (1, 0)])


def last_places():
    pairs = []
    for z in range(NZ):
        for y in range(NY):
            for part in range(NMP):
                pairs.append(((z * NY + y) * NMP + part, (NZ * part + z) * NMP + y))
    return pairs


def in_hbm(count):
    return [pl.BlockSpec(memory_space=pltpu.HBM)] * count


def body(
    grad_proj, tile_counts, tile_home, saved_feat, ln_gain, layer_scale, attn_saved, proj_weight
):
    mp_index = lax.axis_index(MP)
    cols = attn_saved.shape[1]
    send = pl.pallas_call(
        cut_kernel,
        out_shape=jax.ShapeDtypeStruct((NMP, REST + 2 * PR, 128), BF16),
        in_specs=in_hbm(2),
        out_specs=whole(1)[0],
        scratch_shapes=[
            pltpu.VMEM((PR, PW), BF16),
            pltpu.VMEM((PR, PW), BF16),
            pltpu.VMEM((NMP, 2 * VT, 128), F32),
            pltpu.SemaphoreType.DMA((2,)),
        ],
        compiler_params=pltpu.CompilerParams(vmem_limit_bytes=60 * 1024 * 1024),
        name="cut",
    )(grad_proj, saved_feat)
    attn_own, send = lax.optimization_barrier((attn_saved.T, send))
    recv = lax.all_to_all(send, MP, 0, 0)
    attns = (attn_own,) + gather_x(attn_own)
    x_index, c_index = lax.axis_index("x"), lax.axis_index("c")
    near = jnp.stack([x_index, (x_index + 3) % 4, (x_index + 1) % 4, (x_index + 2) % 4]) * 2
    parts = jnp.concatenate([near + c_index, near + 1 - c_index]).astype(jnp.int32)

    slot_ids = jnp.arange(TILES, dtype=jnp.int32)
    matches = tile_home[0][None, :] == slot_ids[:, None]
    source = jnp.sum(jnp.where(matches, slot_ids[None, :], 0), axis=1).astype(jnp.int32)
    live = (source < jnp.sum(tile_counts)).astype(jnp.int32)
    pad = NMP * FEAT - VW
    gain = jnp.pad(ln_gain.reshape(SUB, VW), ((0, 0), (0, pad + WIDE - FEAT)))
    gain = lax.dynamic_slice_in_dim(gain, mp_index * FEAT, WIDE, axis=1)
    scale = jnp.pad(layer_scale, (0, pad + WIDE - FEAT))
    scale = lax.dynamic_slice_in_dim(scale, mp_index * FEAT, WIDE, axis=0)[None]
    inside = (jnp.arange(WIDE) < FEAT)[None]
    gain = jnp.where(inside, gain, 0.0)
    scale = jnp.where(inside, scale, 0.0)

    sums = pl.pallas_call(
        sums_kernel,
        out_shape=jax.ShapeDtypeStruct((NMP, 8, 128), F32),
        in_specs=scalars(2) + whole(2),
        out_specs=whole(1)[0],
        compiler_params=VMEM,
        name="sums",
    )(source, live, recv, gain)
    sums = lax.all_to_all(sums, MP, 0, 0)
    four, sums = lax.optimization_barrier((jnp.stack(attns), sums))
    attns = attns + (swap_cores(four),)

    branch, gains = pl.pallas_call(
        branch_kernel,
        out_shape=(
            jax.ShapeDtypeStruct((TILES * VT, WIDE), BF16),
            jax.ShapeDtypeStruct((GAIN, 128), BF16),
        ),
        in_specs=scalars(2) + whole(4),
        out_specs=tuple(whole(2)),
        compiler_params=VMEM,
        name="branch",
    )(source, live, recv, gain, scale, sums)
    terms = pl.pallas_call(
        terms_kernel,
        out_shape=jax.ShapeDtypeStruct((NMP, MESSAGE, 128), BF16),
        in_specs=scalars(1) + whole(7),
        out_specs=whole(1)[0],
        compiler_params=VMEM,
        name="terms",
    )(parts, branch, gains, *attns)

    terms = lax.all_to_all(terms, "y", 0, 0)
    terms = pl.pallas_call(
        fold_kernel,
        out_shape=jax.ShapeDtypeStruct((NZ, THIRD, 128), BF16),
        in_specs=whole(1),
        out_specs=whole(1)[0],
        compiler_params=VMEM,
        name="fold",
    )(terms)
    terms = lax.all_to_all(terms, "z", 0, 0)

    turned = pl.pallas_call(
        turn_kernel,
        out_shape=jax.ShapeDtypeStruct((ROWS, TILES * VT), BF16),
        in_specs=whole(1),
        out_specs=whole(1)[0],
        compiler_params=VMEM,
        name="turn",
    )(branch)
    turned = (turned,) + gather_x(turned)
    turned = turned + (swap_cores(jnp.stack(turned)),)
    attn_grad, residual_grad = pl.pallas_call(
        gathered_kernel,
        out_shape=(
            jax.ShapeDtypeStruct((cols, TILES * VT), BF16),
            jax.ShapeDtypeStruct((VT, VW), BF16),
        ),
        in_specs=scalars(2) + whole(7),
        out_specs=tuple(whole(2)),
        scratch_shapes=[pltpu.VMEM((NMP, ROWS, TILES * VT), BF16)],
        compiler_params=VMEM,
        name="gathered",
    )(mp_index.astype(jnp.int32)[None], parts, proj_weight.T, layer_scale[None], *turned)

    terms, attn_grad, residual_grad = lax.optimization_barrier((terms, attn_grad, residual_grad))
    part, gains = pl.pallas_call(
        settle_kernel,
        out_shape=(
            jax.ShapeDtypeStruct((64, 256), F32),
            jax.ShapeDtypeStruct((NMP, GAIN, 128), F32),
        ),
        in_specs=whole(1),
        out_specs=tuple(whole(2)),
        compiler_params=VMEM,
        name="settle",
    )(terms)

    proj_grad = lax.ppermute(part, DP + MP, last_places())[:BLOCK, :cols]
    gains = lax.all_to_all(gains, MP, 0, 0)
    gain_grad = pl.pallas_call(
        spread_kernel,
        out_shape=jax.ShapeDtypeStruct((SUB, VW), F32),
        in_specs=whole(1),
        out_specs=whole(1)[0],
        scratch_shapes=[pltpu.VMEM((SUB, 3456), F32)],
        compiler_params=VMEM,
        name="spread",
    )(gains)
    return (residual_grad, attn_grad.T, proj_grad, gain_grad.reshape(-1))


def solution(mesh):
    fine = Mesh(mesh.devices.reshape(NZ, NY, 4, 2), DP + MP)
    in_specs = (
        P(DP + MP, None),
        P(DP, None),
        P(DP, None),
        P(DP + MP, None),
        P(),
        P(),
        P(DP, MP),
        P(None, MP),
    )
    out_specs = (P(DP + MP, None), P(DP, MP), P(DP, MP), P())
    return jax.shard_map(body, mesh=fine, in_specs=in_specs, out_specs=out_specs, check_vma=False)
```

```python
import jax
import jax.numpy as jnp
from jax import lax
from jax.experimental import pallas as pl
from jax.experimental.pallas import tpu as pltpu
from jax.sharding import Mesh
from jax.sharding import PartitionSpec as P

VW = 3200
PW = 12800
EPSILON = 1e-05
DP = ("z", "y")
MP = ("x", "c")
NZ, NY, NMP = 12, 8, 8
BLOCK = 34
FEAT = NZ * BLOCK
WIDE = 512
ROWS = 416
REST = 384
TILES, PR, SUB, VT = 8, 16, 4, 64
VMEM = pltpu.CompilerParams(vmem_limit_bytes=48 * 1024 * 1024)
ROOMY = pltpu.CompilerParams(vmem_limit_bytes=56 * 1024 * 1024)
F32, BF16 = jnp.float32, jnp.bfloat16


def split3(value):
    high = value.astype(BF16).astype(F32)
    middle = (value - high).astype(BF16).astype(F32)
    low = (value - high - middle).astype(BF16).astype(F32)
    return high, middle, low


def cut_kernel(grad_hbm, feat_hbm, out_ref, grad_ref, feat_ref, last_ref, sems):
    feat_copy = pltpu.make_async_copy(feat_hbm, feat_ref, sems.at[0])
    grad_copy = pltpu.make_async_copy(grad_hbm, grad_ref, sems.at[1])
    feat_copy.start()
    grad_copy.start()
    feat_copy.wait()
    values = feat_ref[...].astype(F32)
    mean = jnp.mean(values, axis=-1, keepdims=True)
    centered = values - mean
    inverse_std = lax.rsqrt(jnp.mean(centered * centered, axis=-1, keepdims=True) + EPSILON)
    marks = split3(mean) + split3(inverse_std)
    lane = lax.broadcasted_iota(jnp.int32, (PR, WIDE), 1)
    grad_copy.wait()
    for part in range(NMP):
        live = lane < min(FEAT, VW - part * FEAT)
        for sub in range(SUB):
            low = sub * VW + part * FEAT
            start = low // 128 * 128
            width = min(640, PW - start)
            for which, ref in enumerate((grad_ref, feat_ref)):
                window = ref[:, start : start + width].astype(F32)
                if width < 640:
                    window = jnp.concatenate([window, jnp.zeros((PR, 640 - width), F32)], axis=1)
                if low > start:
                    window = pltpu.roll(window, 640 - (low - start), 1)
                chunk = jnp.where(live, window[:, :WIDE], 0.0)
                if which == 1 and sub == 0:
                    for at, mark in enumerate(marks):
                        chunk = jnp.where(lane == FEAT + at, mark, chunk)
                row = which * VT + sub * PR
                for tile in range(3):
                    at = tile * 2 * VT + row
                    out_ref[part, at : at + PR, :] = chunk[:, tile * 128 : tile * 128 + 128].astype(BF16)
                last_ref[part, row : row + PR, :] = chunk[:, 384:512]
    for part in range(NMP):
        rest = last_ref[part, 0:32, :]
        for group in range(1, 4):
            rest = rest + pltpu.roll(last_ref[part, 32 * group : 32 * group + 32, :], 32 * group, 1)
        out_ref[part, REST : REST + 2 * PR, :] = rest.astype(BF16)


def unpack(ref, tile, which):
    at = [q * 2 * VT + which * VT for q in range(3)]
    pieces = [ref[tile, r : r + VT, :].astype(F32) for r in at]
    rest = ref[tile, REST : REST + 2 * PR, :].astype(F32)
    turn = (128 - 64 * which) % 128
    rest = jnp.concatenate(
        [pltpu.roll(rest, turn, 1) if turn else rest, pltpu.roll(rest, (turn + 96) % 128, 1)], axis=0
    )
    return pieces, rest


def wide(array):
    return jnp.concatenate([array] * (WIDE // 128), axis=1)


def row_stats(recv_ref):
    marks = jnp.concatenate([recv_ref[t, REST : REST + PR, :] for t in range(TILES)], axis=0)
    low = 64 + FEAT - 384
    lane = lax.broadcasted_iota(jnp.int32, (128, 256), 0)
    which = lax.broadcasted_iota(jnp.int32, (128, 256), 1) >> 7
    pick = (lane >= low + 3 * which) & (lane < low + 3 * which + 3)
    return jnp.dot(marks, pick.astype(F32).astype(BF16), preferred_element_type=F32)


def slot_values(tile, source_ref, live_ref, recv_ref, stats):
    pieces, rest = unpack(recv_ref, source_ref[tile], 0)
    rest = jnp.where(lax.broadcasted_iota(jnp.int32, (VT, 128), 1) < FEAT - 384, rest, 0.0)
    grads = jnp.concatenate(pieces + [rest], axis=1)
    grads = jnp.where(live_ref[tile] > 0, grads, 0.0)
    pieces, rest = unpack(recv_ref, tile, 1)
    feats = jnp.concatenate(pieces + [rest], axis=1)
    mean = wide(stats[tile * PR : (tile + 1) * PR, 0:128])
    inverse_std = wide(stats[tile * PR : (tile + 1) * PR, 128:256])
    upstream = [grads[s * PR : (s + 1) * PR] for s in range(SUB)]
    normed = [(feats[s * PR : (s + 1) * PR] - mean) * inverse_std for s in range(SUB)]
    return upstream, normed, inverse_std


def sums_kernel(source_ref, live_ref, recv_ref, gain_ref, out_ref):
    stats = row_stats(recv_ref)
    firsts, seconds = [], []
    for tile in range(TILES):
        upstream, normed, _ = slot_values(tile, source_ref, live_ref, recv_ref, stats)
        first = jnp.zeros((PR, WIDE), F32)
        second = jnp.zeros((PR, WIDE), F32)
        for s in range(SUB):
            scaled = upstream[s] * gain_ref[s : s + 1, :]
            first = first + scaled
            second = second + scaled * normed[s]
        firsts.append(sum(first[:, q * 128 : q * 128 + 128] for q in range(4)))
        seconds.append(sum(second[:, q * 128 : q * 128 + 128] for q in range(4)))
    first = jnp.sum(jnp.concatenate(firsts, axis=0).T, axis=0, keepdims=True)
    second = jnp.sum(jnp.concatenate(seconds, axis=0).T, axis=0, keepdims=True)
    row = lax.broadcasted_iota(jnp.int32, (8, 128), 0)
    both = jnp.where(row == 0, first, jnp.where(row == 1, second, 0.0))
    for part in range(NMP):
        out_ref[part] = both


COLS, GROUP, GAIN = 208, 48, 16
AT1, AT2, AT3 = COLS, 2 * COLS, 3 * COLS
AT4 = AT3 + GROUP
MESSAGE = AT4 + GAIN
THIRD = 72
SPARE = 3 * BLOCK


def branch_kernel(
    source_ref, live_ref, recv_ref, gain_ref, scale_ref, sums_ref, branch_ref, gain_out_ref
):
    total = sums_ref[0]
    for part in range(1, NMP):
        total = total + sums_ref[part]
    total = total * (1.0 / PW)
    firsts = jnp.broadcast_to(total[0:1], (128, 128)).T
    seconds = jnp.broadcast_to(total[1:2], (128, 128)).T
    stats = row_stats(recv_ref)
    token = lax.broadcasted_iota(jnp.int32, (VT, VT), 0)
    place = lax.broadcasted_iota(jnp.int32, (VT, VT), 1)
    sub_of = ((token >> 3) & 1) * 2 + (token & 1)
    row_of = (token >> 4) * 4 + ((token >> 1) & 3)
    order = (place == sub_of * PR + row_of).astype(BF16)
    gains = [jnp.zeros((PR, WIDE), F32) for _ in range(SUB)]
    for tile in range(TILES):
        upstream, normed, inverse_std = slot_values(tile, source_ref, live_ref, recv_ref, stats)
        first = wide(firsts[tile * PR : (tile + 1) * PR])
        second = wide(seconds[tile * PR : (tile + 1) * PR])
        branch = []
        for s in range(SUB):
            scaled = upstream[s] * gain_ref[s : s + 1, :]
            grad = inverse_std * (scaled - first - normed[s] * second)
            branch.append((grad * scale_ref[...]).astype(BF16))
            gains[s] = gains[s] + upstream[s] * normed[s]
        branch = jnp.dot(order, jnp.concatenate(branch, axis=0), preferred_element_type=F32)
        branch_ref[tile * VT : (tile + 1) * VT, :] = branch.astype(BF16)
    gain = jnp.concatenate([jnp.sum(g, axis=0, keepdims=True) for g in gains], axis=0)
    gain = jnp.concatenate([gain[:, q * 128 : (q + 1) * 128] for q in range(4)], axis=0)
    gain_out_ref[...] = gain.astype(BF16)


def terms_kernel(
    parts_ref, branch_ref, gain_ref, own_ref, before_ref, after_ref, far_ref, other_ref,
    terms_ref,
):
    attns = [own_ref, before_ref, after_ref, far_ref] + [other_ref.at[p] for p in range(4)]
    for place, attn in enumerate(attns):
        part = parts_ref[place]
        term = jnp.dot(attn[...], branch_ref[...], preferred_element_type=F32)
        for q in range(3):
            terms_ref[part, q * COLS : (q + 1) * COLS, :] = term[:, q * 128 : q * 128 + 128].astype(BF16)
        last = term[:, 384:512]
        rest = last[0:GROUP]
        for g in range(1, 4):
            rest = rest + pltpu.roll(last[g * GROUP : (g + 1) * GROUP], 24 * g, 1)
        tail = pltpu.roll(last[4 * GROUP : COLS], 96, 1)
        rest = jnp.concatenate([rest[0:16] + tail, rest[16:]], axis=0)
        terms_ref[part, AT3:AT4, :] = rest.astype(BF16)
        terms_ref[part, AT4:MESSAGE, :] = gain_ref[...]


def turn_kernel(branch_ref, turned_ref):
    turned_ref[...] = branch_ref[...].T[:ROWS]


def left(array, lanes):
    lanes = lanes % 128
    return pltpu.roll(array, 128 - lanes, 1) if lanes else array


def fold_kernel(recv_ref, out_ref):
    total = recv_ref[0].astype(F32)
    for part in range(1, NY):
        total = total + recv_ref[part].astype(F32)
    rest = total[AT3:AT4]
    rest = [left(rest, 24 * g) for g in range(5)]
    rest = jnp.concatenate(rest[:4] + [rest[4][0:16]], axis=0)
    tiles = [total[0:AT1], total[AT1:AT2], total[AT2:AT3], rest]
    gain = total[AT4:MESSAGE]
    gains = [left(gain[0:12], 26 * e - SPARE) for e in range(5)] + [left(gain[12:16], -SPARE)]
    gains = jnp.concatenate(gains + [jnp.zeros((THIRD - 64, 128), F32)], axis=0)
    lane = lax.broadcasted_iota(jnp.int32, (THIRD, 128), 1)
    for z in range(NZ):
        tile, at = divmod(z * BLOCK, 128)
        packed = gains
        for group in range(3):
            rows = slice(group * THIRD, min(COLS, (group + 1) * THIRD))
            shift = at - group * BLOCK
            piece = left(tiles[tile][rows], shift)
            if at + BLOCK > 128:
                inside = lane[: piece.shape[0]] < group * BLOCK + 128 - at
                piece = jnp.where(inside, piece, left(tiles[tile + 1][rows], shift))
            if group == 2:
                piece = jnp.concatenate([piece, jnp.zeros((3 * THIRD - COLS, 128), F32)], axis=0)
            inside = (lane >= group * BLOCK) & (lane < (group + 1) * BLOCK)
            packed = jnp.where(inside, piece, packed)
        out_ref[z] = packed.astype(BF16)


def settle_kernel(recv_ref, block_ref, gain_ref):
    total = recv_ref[0].astype(F32)
    for part in range(1, NZ):
        total = total + recv_ref[part].astype(F32)
    block = [total, left(total, BLOCK), left(total, 2 * BLOCK)[0 : COLS - 2 * THIRD]]
    block = jnp.concatenate(block + [jnp.zeros((256 - COLS, 128), F32)], axis=0).T
    block_ref[...] = block[0 : block_ref.shape[0]]
    lane = lax.broadcasted_iota(jnp.int32, (12, 128), 1)
    gain = jnp.zeros((12, 128), F32)
    for e in range(5):
        inside = (lane >= 26 * e) & (lane < 26 * e + 26)
        gain = jnp.where(inside, left(total[12 * e : 12 * e + 12], SPARE - 26 * e), gain)
    rest = jnp.where(lane[0:4] < FEAT - 384, left(total[60:64], SPARE), 0.0)
    gain = jnp.concatenate([gain, rest], axis=0)
    for part in range(NMP):
        gain_ref[part] = gain


def spread_kernel(gain_ref, out_ref, wide_ref):
    wide_ref[...] = jnp.zeros_like(wide_ref)
    for part in range(NMP):
        gain = gain_ref[part]
        pieces = [gain[q * SUB : (q + 1) * SUB] for q in range(4)] + [jnp.zeros((SUB, 128), F32)]
        low = part * FEAT
        start = low // 128 * 128
        pieces = jnp.concatenate(pieces, axis=1)
        if low > start:
            pieces = pltpu.roll(pieces, low - start, 1)
        wide_ref[:, start : start + 640] += pieces
    for sub in range(SUB):
        for tile in range(VW // 128):
            row = sub * (VW // 128) + tile
            out_ref[row : row + 1, :] = wide_ref[sub : sub + 1, tile * 128 : tile * 128 + 128]


def gathered_kernel(
    tile_ref, parts_ref, weight_ref, scale_ref, own_ref, before_ref, after_ref, far_ref, other_ref,
    attn_ref, residual_ref, all_ref,
):
    pieces = [own_ref, before_ref, after_ref, far_ref] + [other_ref.at[p] for p in range(4)]
    for place, piece in enumerate(pieces):
        all_ref[parts_ref[place]] = piece[...]
    tile = tile_ref[0]
    at = pl.multiple_of((tile >> 1) * 128, 128)
    lane = lax.broadcasted_iota(jnp.int32, (COLS, WIDE), 1)
    total = jnp.zeros((COLS, TILES * VT), F32)
    tokens = []
    for part in range(NMP):
        low = part * FEAT
        start = low // 128 * 128
        width = min(640, VW - start)
        weight = weight_ref[:, start : start + width].astype(F32)
        if width < 640:
            weight = jnp.concatenate([weight, jnp.zeros((COLS, 640 - width), F32)], axis=1)
        if low > start:
            weight = pltpu.roll(weight, 640 - (low - start), 1)
        weight = jnp.where(lane < min(FEAT, VW - low), weight[:, :WIDE], 0.0).astype(BF16)
        total += jnp.dot(weight[:, :ROWS], all_ref[part], preferred_element_type=F32)
        tokens.append(all_ref[part, :, pl.ds(at, 128)].astype(F32)[:FEAT])
    attn_ref[...] = total.astype(BF16)
    tokens = jnp.concatenate(tokens, axis=0)[:VW].T
    tokens = jnp.where((tile & 1) == 0, tokens[0:VT], tokens[VT : 2 * VT])
    residual_ref[...] = (tokens / scale_ref[...]).astype(BF16)


def whole(count):
    return [pl.BlockSpec(memory_space=pltpu.VMEM)] * count


def scalars(count):
    return [pl.BlockSpec(memory_space=pltpu.SMEM)] * count


def gather_x(own):
    return tuple(
        lax.ppermute(own, "x", [(x, (x + step) % 4) for x in range(4)]) for step in (1, 3, 2)
    )


def swap_cores(four):
    return lax.ppermute(four, "c", [(0, 1), (1, 0)])


def last_places():
    pairs = []
    for z in range(NZ):
        for y in range(NY):
            for part in range(NMP):
                pairs.append(((z * NY + y) * NMP + part, (NZ * part + z) * NMP + y))
    return pairs


def in_hbm(count):
    return [pl.BlockSpec(memory_space=pltpu.HBM)] * count


def body(
    grad_proj, tile_counts, tile_home, saved_feat, ln_gain, layer_scale, attn_saved, proj_weight
):
    mp_index = lax.axis_index(MP)
    cols = attn_saved.shape[1]
    send = pl.pallas_call(
        cut_kernel,
        out_shape=jax.ShapeDtypeStruct((NMP, REST + 2 * PR, 128), BF16),
        in_specs=in_hbm(2),
        out_specs=whole(1)[0],
        scratch_shapes=[
            pltpu.VMEM((PR, PW), BF16),
            pltpu.VMEM((PR, PW), BF16),
            pltpu.VMEM((NMP, 2 * VT, 128), F32),
            pltpu.SemaphoreType.DMA((2,)),
        ],
        compiler_params=pltpu.CompilerParams(vmem_limit_bytes=60 * 1024 * 1024),
        name="cut",
    )(grad_proj, saved_feat)
    attn_own, send = lax.optimization_barrier((attn_saved.T, send))
    recv = lax.all_to_all(send, MP, 0, 0)
    attns = (attn_own,) + gather_x(attn_own)
    x_index, c_index = lax.axis_index("x"), lax.axis_index("c")
    near = jnp.stack([x_index, (x_index + 3) % 4, (x_index + 1) % 4, (x_index + 2) % 4]) * 2
    parts = jnp.concatenate([near + c_index, near + 1 - c_index]).astype(jnp.int32)

    slot_ids = jnp.arange(TILES, dtype=jnp.int32)
    matches = tile_home[0][None, :] == slot_ids[:, None]
    source = jnp.sum(jnp.where(matches, slot_ids[None, :], 0), axis=1).astype(jnp.int32)
    live = (source < jnp.sum(tile_counts)).astype(jnp.int32)
    pad = NMP * FEAT - VW
    gain = jnp.pad(ln_gain.reshape(SUB, VW), ((0, 0), (0, pad + WIDE - FEAT)))
    gain = lax.dynamic_slice_in_dim(gain, mp_index * FEAT, WIDE, axis=1)
    scale = jnp.pad(layer_scale, (0, pad + WIDE - FEAT))
    scale = lax.dynamic_slice_in_dim(scale, mp_index * FEAT, WIDE, axis=0)[None]
    inside = (jnp.arange(WIDE) < FEAT)[None]
    gain = jnp.where(inside, gain, 0.0)
    scale = jnp.where(inside, scale, 0.0)

    sums = pl.pallas_call(
        sums_kernel,
        out_shape=jax.ShapeDtypeStruct((NMP, 8, 128), F32),
        in_specs=scalars(2) + whole(2),
        out_specs=whole(1)[0],
        compiler_params=VMEM,
        name="sums",
    )(source, live, recv, gain)
    sums = lax.all_to_all(sums, MP, 0, 0)
    four, sums = lax.optimization_barrier((jnp.stack(attns), sums))
    attns = attns + (swap_cores(four),)

    branch, gains = pl.pallas_call(
        branch_kernel,
        out_shape=(
            jax.ShapeDtypeStruct((TILES * VT, WIDE), BF16),
            jax.ShapeDtypeStruct((GAIN, 128), BF16),
        ),
        in_specs=scalars(2) + whole(4),
        out_specs=tuple(whole(2)),
        compiler_params=VMEM,
        name="branch",
    )(source, live, recv, gain, scale, sums)
    terms = pl.pallas_call(
        terms_kernel,
        out_shape=jax.ShapeDtypeStruct((NMP, MESSAGE, 128), BF16),
        in_specs=scalars(1) + whole(7),
        out_specs=whole(1)[0],
        compiler_params=VMEM,
        name="terms",
    )(parts, branch, gains, *attns)

    terms = lax.all_to_all(terms, "y", 0, 0)
    terms = pl.pallas_call(
        fold_kernel,
        out_shape=jax.ShapeDtypeStruct((NZ, THIRD, 128), BF16),
        in_specs=whole(1),
        out_specs=whole(1)[0],
        compiler_params=ROOMY,
        name="fold",
    )(terms)
    terms = lax.all_to_all(terms, "z", 0, 0)

    turned = pl.pallas_call(
        turn_kernel,
        out_shape=jax.ShapeDtypeStruct((ROWS, TILES * VT), BF16),
        in_specs=whole(1),
        out_specs=whole(1)[0],
        compiler_params=VMEM,
        name="turn",
    )(branch)
    turned = (turned,) + gather_x(turned)
    turned = turned + (swap_cores(jnp.stack(turned)),)
    attn_grad, residual_grad = pl.pallas_call(
        gathered_kernel,
        out_shape=(
            jax.ShapeDtypeStruct((cols, TILES * VT), BF16),
            jax.ShapeDtypeStruct((VT, VW), BF16),
        ),
        in_specs=scalars(2) + whole(7),
        out_specs=tuple(whole(2)),
        scratch_shapes=[pltpu.VMEM((NMP, ROWS, TILES * VT), BF16)],
        compiler_params=VMEM,
        name="gathered",
    )(mp_index.astype(jnp.int32)[None], parts, proj_weight.T, layer_scale[None], *turned)

    terms, attn_grad, residual_grad = lax.optimization_barrier((terms, attn_grad, residual_grad))
    part, gains = pl.pallas_call(
        settle_kernel,
        out_shape=(
            jax.ShapeDtypeStruct((64, 256), F32),
            jax.ShapeDtypeStruct((NMP, GAIN, 128), F32),
        ),
        in_specs=whole(1),
        out_specs=tuple(whole(2)),
        compiler_params=VMEM,
        name="settle",
    )(terms)

    proj_grad = lax.ppermute(part, DP + MP, last_places())[:BLOCK, :cols]
    gains = lax.all_to_all(gains, MP, 0, 0)
    gain_grad = pl.pallas_call(
        spread_kernel,
        out_shape=jax.ShapeDtypeStruct((PW // 128, 128), F32),
        in_specs=whole(1),
        out_specs=whole(1)[0],
        scratch_shapes=[pltpu.VMEM((SUB, 3456), F32)],
        compiler_params=VMEM,
        name="spread",
    )(gains)
    return (residual_grad, attn_grad.T, proj_grad, gain_grad.reshape(-1))


def solution(mesh):
    fine = Mesh(mesh.devices.reshape(NZ, NY, 4, 2), DP + MP)
    in_specs = (
        P(DP + MP, None),
        P(DP, None),
        P(DP, None),
        P(DP + MP, None),
        P(),
        P(),
        P(DP, MP),
        P(None, MP),
    )
    out_specs = (P(DP + MP, None), P(DP, MP), P(DP, MP), P())
    return jax.shard_map(body, mesh=fine, in_specs=in_specs, out_specs=out_specs, check_vma=False)
```

```python
import jax
import jax.numpy as jnp
from jax import lax
from jax.experimental import pallas as pl
from jax.experimental.pallas import tpu as pltpu
from jax.sharding import Mesh
from jax.sharding import PartitionSpec as P

VW = 3200
PW = 12800
EPSILON = 1e-05
DP = ("z", "y")
MP = ("x", "c")
NZ, NY, NMP = 12, 8, 8
BLOCK = 34
FEAT = NZ * BLOCK
WIDE = 512
ROWS = 416
REST = 384
TILES, PR, SUB, VT = 8, 16, 4, 64
VMEM = pltpu.CompilerParams(vmem_limit_bytes=48 * 1024 * 1024)
F32, BF16 = jnp.float32, jnp.bfloat16


def split3(value):
    high = value.astype(BF16).astype(F32)
    middle = (value - high).astype(BF16).astype(F32)
    low = (value - high - middle).astype(BF16).astype(F32)
    return high, middle, low


def cut_kernel(grad_hbm, feat_hbm, out_ref, grad_ref, feat_ref, last_ref, sems):
    feat_copy = pltpu.make_async_copy(feat_hbm, feat_ref, sems.at[0])
    grad_copy = pltpu.make_async_copy(grad_hbm, grad_ref, sems.at[1])
    feat_copy.start()
    grad_copy.start()
    feat_copy.wait()
    values = feat_ref[...].astype(F32)
    mean = jnp.mean(values, axis=-1, keepdims=True)
    centered = values - mean
    inverse_std = lax.rsqrt(jnp.mean(centered * centered, axis=-1, keepdims=True) + EPSILON)
    marks = split3(mean) + split3(inverse_std)
    lane = lax.broadcasted_iota(jnp.int32, (PR, WIDE), 1)
    grad_copy.wait()
    for part in range(NMP):
        live = lane < min(FEAT, VW - part * FEAT)
        for sub in range(SUB):
            low = sub * VW + part * FEAT
            start = low // 128 * 128
            width = min(640, PW - start)
            for which, ref in enumerate((grad_ref, feat_ref)):
                window = ref[:, start : start + width].astype(F32)
                if width < 640:
                    window = jnp.concatenate([window, jnp.zeros((PR, 640 - width), F32)], axis=1)
                if low > start:
                    window = pltpu.roll(window, 640 - (low - start), 1)
                chunk = jnp.where(live, window[:, :WIDE], 0.0)
                if which == 1 and sub == 0:
                    for at, mark in enumerate(marks):
                        chunk = jnp.where(lane == FEAT + at, mark, chunk)
                row = which * VT + sub * PR
                for tile in range(3):
                    at = tile * 2 * VT + row
                    out_ref[part, at : at + PR, :] = chunk[:, tile * 128 : tile * 128 + 128].astype(BF16)
                last_ref[part, row : row + PR, :] = chunk[:, 384:512]
    for part in range(NMP):
        rest = last_ref[part, 0:32, :]
        for group in range(1, 4):
            rest = rest + pltpu.roll(last_ref[part, 32 * group : 32 * group + 32, :], 32 * group, 1)
        out_ref[part, REST : REST + 2 * PR, :] = rest.astype(BF16)


def unpack(ref, tile, which):
    at = [q * 2 * VT + which * VT for q in range(3)]
    pieces = [ref[tile, r : r + VT, :].astype(F32) for r in at]
    rest = ref[tile, REST : REST + 2 * PR, :].astype(F32)
    turn = (128 - 64 * which) % 128
    rest = jnp.concatenate(
        [pltpu.roll(rest, turn, 1) if turn else rest, pltpu.roll(rest, (turn + 96) % 128, 1)], axis=0
    )
    return pieces, rest


def wide(array):
    return jnp.concatenate([array] * (WIDE // 128), axis=1)


def row_stats(recv_ref):
    marks = jnp.concatenate([recv_ref[t, REST : REST + PR, :] for t in range(TILES)], axis=0)
    low = 64 + FEAT - 384
    lane = lax.broadcasted_iota(jnp.int32, (128, 256), 0)
    which = lax.broadcasted_iota(jnp.int32, (128, 256), 1) >> 7
    pick = (lane >= low + 3 * which) & (lane < low + 3 * which + 3)
    return jnp.dot(marks, pick.astype(F32).astype(BF16), preferred_element_type=F32)


def slot_values(tile, source_ref, live_ref, recv_ref, stats):
    pieces, rest = unpack(recv_ref, source_ref[tile], 0)
    rest = jnp.where(lax.broadcasted_iota(jnp.int32, (VT, 128), 1) < FEAT - 384, rest, 0.0)
    grads = jnp.concatenate(pieces + [rest], axis=1)
    grads = jnp.where(live_ref[tile] > 0, grads, 0.0)
    pieces, rest = unpack(recv_ref, tile, 1)
    feats = jnp.concatenate(pieces + [rest], axis=1)
    mean = wide(stats[tile * PR : (tile + 1) * PR, 0:128])
    inverse_std = wide(stats[tile * PR : (tile + 1) * PR, 128:256])
    upstream = [grads[s * PR : (s + 1) * PR] for s in range(SUB)]
    normed = [(feats[s * PR : (s + 1) * PR] - mean) * inverse_std for s in range(SUB)]
    return upstream, normed, inverse_std


def sums_kernel(source_ref, live_ref, recv_ref, gain_ref, out_ref):
    stats = row_stats(recv_ref)
    firsts, seconds = [], []
    for tile in range(TILES):
        upstream, normed, _ = slot_values(tile, source_ref, live_ref, recv_ref, stats)
        first = jnp.zeros((PR, WIDE), F32)
        second = jnp.zeros((PR, WIDE), F32)
        for s in range(SUB):
            scaled = upstream[s] * gain_ref[s : s + 1, :]
            first = first + scaled
            second = second + scaled * normed[s]
        firsts.append(sum(first[:, q * 128 : q * 128 + 128] for q in range(4)))
        seconds.append(sum(second[:, q * 128 : q * 128 + 128] for q in range(4)))
    first = jnp.sum(jnp.concatenate(firsts, axis=0).T, axis=0, keepdims=True)
    second = jnp.sum(jnp.concatenate(seconds, axis=0).T, axis=0, keepdims=True)
    row = lax.broadcasted_iota(jnp.int32, (8, 128), 0)
    both = jnp.where(row == 0, first, jnp.where(row == 1, second, 0.0))
    for part in range(NMP):
        out_ref[part] = both


COLS, GROUP, GAIN = 208, 48, 16
AT1, AT2, AT3 = COLS, 2 * COLS, 3 * COLS
AT4 = AT3 + GROUP
MESSAGE = AT4 + GAIN
THIRD = 72
SPARE = 3 * BLOCK


def branch_kernel(
    source_ref, live_ref, recv_ref, gain_ref, scale_ref, sums_ref, branch_ref, gain_out_ref
):
    total = sums_ref[0]
    for part in range(1, NMP):
        total = total + sums_ref[part]
    total = total * (1.0 / PW)
    firsts = jnp.broadcast_to(total[0:1], (128, 128)).T
    seconds = jnp.broadcast_to(total[1:2], (128, 128)).T
    stats = row_stats(recv_ref)
    token = lax.broadcasted_iota(jnp.int32, (VT, VT), 0)
    place = lax.broadcasted_iota(jnp.int32, (VT, VT), 1)
    sub_of = ((token >> 3) & 1) * 2 + (token & 1)
    row_of = (token >> 4) * 4 + ((token >> 1) & 3)
    order = (place == sub_of * PR + row_of).astype(BF16)
    gains = [jnp.zeros((PR, WIDE), F32) for _ in range(SUB)]
    for tile in range(TILES):
        upstream, normed, inverse_std = slot_values(tile, source_ref, live_ref, recv_ref, stats)
        first = wide(firsts[tile * PR : (tile + 1) * PR])
        second = wide(seconds[tile * PR : (tile + 1) * PR])
        branch = []
        for s in range(SUB):
            scaled = upstream[s] * gain_ref[s : s + 1, :]
            grad = inverse_std * (scaled - first - normed[s] * second)
            branch.append((grad * scale_ref[...]).astype(BF16))
            gains[s] = gains[s] + upstream[s] * normed[s]
        branch = jnp.dot(order, jnp.concatenate(branch, axis=0), preferred_element_type=F32)
        branch_ref[tile * VT : (tile + 1) * VT, :] = branch.astype(BF16)
    gain = jnp.concatenate([jnp.sum(g, axis=0, keepdims=True) for g in gains], axis=0)
    gain = jnp.concatenate([gain[:, q * 128 : (q + 1) * 128] for q in range(4)], axis=0)
    gain_out_ref[...] = gain.astype(BF16)


def terms_kernel(
    parts_ref, branch_ref, gain_ref, own_ref, before_ref, after_ref, far_ref, other_ref,
    terms_ref,
):
    attns = [own_ref, before_ref, after_ref, far_ref] + [other_ref.at[p] for p in range(4)]
    for place, attn in enumerate(attns):
        part = parts_ref[place]
        term = jnp.dot(attn[...], branch_ref[...], preferred_element_type=F32)
        for q in range(3):
            terms_ref[part, q * COLS : (q + 1) * COLS, :] = term[:, q * 128 : q * 128 + 128].astype(BF16)
        last = term[:, 384:512]
        rest = last[0:GROUP]
        for g in range(1, 4):
            rest = rest + pltpu.roll(last[g * GROUP : (g + 1) * GROUP], 24 * g, 1)
        tail = pltpu.roll(last[4 * GROUP : COLS], 96, 1)
        rest = jnp.concatenate([rest[0:16] + tail, rest[16:]], axis=0)
        terms_ref[part, AT3:AT4, :] = rest.astype(BF16)
        terms_ref[part, AT4:MESSAGE, :] = gain_ref[...]


def turn_kernel(branch_ref, turned_ref):
    turned_ref[...] = branch_ref[...].T[:ROWS]


def left(array, lanes):
    lanes = lanes % 128
    return pltpu.roll(array, 128 - lanes, 1) if lanes else array


def fold_kernel(recv_ref, out_ref):
    total = recv_ref[0].astype(F32)
    for part in range(1, NY):
        total = total + recv_ref[part].astype(F32)
    rest = total[AT3:AT4]
    rest = [left(rest, 24 * g) for g in range(5)]
    rest = jnp.concatenate(rest[:4] + [rest[4][0:16]], axis=0)
    tiles = [total[0:AT1], total[AT1:AT2], total[AT2:AT3], rest]
    gain = total[AT4:MESSAGE]
    gains = [left(gain[0:12], 26 * e - SPARE) for e in range(5)] + [left(gain[12:16], -SPARE)]
    gains = jnp.concatenate(gains + [jnp.zeros((THIRD - 64, 128), F32)], axis=0)
    lane = lax.broadcasted_iota(jnp.int32, (THIRD, 128), 1)
    for z in range(NZ):
        tile, at = divmod(z * BLOCK, 128)
        packed = gains
        for group in range(3):
            rows = slice(group * THIRD, min(COLS, (group + 1) * THIRD))
            shift = at - group * BLOCK
            piece = left(tiles[tile][rows], shift)
            if at + BLOCK > 128:
                inside = lane[: piece.shape[0]] < group * BLOCK + 128 - at
                piece = jnp.where(inside, piece, left(tiles[tile + 1][rows], shift))
            if group == 2:
                piece = jnp.concatenate([piece, jnp.zeros((3 * THIRD - COLS, 128), F32)], axis=0)
            inside = (lane >= group * BLOCK) & (lane < (group + 1) * BLOCK)
            packed = jnp.where(inside, piece, packed)
        out_ref[z] = packed.astype(BF16)


def settle_kernel(recv_ref, block_ref, gain_ref):
    total = recv_ref[0].astype(F32)
    for part in range(1, NZ):
        total = total + recv_ref[part].astype(F32)
    block = [total, left(total, BLOCK), left(total, 2 * BLOCK)[0 : COLS - 2 * THIRD]]
    block = jnp.concatenate(block + [jnp.zeros((256 - COLS, 128), F32)], axis=0).T
    block_ref[...] = block[0 : block_ref.shape[0]]
    lane = lax.broadcasted_iota(jnp.int32, (12, 128), 1)
    gain = jnp.zeros((12, 128), F32)
    for e in range(5):
        inside = (lane >= 26 * e) & (lane < 26 * e + 26)
        gain = jnp.where(inside, left(total[12 * e : 12 * e + 12], SPARE - 26 * e), gain)
    rest = jnp.where(lane[0:4] < FEAT - 384, left(total[60:64], SPARE), 0.0)
    gain = jnp.concatenate([gain, rest], axis=0)
    for part in range(NMP):
        gain_ref[part] = gain


def spread_kernel(gain_ref, out_ref, wide_ref):
    wide_ref[...] = jnp.zeros_like(wide_ref)
    for part in range(NMP):
        gain = gain_ref[part]
        pieces = [gain[q * SUB : (q + 1) * SUB] for q in range(4)] + [jnp.zeros((SUB, 128), F32)]
        low = part * FEAT
        start = low // 128 * 128
        pieces = jnp.concatenate(pieces, axis=1)
        if low > start:
            pieces = pltpu.roll(pieces, low - start, 1)
        wide_ref[:, start : start + 640] += pieces
    out_ref[...] = wide_ref[:, 0:VW]


def gathered_kernel(
    tile_ref, parts_ref, weight_ref, scale_ref, own_ref, before_ref, after_ref, far_ref, other_ref,
    attn_ref, residual_ref, all_ref,
):
    pieces = [own_ref, before_ref, after_ref, far_ref] + [other_ref.at[p] for p in range(4)]
    for place, piece in enumerate(pieces):
        all_ref[parts_ref[place]] = piece[...]
    tile = tile_ref[0]
    at = pl.multiple_of((tile >> 1) * 128, 128)
    lane = lax.broadcasted_iota(jnp.int32, (COLS, WIDE), 1)
    total = jnp.zeros((COLS, TILES * VT), F32)
    tokens = []
    for part in range(NMP):
        low = part * FEAT
        start = low // 128 * 128
        width = min(640, VW - start)
        weight = weight_ref[:, start : start + width].astype(F32)
        if width < 640:
            weight = jnp.concatenate([weight, jnp.zeros((COLS, 640 - width), F32)], axis=1)
        if low > start:
            weight = pltpu.roll(weight, 640 - (low - start), 1)
        weight = jnp.where(lane < min(FEAT, VW - low), weight[:, :WIDE], 0.0).astype(BF16)
        total += jnp.dot(weight[:, :ROWS], all_ref[part], preferred_element_type=F32)
        tokens.append(all_ref[part, :, pl.ds(at, 128)].astype(F32)[:FEAT])
    attn_ref[...] = total.astype(BF16)
    tokens = jnp.concatenate(tokens, axis=0)[:VW].T
    tokens = jnp.where((tile & 1) == 0, tokens[0:VT], tokens[VT : 2 * VT])
    residual_ref[...] = (tokens / scale_ref[...]).astype(BF16)


def whole(count):
    return [pl.BlockSpec(memory_space=pltpu.VMEM)] * count


def scalars(count):
    return [pl.BlockSpec(memory_space=pltpu.SMEM)] * count


def gather_x(own):
    return tuple(
        lax.ppermute(own, "x", [(x, (x + step) % 4) for x in range(4)]) for step in (1, 3, 2)
    )


def swap_cores(four):
    return lax.ppermute(four, "c", [(0, 1), (1, 0)])


def last_places():
    pairs = []
    for z in range(NZ):
        for y in range(NY):
            for part in range(NMP):
                pairs.append(((z * NY + y) * NMP + part, (NZ * part + z) * NMP + y))
    return pairs


def in_hbm(count):
    return [pl.BlockSpec(memory_space=pltpu.HBM)] * count


def body(
    grad_proj, tile_counts, tile_home, saved_feat, ln_gain, layer_scale, attn_saved, proj_weight
):
    mp_index = lax.axis_index(MP)
    cols = attn_saved.shape[1]
    send = pl.pallas_call(
        cut_kernel,
        out_shape=jax.ShapeDtypeStruct((NMP, REST + 2 * PR, 128), BF16),
        in_specs=in_hbm(2),
        out_specs=whole(1)[0],
        scratch_shapes=[
            pltpu.VMEM((PR, PW), BF16),
            pltpu.VMEM((PR, PW), BF16),
            pltpu.VMEM((NMP, 2 * VT, 128), F32),
            pltpu.SemaphoreType.DMA((2,)),
        ],
        compiler_params=pltpu.CompilerParams(vmem_limit_bytes=60 * 1024 * 1024),
        name="cut",
    )(grad_proj, saved_feat)
    attn_own, send = lax.optimization_barrier((attn_saved.T, send))
    recv = lax.all_to_all(send, MP, 0, 0)
    attns = (attn_own,) + gather_x(attn_own)
    x_index, c_index = lax.axis_index("x"), lax.axis_index("c")
    near = jnp.stack([x_index, (x_index + 3) % 4, (x_index + 1) % 4, (x_index + 2) % 4]) * 2
    parts = jnp.concatenate([near + c_index, near + 1 - c_index]).astype(jnp.int32)

    slot_ids = jnp.arange(TILES, dtype=jnp.int32)
    matches = tile_home[0][None, :] == slot_ids[:, None]
    source = jnp.sum(jnp.where(matches, slot_ids[None, :], 0), axis=1).astype(jnp.int32)
    live = (source < jnp.sum(tile_counts)).astype(jnp.int32)
    pad = NMP * FEAT - VW
    gain = jnp.pad(ln_gain.reshape(SUB, VW), ((0, 0), (0, pad + WIDE - FEAT)))
    gain = lax.dynamic_slice_in_dim(gain, mp_index * FEAT, WIDE, axis=1)
    scale = jnp.pad(layer_scale, (0, pad + WIDE - FEAT))
    scale = lax.dynamic_slice_in_dim(scale, mp_index * FEAT, WIDE, axis=0)[None]
    inside = (jnp.arange(WIDE) < FEAT)[None]
    gain = jnp.where(inside, gain, 0.0)
    scale = jnp.where(inside, scale, 0.0)

    sums = pl.pallas_call(
        sums_kernel,
        out_shape=jax.ShapeDtypeStruct((NMP, 8, 128), F32),
        in_specs=scalars(2) + whole(2),
        out_specs=whole(1)[0],
        compiler_params=VMEM,
        name="sums",
    )(source, live, recv, gain)
    sums = lax.all_to_all(sums, MP, 0, 0)
    four, sums = lax.optimization_barrier((jnp.stack(attns), sums))
    attns = attns + (swap_cores(four),)

    branch, gains = pl.pallas_call(
        branch_kernel,
        out_shape=(
            jax.ShapeDtypeStruct((TILES * VT, WIDE), BF16),
            jax.ShapeDtypeStruct((GAIN, 128), BF16),
        ),
        in_specs=scalars(2) + whole(4),
        out_specs=tuple(whole(2)),
        compiler_params=VMEM,
        name="branch",
    )(source, live, recv, gain, scale, sums)
    terms = pl.pallas_call(
        terms_kernel,
        out_shape=jax.ShapeDtypeStruct((NMP, MESSAGE, 128), BF16),
        in_specs=scalars(1) + whole(7),
        out_specs=whole(1)[0],
        compiler_params=VMEM,
        name="terms",
    )(parts, branch, gains, *attns)

    terms = lax.all_to_all(terms, "y", 0, 0)
    terms = pl.pallas_call(
        fold_kernel,
        out_shape=jax.ShapeDtypeStruct((NZ, THIRD, 128), BF16),
        in_specs=whole(1),
        out_specs=whole(1)[0],
        compiler_params=VMEM,
        name="fold",
    )(terms)
    terms = lax.all_to_all(terms, "z", 0, 0)

    turned = pl.pallas_call(
        turn_kernel,
        out_shape=jax.ShapeDtypeStruct((ROWS, TILES * VT), BF16),
        in_specs=whole(1),
        out_specs=whole(1)[0],
        compiler_params=VMEM,
        name="turn",
    )(branch)
    turned = (turned,) + gather_x(turned)
    turned = turned + (swap_cores(jnp.stack(turned)),)
    attn_grad, residual_grad = pl.pallas_call(
        gathered_kernel,
        out_shape=(
            jax.ShapeDtypeStruct((cols, TILES * VT), BF16),
            jax.ShapeDtypeStruct((VT, VW), BF16),
        ),
        in_specs=scalars(2) + whole(7),
        out_specs=tuple(whole(2)),
        scratch_shapes=[pltpu.VMEM((NMP, ROWS, TILES * VT), BF16)],
        compiler_params=VMEM,
        name="gathered",
    )(mp_index.astype(jnp.int32)[None], parts, proj_weight.T, layer_scale[None], *turned)

    terms, attn_grad, residual_grad = lax.optimization_barrier((terms, attn_grad, residual_grad))
    part, gains = pl.pallas_call(
        settle_kernel,
        out_shape=(
            jax.ShapeDtypeStruct((64, 256), F32),
            jax.ShapeDtypeStruct((NMP, GAIN, 128), F32),
        ),
        in_specs=whole(1),
        out_specs=tuple(whole(2)),
        compiler_params=VMEM,
        name="settle",
    )(terms)

    proj_grad = lax.ppermute(part, DP + MP, last_places())[:BLOCK, :cols]
    gains = lax.all_to_all(gains, MP, 0, 0)
    gain_grad = pl.pallas_call(
        spread_kernel,
        out_shape=jax.ShapeDtypeStruct((SUB, VW), F32),
        in_specs=whole(1),
        out_specs=whole(1)[0],
        scratch_shapes=[pltpu.VMEM((SUB, 3456), F32)],
        compiler_params=VMEM,
        name="spread",
    )(gains)
    return (residual_grad, attn_grad.T, proj_grad, gain_grad.reshape(-1))


def solution(mesh):
    fine = Mesh(mesh.devices.reshape(NZ, NY, 4, 2), DP + MP)
    in_specs = (
        P(DP + MP, None),
        P(DP, None),
        P(DP, None),
        P(DP + MP, None),
        P(),
        P(),
        P(DP, MP),
        P(None, MP),
    )
    out_specs = (P(DP + MP, None), P(DP, MP), P(DP, MP), P())
    return jax.shard_map(body, mesh=fine, in_specs=in_specs, out_specs=out_specs, check_vma=False)
```

```python
import jax
import jax.numpy as jnp
from jax import lax
from jax.experimental import pallas as pl
from jax.experimental.pallas import tpu as pltpu
from jax.sharding import Mesh
from jax.sharding import PartitionSpec as P

VW = 3200
PW = 12800
EPSILON = 1e-05
DP = ("z", "y")
MP = ("x", "c")
NZ, NY, NMP = 12, 8, 8
BLOCK = 34
FEAT = NZ * BLOCK
WIDE = 512
ROWS = 416
REST = 384
TILES, PR, SUB, VT = 8, 16, 4, 64
VMEM = pltpu.CompilerParams(vmem_limit_bytes=48 * 1024 * 1024)
F32, BF16 = jnp.float32, jnp.bfloat16


def split3(value):
    high = value.astype(BF16).astype(F32)
    middle = (value - high).astype(BF16).astype(F32)
    low = (value - high - middle).astype(BF16).astype(F32)
    return high, middle, low


def cut_kernel(grad_hbm, feat_hbm, out_ref, grad_ref, feat_ref, last_ref, sems):
    feat_copy = pltpu.make_async_copy(feat_hbm, feat_ref, sems.at[0])
    grad_copy = pltpu.make_async_copy(grad_hbm, grad_ref, sems.at[1])
    feat_copy.start()
    grad_copy.start()
    feat_copy.wait()
    values = feat_ref[...].astype(F32)
    mean = jnp.mean(values, axis=-1, keepdims=True)
    centered = values - mean
    inverse_std = lax.rsqrt(jnp.mean(centered * centered, axis=-1, keepdims=True) + EPSILON)
    marks = split3(mean) + split3(inverse_std)
    lane = lax.broadcasted_iota(jnp.int32, (PR, WIDE), 1)
    grad_copy.wait()
    for part in range(NMP):
        live = lane < min(FEAT, VW - part * FEAT)
        for sub in range(SUB):
            low = sub * VW + part * FEAT
            start = low // 128 * 128
            width = min(640, PW - start)
            for which, ref in enumerate((grad_ref, feat_ref)):
                window = ref[:, start : start + width].astype(F32)
                if width < 640:
                    window = jnp.concatenate([window, jnp.zeros((PR, 640 - width), F32)], axis=1)
                if low > start:
                    window = pltpu.roll(window, 640 - (low - start), 1)
                chunk = jnp.where(live, window[:, :WIDE], 0.0)
                if which == 1 and sub == 0:
                    for at, mark in enumerate(marks):
                        chunk = jnp.where(lane == FEAT + at, mark, chunk)
                row = which * VT + sub * PR
                for tile in range(3):
                    at = tile * 2 * VT + row
                    out_ref[part, at : at + PR, :] = chunk[:, tile * 128 : tile * 128 + 128].astype(BF16)
                last_ref[part, row : row + PR, :] = chunk[:, 384:512]
    for part in range(NMP):
        rest = last_ref[part, 0:32, :]
        for group in range(1, 4):
            rest = rest + pltpu.roll(last_ref[part, 32 * group : 32 * group + 32, :], 32 * group, 1)
        out_ref[part, REST : REST + 2 * PR, :] = rest.astype(BF16)


def unpack(ref, tile, which):
    at = [q * 2 * VT + which * VT for q in range(3)]
    pieces = [ref[tile, r : r + VT, :].astype(F32) for r in at]
    rest = ref[tile, REST : REST + 2 * PR, :].astype(F32)
    turn = (128 - 64 * which) % 128
    rest = jnp.concatenate(
        [pltpu.roll(rest, turn, 1) if turn else rest, pltpu.roll(rest, (turn + 96) % 128, 1)], axis=0
    )
    return pieces, rest


def wide(array):
    return jnp.concatenate([array] * (WIDE // 128), axis=1)


def row_stats(recv_ref):
    marks = jnp.concatenate([recv_ref[t, REST : REST + PR, :] for t in range(TILES)], axis=0)
    low = 64 + FEAT - 384
    lane = lax.broadcasted_iota(jnp.int32, (128, 256), 0)
    which = lax.broadcasted_iota(jnp.int32, (128, 256), 1) >> 7
    pick = (lane >= low + 3 * which) & (lane < low + 3 * which + 3)
    return jnp.dot(marks, pick.astype(F32).astype(BF16), preferred_element_type=F32)


def slot_values(tile, source_ref, live_ref, recv_ref, stats):
    pieces, rest = unpack(recv_ref, source_ref[tile], 0)
    rest = jnp.where(lax.broadcasted_iota(jnp.int32, (VT, 128), 1) < FEAT - 384, rest, 0.0)
    grads = jnp.concatenate(pieces + [rest], axis=1)
    grads = jnp.where(live_ref[tile] > 0, grads, 0.0)
    pieces, rest = unpack(recv_ref, tile, 1)
    feats = jnp.concatenate(pieces + [rest], axis=1)
    mean = wide(stats[tile * PR : (tile + 1) * PR, 0:128])
    inverse_std = wide(stats[tile * PR : (tile + 1) * PR, 128:256])
    upstream = [grads[s * PR : (s + 1) * PR] for s in range(SUB)]
    normed = [(feats[s * PR : (s + 1) * PR] - mean) * inverse_std for s in range(SUB)]
    return upstream, normed, inverse_std


def sums_kernel(source_ref, live_ref, recv_ref, gain_ref, out_ref):
    stats = row_stats(recv_ref)
    firsts, seconds = [], []
    for tile in range(TILES):
        upstream, normed, _ = slot_values(tile, source_ref, live_ref, recv_ref, stats)
        first = jnp.zeros((PR, WIDE), F32)
        second = jnp.zeros((PR, WIDE), F32)
        for s in range(SUB):
            scaled = upstream[s] * gain_ref[s : s + 1, :]
            first = first + scaled
            second = second + scaled * normed[s]
        firsts.append(sum(first[:, q * 128 : q * 128 + 128] for q in range(4)))
        seconds.append(sum(second[:, q * 128 : q * 128 + 128] for q in range(4)))
    first = jnp.sum(jnp.concatenate(firsts, axis=0).T, axis=0, keepdims=True)
    second = jnp.sum(jnp.concatenate(seconds, axis=0).T, axis=0, keepdims=True)
    row = lax.broadcasted_iota(jnp.int32, (8, 128), 0)
    both = jnp.where(row == 0, first, jnp.where(row == 1, second, 0.0))
    for part in range(NMP):
        out_ref[part] = both


COLS, GROUP, GAIN = 208, 48, 16
AT1, AT2, AT3 = COLS, 2 * COLS, 3 * COLS
AT4 = AT3 + GROUP
MESSAGE = AT4 + GAIN
THIRD = 72
SPARE = 3 * BLOCK


def branch_kernel(
    source_ref, live_ref, recv_ref, gain_ref, scale_ref, sums_ref, branch_ref, gain_out_ref
):
    total = sums_ref[0]
    for part in range(1, NMP):
        total = total + sums_ref[part]
    total = total * (1.0 / PW)
    firsts = jnp.broadcast_to(total[0:1], (128, 128)).T
    seconds = jnp.broadcast_to(total[1:2], (128, 128)).T
    stats = row_stats(recv_ref)
    token = lax.broadcasted_iota(jnp.int32, (VT, VT), 0)
    place = lax.broadcasted_iota(jnp.int32, (VT, VT), 1)
    sub_of = ((token >> 3) & 1) * 2 + (token & 1)
    row_of = (token >> 4) * 4 + ((token >> 1) & 3)
    order = (place == sub_of * PR + row_of).astype(BF16)
    gains = [jnp.zeros((PR, WIDE), F32) for _ in range(SUB)]
    for tile in range(TILES):
        upstream, normed, inverse_std = slot_values(tile, source_ref, live_ref, recv_ref, stats)
        first = wide(firsts[tile * PR : (tile + 1) * PR])
        second = wide(seconds[tile * PR : (tile + 1) * PR])
        branch = []
        for s in range(SUB):
            scaled = upstream[s] * gain_ref[s : s + 1, :]
            grad = inverse_std * (scaled - first - normed[s] * second)
            branch.append((grad * scale_ref[...]).astype(BF16))
            gains[s] = gains[s] + upstream[s] * normed[s]
        branch = jnp.dot(order, jnp.concatenate(branch, axis=0), preferred_element_type=F32)
        branch_ref[tile * VT : (tile + 1) * VT, :] = branch.astype(BF16)
    gain = jnp.concatenate([jnp.sum(g, axis=0, keepdims=True) for g in gains], axis=0)
    gain = jnp.concatenate([gain[:, q * 128 : (q + 1) * 128] for q in range(4)], axis=0)
    gain_out_ref[...] = gain.astype(BF16)


def terms_kernel(
    parts_ref, branch_ref, gain_ref, own_ref, before_ref, after_ref, far_ref, other_ref,
    terms_ref,
):
    attns = [own_ref, before_ref, after_ref, far_ref] + [other_ref.at[p] for p in range(4)]
    for place, attn in enumerate(attns):
        part = parts_ref[place]
        term = jnp.dot(attn[...], branch_ref[...], preferred_element_type=F32)
        for q in range(3):
            terms_ref[part, q * COLS : (q + 1) * COLS, :] = term[:, q * 128 : q * 128 + 128].astype(BF16)
        last = term[:, 384:512]
        rest = last[0:GROUP]
        for g in range(1, 4):
            rest = rest + pltpu.roll(last[g * GROUP : (g + 1) * GROUP], 24 * g, 1)
        tail = pltpu.roll(last[4 * GROUP : COLS], 96, 1)
        rest = jnp.concatenate([rest[0:16] + tail, rest[16:]], axis=0)
        terms_ref[part, AT3:AT4, :] = rest.astype(BF16)
        terms_ref[part, AT4:MESSAGE, :] = gain_ref[...]


def turn_kernel(branch_ref, turned_ref):
    turned_ref[...] = branch_ref[...].T[:ROWS]


def left(array, lanes):
    lanes = lanes % 128
    return pltpu.roll(array, 128 - lanes, 1) if lanes else array


def fold_kernel(recv_ref, out_ref):
    total = recv_ref[0].astype(F32)
    for part in range(1, NY):
        total = total + recv_ref[part].astype(F32)
    rest = total[AT3:AT4]
    rest = [left(rest, 24 * g) for g in range(5)]
    rest = jnp.concatenate(rest[:4] + [rest[4][0:16]], axis=0)
    tiles = [total[0:AT1], total[AT1:AT2], total[AT2:AT3], rest]
    gain = total[AT4:MESSAGE]
    gains = [left(gain[0:12], 26 * e - SPARE) for e in range(5)] + [left(gain[12:16], -SPARE)]
    gains = jnp.concatenate(gains + [jnp.zeros((THIRD - 64, 128), F32)], axis=0)
    lane = lax.broadcasted_iota(jnp.int32, (THIRD, 128), 1)
    for z in range(NZ):
        tile, at = divmod(z * BLOCK, 128)
        packed = gains
        for group in range(3):
            rows = slice(group * THIRD, min(COLS, (group + 1) * THIRD))
            shift = at - group * BLOCK
            piece = left(tiles[tile][rows], shift)
            if at + BLOCK > 128:
                inside = lane[: piece.shape[0]] < group * BLOCK + 128 - at
                piece = jnp.where(inside, piece, left(tiles[tile + 1][rows], shift))
            if group == 2:
                piece = jnp.concatenate([piece, jnp.zeros((3 * THIRD - COLS, 128), F32)], axis=0)
            inside = (lane >= group * BLOCK) & (lane < (group + 1) * BLOCK)
            packed = jnp.where(inside, piece, packed)
        out_ref[z] = packed.astype(BF16)


def settle_kernel(recv_ref, block_ref, gain_ref):
    total = recv_ref[0].astype(F32)
    for part in range(1, NZ):
        total = total + recv_ref[part].astype(F32)
    block = [total, left(total, BLOCK), left(total, 2 * BLOCK)[0 : COLS - 2 * THIRD]]
    block = jnp.concatenate(block + [jnp.zeros((256 - COLS, 128), F32)], axis=0).T
    block_ref[...] = block[0 : block_ref.shape[0]]
    lane = lax.broadcasted_iota(jnp.int32, (12, 128), 1)
    gain = jnp.zeros((12, 128), F32)
    for e in range(5):
        inside = (lane >= 26 * e) & (lane < 26 * e + 26)
        gain = jnp.where(inside, left(total[12 * e : 12 * e + 12], SPARE - 26 * e), gain)
    rest = jnp.where(lane[0:4] < FEAT - 384, left(total[60:64], SPARE), 0.0)
    gain = jnp.concatenate([gain, rest], axis=0)
    for part in range(NMP):
        gain_ref[part] = gain


def spread_kernel(gain_ref, part_ref, out_ref, block_ref, wide_ref):
    block_ref[...] = part_ref[0:BLOCK, 0 : block_ref.shape[1]]
    wide_ref[...] = jnp.zeros_like(wide_ref)
    for part in range(NMP):
        gain = gain_ref[part]
        pieces = [gain[q * SUB : (q + 1) * SUB] for q in range(4)] + [jnp.zeros((SUB, 128), F32)]
        low = part * FEAT
        start = low // 128 * 128
        pieces = jnp.concatenate(pieces, axis=1)
        if low > start:
            pieces = pltpu.roll(pieces, low - start, 1)
        wide_ref[:, start : start + 640] += pieces
    for sub in range(SUB):
        for tile in range(VW // 128):
            row = sub * (VW // 128) + tile
            out_ref[row : row + 1, :] = wide_ref[sub : sub + 1, tile * 128 : tile * 128 + 128]


def gathered_kernel(
    tile_ref, parts_ref, weight_ref, scale_ref, own_ref, before_ref, after_ref, far_ref, other_ref,
    attn_ref, residual_ref, all_ref,
):
    pieces = [own_ref, before_ref, after_ref, far_ref] + [other_ref.at[p] for p in range(4)]
    for place, piece in enumerate(pieces):
        all_ref[parts_ref[place]] = piece[...]
    tile = tile_ref[0]
    at = pl.multiple_of((tile >> 1) * 128, 128)
    lane = lax.broadcasted_iota(jnp.int32, (COLS, WIDE), 1)
    total = jnp.zeros((COLS, TILES * VT), F32)
    tokens = []
    for part in range(NMP):
        low = part * FEAT
        start = low // 128 * 128
        width = min(640, VW - start)
        weight = weight_ref[:, start : start + width].astype(F32)
        if width < 640:
            weight = jnp.concatenate([weight, jnp.zeros((COLS, 640 - width), F32)], axis=1)
        if low > start:
            weight = pltpu.roll(weight, 640 - (low - start), 1)
        weight = jnp.where(lane < min(FEAT, VW - low), weight[:, :WIDE], 0.0).astype(BF16)
        total += jnp.dot(weight[:, :ROWS], all_ref[part], preferred_element_type=F32)
        tokens.append(all_ref[part, :, pl.ds(at, 128)].astype(F32)[:FEAT])
    attn_ref[...] = total.astype(BF16)
    tokens = jnp.concatenate(tokens, axis=0)[:VW].T
    tokens = jnp.where((tile & 1) == 0, tokens[0:VT], tokens[VT : 2 * VT])
    residual_ref[...] = (tokens / scale_ref[...]).astype(BF16)


def whole(count):
    return [pl.BlockSpec(memory_space=pltpu.VMEM)] * count


def scalars(count):
    return [pl.BlockSpec(memory_space=pltpu.SMEM)] * count


def gather_x(own):
    return tuple(
        lax.ppermute(own, "x", [(x, (x + step) % 4) for x in range(4)]) for step in (1, 3, 2)
    )


def swap_cores(four):
    return lax.ppermute(four, "c", [(0, 1), (1, 0)])


def last_places():
    pairs = []
    for z in range(NZ):
        for y in range(NY):
            for part in range(NMP):
                pairs.append(((z * NY + y) * NMP + part, (NZ * part + z) * NMP + y))
    return pairs


def in_hbm(count):
    return [pl.BlockSpec(memory_space=pltpu.HBM)] * count


def body(
    grad_proj, tile_counts, tile_home, saved_feat, ln_gain, layer_scale, attn_saved, proj_weight
):
    mp_index = lax.axis_index(MP)
    cols = attn_saved.shape[1]
    send = pl.pallas_call(
        cut_kernel,
        out_shape=jax.ShapeDtypeStruct((NMP, REST + 2 * PR, 128), BF16),
        in_specs=in_hbm(2),
        out_specs=whole(1)[0],
        scratch_shapes=[
            pltpu.VMEM((PR, PW), BF16),
            pltpu.VMEM((PR, PW), BF16),
            pltpu.VMEM((NMP, 2 * VT, 128), F32),
            pltpu.SemaphoreType.DMA((2,)),
        ],
        compiler_params=pltpu.CompilerParams(vmem_limit_bytes=60 * 1024 * 1024),
        name="cut",
    )(grad_proj, saved_feat)
    attn_own, send = lax.optimization_barrier((attn_saved.T, send))
    recv = lax.all_to_all(send, MP, 0, 0)
    attns = (attn_own,) + gather_x(attn_own)
    x_index, c_index = lax.axis_index("x"), lax.axis_index("c")
    near = jnp.stack([x_index, (x_index + 3) % 4, (x_index + 1) % 4, (x_index + 2) % 4]) * 2
    parts = jnp.concatenate([near + c_index, near + 1 - c_index]).astype(jnp.int32)

    slot_ids = jnp.arange(TILES, dtype=jnp.int32)
    matches = tile_home[0][None, :] == slot_ids[:, None]
    source = jnp.sum(jnp.where(matches, slot_ids[None, :], 0), axis=1).astype(jnp.int32)
    live = (source < jnp.sum(tile_counts)).astype(jnp.int32)
    pad = NMP * FEAT - VW
    gain = jnp.pad(ln_gain.reshape(SUB, VW), ((0, 0), (0, pad + WIDE - FEAT)))
    gain = lax.dynamic_slice_in_dim(gain, mp_index * FEAT, WIDE, axis=1)
    scale = jnp.pad(layer_scale, (0, pad + WIDE - FEAT))
    scale = lax.dynamic_slice_in_dim(scale, mp_index * FEAT, WIDE, axis=0)[None]
    inside = (jnp.arange(WIDE) < FEAT)[None]
    gain = jnp.where(inside, gain, 0.0)
    scale = jnp.where(inside, scale, 0.0)

    sums = pl.pallas_call(
        sums_kernel,
        out_shape=jax.ShapeDtypeStruct((NMP, 8, 128), F32),
        in_specs=scalars(2) + whole(2),
        out_specs=whole(1)[0],
        compiler_params=VMEM,
        name="sums",
    )(source, live, recv, gain)
    sums = lax.all_to_all(sums, MP, 0, 0)
    four, sums = lax.optimization_barrier((jnp.stack(attns), sums))
    attns = attns + (swap_cores(four),)

    branch, gains = pl.pallas_call(
        branch_kernel,
        out_shape=(
            jax.ShapeDtypeStruct((TILES * VT, WIDE), BF16),
            jax.ShapeDtypeStruct((GAIN, 128), BF16),
        ),
        in_specs=scalars(2) + whole(4),
        out_specs=tuple(whole(2)),
        compiler_params=VMEM,
        name="branch",
    )(source, live, recv, gain, scale, sums)
    terms = pl.pallas_call(
        terms_kernel,
        out_shape=jax.ShapeDtypeStruct((NMP, MESSAGE, 128), BF16),
        in_specs=scalars(1) + whole(7),
        out_specs=whole(1)[0],
        compiler_params=VMEM,
        name="terms",
    )(parts, branch, gains, *attns)

    terms = lax.all_to_all(terms, "y", 0, 0)
    terms = pl.pallas_call(
        fold_kernel,
        out_shape=jax.ShapeDtypeStruct((NZ, THIRD, 128), BF16),
        in_specs=whole(1),
        out_specs=whole(1)[0],
        compiler_params=VMEM,
        name="fold",
    )(terms)
    terms = lax.all_to_all(terms, "z", 0, 0)

    turned = pl.pallas_call(
        turn_kernel,
        out_shape=jax.ShapeDtypeStruct((ROWS, TILES * VT), BF16),
        in_specs=whole(1),
        out_specs=whole(1)[0],
        compiler_params=VMEM,
        name="turn",
    )(branch)
    turned = (turned,) + gather_x(turned)
    turned = turned + (swap_cores(jnp.stack(turned)),)
    attn_grad, residual_grad = pl.pallas_call(
        gathered_kernel,
        out_shape=(
            jax.ShapeDtypeStruct((cols, TILES * VT), BF16),
            jax.ShapeDtypeStruct((VT, VW), BF16),
        ),
        in_specs=scalars(2) + whole(7),
        out_specs=tuple(whole(2)),
        scratch_shapes=[pltpu.VMEM((NMP, ROWS, TILES * VT), BF16)],
        compiler_params=VMEM,
        name="gathered",
    )(mp_index.astype(jnp.int32)[None], parts, proj_weight.T, layer_scale[None], *turned)

    terms, attn_grad, residual_grad = lax.optimization_barrier((terms, attn_grad, residual_grad))
    part, gains = pl.pallas_call(
        settle_kernel,
        out_shape=(
            jax.ShapeDtypeStruct((64, 256), F32),
            jax.ShapeDtypeStruct((NMP, GAIN, 128), F32),
        ),
        in_specs=whole(1),
        out_specs=tuple(whole(2)),
        compiler_params=VMEM,
        name="settle",
    )(terms)

    part = lax.ppermute(part, DP + MP, last_places())
    gains = lax.all_to_all(gains, MP, 0, 0)
    gain_grad, proj_grad = pl.pallas_call(
        spread_kernel,
        out_shape=(
            jax.ShapeDtypeStruct((PW // 128, 128), F32),
            jax.ShapeDtypeStruct((BLOCK, cols), F32),
        ),
        in_specs=whole(2),
        out_specs=tuple(whole(2)),
        scratch_shapes=[pltpu.VMEM((SUB, 3456), F32)],
        compiler_params=VMEM,
        name="spread",
    )(gains, part)
    return (residual_grad, attn_grad.T, proj_grad, gain_grad.reshape(-1))


def solution(mesh):
    fine = Mesh(mesh.devices.reshape(NZ, NY, 4, 2), DP + MP)
    in_specs = (
        P(DP + MP, None),
        P(DP, None),
        P(DP, None),
        P(DP + MP, None),
        P(),
        P(),
        P(DP, MP),
        P(None, MP),
    )
    out_specs = (P(DP + MP, None), P(DP, MP), P(DP, MP), P())
    return jax.shard_map(body, mesh=fine, in_specs=in_specs, out_specs=out_specs, check_vma=False)
```
